32 devices in a mesh: dp: 4 (over x, core), seq: 8 (over z, y).
Axes of the slice: x: 2, y: 2, z: 4, core: 2. Of those that a mesh axis runs over, the one named last changes fastest.
Arguments:
- inputs: bfloat16 [8, 4096, 512], P('dp', 'seq'), may hold values from -6 to 6
- starts: int32 [8, 8], P('dp', 'seq'), may hold values from 0 to 1, as said below
- attn_gain: float32 [512], replicated, may hold values from 0.5 to 1.5
- attn_shift: float32 [512], replicated, may hold values from -1.2 to 1.2
- query_weight: bfloat16 [512, 512], replicated, may hold values from -0.125 to 0.125
- key_weight: bfloat16 [512, 512], replicated, may hold values from -0.25 to 0.25
- value_weight: bfloat16 [512, 512], replicated, may hold values from -0.25 to 0.25
- control_weight: bfloat16 [512, 512], replicated, may hold values from -0.375 to 0.375
- output_weight: bfloat16 [512, 512], replicated, may hold values from -3 to 3
- ffn_gain: float32 [512], replicated, may hold values from 0.5 to 1.5
- ffn_shift: float32 [512], replicated, may hold values from -1.2 to 1.2
- up_weight: bfloat16 [512, 2048], replicated, may hold values from -0.25 to 0.25
- up_bias: float32 [2048], replicated, may hold values from -3 to 3
- down_weight: bfloat16 [2048, 512], replicated, may hold values from -0.125 to 0.125
- down_bias: float32 [512], replicated, may hold values from -1.8 to 1.8
- slot_means: float32 [8, 64], replicated, may hold values from 0.5 to 1.5
- cotangent: bfloat16 [8, 4096, 512], P('dp', 'seq'), may hold values from -6 to 6
Outputs:
- result: bfloat16 [8, 4096, 512], P('dp', 'seq')
- input_grad: float32 [8, 4096, 512], P('dp', 'seq')
- attn_gain_grad: float32 [512], replicated
- attn_shift_grad: float32 [512], replicated
- query_weight_grad: float32 [512, 512], replicated
- key_weight_grad: float32 [512, 512], replicated
- value_weight_grad: float32 [512, 512], replicated
- control_weight_grad: float32 [512, 512], replicated
- output_weight_grad: float32 [512, 512], replicated
- ffn_gain_grad: float32 [512], replicated
- ffn_shift_grad: float32 [512], replicated
- up_weight_grad: float32 [512, 2048], replicated
- up_bias_grad: float32 [2048], replicated
- down_weight_grad: float32 [2048, 512], replicated
- down_bias_grad: float32 [512], replicated
- new_means: float32 [8, 64], replicated
The draws below stay inside these ranges and needn't reach their ends.
Inputs may be any that keep to these rules, and one draw needn't show every extreme that they name: `starts`: 1 marks a block of 512 tokens at which a stream's memory begins anew; of the streams 2 p .. 2 p + 1 on one index of dp, one, drawn, has no mark at all.
All inputs are finite; a program needn't handle non-finite values.
Results may differ from the reference program's by a relative error of at most 0.014.
The reference program's roundings to bfloat16 on the way count: a program that leaves them out, or rounds other values in their place, can miss the bound.
Values sent between devices are 32-bit elements; how exact they have to be, the bound alone decides.
A program may use at most 256 MiB of HBM per device.

```python
import jax
import jax.numpy as jnp
from jax import lax

D = 512
HEADS = 8
HEAD = 64
SLOTS = 64
FF = 2048
BLOCK = 512
PAIR = 2
STREAMS = 8
BLOCKS = 8
LEN = 4096


def draw_starts(key, part):
    key = jax.random.fold_in(key, 11)
    choose_key, mark_key = jax.random.split(key)
    groups = STREAMS // PAIR
    longest = jax.random.randint(choose_key, (groups,), 0, PAIR)
    marked = (jax.random.randint(mark_key, (groups, PAIR, BLOCKS), 0, 4) == 0).astype(jnp.int32)
    row_index = jnp.arange(PAIR)
    others = (row_index[None, :] != longest[:, None]).astype(jnp.int32)
    return (marked * others[:, :, None]).reshape(STREAMS, BLOCKS)


def block_scale(stream_key, extent, cuts, least, top_value):
    level = 1.0
    for axis_at, shards_of in cuts:
        draws = jax.random.uniform(jax.random.fold_in(jax.random.fold_in(stream_key, 6), axis_at), (shards_of,), jnp.float32, least / len(cuts), top_value / len(cuts))
        level = level * jnp.repeat(jnp.exp(draws), extent[axis_at] // shards_of).reshape((-1,) + (1,) * (len(extent) - 1 - axis_at))
    return level


def scatter_about(rng, extent, width, limit, cuts=(), held_as=jnp.bfloat16):
    loudness = block_scale(rng, extent, cuts, -0.22, 0.18) if cuts else 1.0
    values = jax.random.normal(rng, extent, jnp.float32) * width * loudness
    return jnp.minimum(jnp.maximum(values, -limit), limit).astype(held_as)


def setup_inputs(seed: int = 0) -> dict:
    key_of = jax.random.split(jax.random.key(seed), 18)
    return {
        "inputs": scatter_about(key_of[0], (STREAMS, LEN, D), 1.0, 6.0, ((0, 4), (1, 8))),
        "starts": draw_starts(jax.random.fold_in(key_of[17], 71), 0),
        "attn_gain": jnp.clip(1.0 + 0.1 * jax.random.normal(key_of[2], (D,), jnp.float32), 0.5, 1.5),
        "attn_shift": scatter_about(key_of[3], (D,), 0.2, 1.2, (), jnp.float32),
        "query_weight": scatter_about(key_of[4], (D, D), (4 * D) ** -0.5, 0.125),
        "key_weight": scatter_about(key_of[5], (D, D), D ** -0.5, 0.25),
        "value_weight": scatter_about(key_of[6], (D, D), D ** -0.5, 0.25),
        "control_weight": scatter_about(key_of[7], (D, HEADS * SLOTS), (D // 2) ** -0.5, 0.375),
        "output_weight": scatter_about(key_of[8], (D, D), 4 ** -0.5, 3.0),
        "ffn_gain": jnp.clip(1.0 + 0.1 * jax.random.normal(key_of[9], (D,), jnp.float32), 0.5, 1.5),
        "ffn_shift": scatter_about(key_of[10], (D,), 0.2, 1.2, (), jnp.float32),
        "up_weight": scatter_about(key_of[11], (D, FF), D ** -0.5, 0.25),
        "up_bias": scatter_about(key_of[12], (FF,), 0.5, 3.0, (), jnp.float32),
        "down_weight": scatter_about(key_of[13], (FF, D), FF ** -0.5, 0.125),
        "down_bias": scatter_about(key_of[14], (D,), 0.3, 1.8, (), jnp.float32),
        "slot_means": jnp.clip(jax.random.uniform(key_of[15], (HEADS, SLOTS), jnp.float32, 0.5, 1.5), 0.5, 1.5),
        "cotangent": scatter_about(key_of[16], (STREAMS, LEN, D), 1.0, 6.0, ((0, 4), (1, 8))),
    }


EPSILON = 1e-05
HUGE_VALUE = 1e+30
HIGHEST = lax.Precision.HIGHEST

@jax.custom_vjp
def low(v):
    return lax.optimization_barrier(v.astype(jnp.bfloat16)).astype(jnp.float32)

@jax.custom_vjp
def low_back(v):
    return v

def low_keep(v):
    return (low(v), None)

def low_pass(kept, grad):
    return (grad,)

def back_keep(v):
    return (v, None)

def back_low(kept, grad):
    return (low(grad),)
low.defvjp(low_keep, low_pass)
low_back.defvjp(back_keep, back_low)

def layer_norm(values, gain, shift):
    centre = values - lax.optimization_barrier(jnp.mean(values, axis=-1, keepdims=True))
    spread = lax.optimization_barrier(jnp.mean(centre * centre, axis=-1, keepdims=True))
    return centre * lax.rsqrt(spread + EPSILON) * gain + shift

def matmul(left, right):
    return jnp.dot(left, right, precision=HIGHEST, preferred_element_type=jnp.float32)

def block_step(memory_state, pieces):
    past_max, past_total, past_memory = memory_state
    queries, keys_now, values_now, control, start_flag = pieces
    keeping = 1.0 - start_flag.astype(jnp.float32)
    block_max = jnp.floor(lax.optimization_barrier(jnp.max(control, axis=0)))
    ceiling = jnp.maximum(past_max, block_max)
    carried = keeping * jnp.exp(past_max - ceiling)
    prior_total = carried * past_total
    prior_memory = low(carried[:, :, None] * past_memory)
    prior_keys = prior_memory[:, :, :HEAD]
    prior_values = prior_memory[:, :, HEAD:]
    weights_now = jnp.exp(control - ceiling[None])
    length = control.shape[0]
    causal = (jnp.arange(length)[:, None] >= jnp.arange(length)[None, :]).astype(jnp.float32)
    totals = prior_total[None] + jnp.einsum('ts,shn->thn', causal, weights_now, precision=HIGHEST)
    weights_low = low(weights_now)
    raw_scores = jnp.einsum('thd,shd->hts', queries, keys_now, precision=HIGHEST) * causal[None]
    scores = low_back(low(raw_scores))
    numerator = low_back(jnp.einsum('thd,hnd->thn', queries, prior_keys, precision=HIGHEST) + jnp.einsum('hts,shn->thn', scores, weights_low, precision=HIGHEST))
    logits = numerator / totals
    probabilities = jax.nn.softmax(logits, axis=-1)
    shares = low(probabilities / totals)
    mixing = low_back(low(jnp.einsum('thn,shn->hts', shares, weights_low, precision=HIGHEST) * causal[None]))
    attended = jnp.einsum('thn,hnd->thd', shares, prior_values, precision=HIGHEST) + jnp.einsum('hts,shd->thd', mixing, values_now, precision=HIGHEST)
    writes = lax.optimization_barrier(jnp.sum(weights_now / totals, axis=0))
    local_weights = jnp.exp(control - block_max[None])
    local_total = lax.optimization_barrier(jnp.sum(local_weights, axis=0))
    pair_rows = jnp.concatenate([keys_now, values_now], axis=-1)
    local_memory = jnp.einsum('thn,thd->hnd', local_weights, pair_rows, precision=HIGHEST)
    factor = jnp.exp(block_max - ceiling)
    new_total = prior_total + factor * local_total
    new_memory = carried[:, :, None] * past_memory + factor[:, :, None] * local_memory
    return ((ceiling, new_total, new_memory), (attended, writes))

def stream_layer(tokens, flags, params):
    attn_gain, attn_shift, query_weight, key_weight, value_weight, control_weight, output_weight, ffn_gain, ffn_shift, up_weight, up_bias, down_weight, down_bias = params
    normed = low(layer_norm(tokens, attn_gain, attn_shift))
    queries = low_back(low(matmul(normed, query_weight)))
    keys_now = low_back(low(matmul(normed, key_weight)))
    values_now = low_back(low(matmul(normed, value_weight)))
    control = low_back(matmul(normed, control_weight))

    def split_heads(values, width_last):
        return values.reshape(BLOCKS, BLOCK, HEADS, width_last)
    start_state = (jnp.full((HEADS, SLOTS), -HUGE_VALUE, jnp.float32), jnp.zeros((HEADS, SLOTS), jnp.float32), jnp.zeros((HEADS, SLOTS, 2 * HEAD), jnp.float32))
    unused, (attended, writes) = lax.scan(jax.checkpoint(block_step), start_state, (split_heads(queries, HEAD), split_heads(keys_now, HEAD), split_heads(values_now, HEAD), split_heads(control, SLOTS), flags))
    mixed = low_back(low(attended.reshape(LEN, D)))
    hidden = tokens + low_back(matmul(mixed, output_weight))
    normed_ffn = low(layer_norm(hidden, ffn_gain, ffn_shift))
    raised = low_back(matmul(normed_ffn, up_weight) + up_bias)
    activated = low(jax.nn.gelu(raised))
    result = hidden + matmul(activated, down_weight) + down_bias
    return (result, lax.optimization_barrier(jnp.sum(writes, axis=0)))

def reference(inputs, starts, attn_gain, attn_shift, query_weight, key_weight, value_weight, control_weight, output_weight, ffn_gain, ffn_shift, up_weight, up_bias, down_weight, down_bias, slot_means, cotangent):
    params = tuple((weight.astype(jnp.float32) for weight in (attn_gain, attn_shift, query_weight, key_weight, value_weight, control_weight, output_weight, ffn_gain, ffn_shift, up_weight, up_bias, down_weight, down_bias)))

    def whole(tokens, weights):

        def one_stream(stream_item):
            return stream_layer(stream_item[0], stream_item[1], weights)
        results, writes = lax.map(jax.checkpoint(one_stream), (tokens, starts))
        return (results, lax.optimization_barrier(jnp.sum(writes, axis=0)))
    result, pullback, written = jax.vjp(whole, inputs.astype(jnp.float32), params, has_aux=True)
    input_grad, grads = pullback(cotangent.astype(jnp.float32))
    new_means = 0.9 * slot_means + 0.1 * written / STREAMS
    return (result.astype(jnp.bfloat16), input_grad, grads[0], grads[1], grads[2], grads[3], grads[4], grads[5], grads[6], grads[7], grads[8], grads[9], grads[10], grads[11], grads[12], new_means)
```

```python
import jax
import jax.numpy as jnp
from jax import lax
from jax.sharding import PartitionSpec as P

HEADS = 8
HEAD = 64
SLOTS = 64


EPSILON = 1e-05
HUGE_VALUE = 1e30
HIGHEST = lax.Precision.HIGHEST


def carried_in(part, axis, combine, identity, reverse):
    count = lax.axis_size(axis)
    place = lax.axis_index(axis)
    ahead = count - 1 - place if reverse else place
    gathered = jax.tree.map(lambda a: lax.all_gather(a, axis), part)
    state = jax.tree.map(lambda a, e: jnp.zeros_like(a) + jnp.asarray(e, a.dtype), part, identity)

    def one(step, state):
        source = count - 1 - step if reverse else step
        return combine(
            state, jax.tree.map(lambda a: lax.dynamic_index_in_dim(a, source, 0, False), gathered)
        )

    return lax.fori_loop(0, ahead, one, state)


def product(form, left, right):
    return jnp.einsum(form, left, right, preferred_element_type=jnp.float32)


def exact_product(form, left, right):
    return jnp.einsum(form, left, right, precision=HIGHEST, preferred_element_type=jnp.float32)


def running_sum(form, mask, values):
    high = values.astype(jnp.bfloat16)
    rest = (values - high.astype(jnp.float32)).astype(jnp.bfloat16)
    mask = mask.astype(jnp.bfloat16)
    return product(form, mask, high) + product(form, mask, rest)


def contract_rows(left, right):
    return lax.dot_general(
        left, right, (((0,), (0,)), ((), ())), preferred_element_type=jnp.float32
    )


def against_rows(left, right):
    return lax.dot_general(
        left, right, (((1,), (1,)), ((), ())), preferred_element_type=jnp.float32
    )


def norm_forward(values, gain, shift):
    centre = values - jnp.mean(values, axis=-1, keepdims=True)
    inverse = lax.rsqrt(jnp.mean(centre * centre, axis=-1, keepdims=True) + EPSILON)
    scaled = centre * inverse
    return (scaled * gain + shift, scaled, inverse)


def norm_backward(upstream, scaled, inverse, gain):
    inside = upstream * gain
    first = jnp.mean(inside, axis=-1, keepdims=True)
    second = jnp.mean(inside * scaled, axis=-1, keepdims=True)
    return (
        inverse * (inside - first - scaled * second),
        jnp.sum(upstream * scaled, axis=0),
        jnp.sum(upstream, axis=0),
    )


def advance(earlier, later):
    flag_old, max_old, total_old, memory_old = earlier
    flag_new, max_new, total_new, memory_new = later
    ceiling = jnp.maximum(max_old, max_new)
    old_factor = (1.0 - flag_new)[:, None, None] * jnp.exp(max_old - ceiling)
    new_factor = jnp.exp(max_new - ceiling)
    flagged = flag_old + flag_new - flag_old * flag_new
    return (
        flagged,
        ceiling,
        old_factor * total_old + new_factor * total_new,
        old_factor[..., None] * memory_old + new_factor[..., None] * memory_new,
    )


def retreat(earlier, later):
    flag_high, floor_high, total_high, memory_high = earlier
    flag_near, floor_near, total_near, memory_near = later
    lowest = jnp.minimum(floor_high, floor_near)
    near_factor = jnp.exp(lowest - floor_near)
    far_factor = (1.0 - flag_near)[:, None, None] * jnp.exp(lowest - floor_high)
    flagged = flag_near + flag_high - flag_near * flag_high
    return (
        flagged,
        lowest,
        near_factor * total_near + far_factor * total_high,
        near_factor[..., None] * memory_near + far_factor[..., None] * memory_high,
    )


def shards(
    inputs,
    starts,
    attn_gain,
    attn_shift,
    query_weight,
    key_weight,
    value_weight,
    control_weight,
    output_weight,
    ffn_gain,
    ffn_shift,
    up_weight,
    up_bias,
    down_weight,
    down_bias,
    slot_means,
    cotangent,
):
    streams, length, width = inputs.shape
    heads, head_size, slot_count = (HEADS, HEAD, SLOTS)
    row_count = streams * length
    tokens = inputs.astype(jnp.float32).reshape(row_count, width)
    normed, scaled_one, inverse_one = norm_forward(tokens, attn_gain, attn_shift)
    normed_low = normed.astype(jnp.bfloat16)
    queries = (
        jnp.dot(normed_low, query_weight, preferred_element_type=jnp.float32)
        .astype(jnp.bfloat16)
        .reshape(streams, length, heads, head_size)
    )
    keys_now = (
        jnp.dot(normed_low, key_weight, preferred_element_type=jnp.float32)
        .astype(jnp.bfloat16)
        .reshape(streams, length, heads, head_size)
    )
    values_now = (
        jnp.dot(normed_low, value_weight, preferred_element_type=jnp.float32)
        .astype(jnp.bfloat16)
        .reshape(streams, length, heads, head_size)
    )
    control = jnp.dot(normed_low, control_weight, preferred_element_type=jnp.float32).reshape(
        streams, length, heads, slot_count
    )
    block_max = jnp.floor(jnp.max(control, axis=1))
    local_weights = jnp.exp(control - block_max[:, None])
    local_total = jnp.sum(local_weights, axis=1)
    pair_rows = jnp.concatenate([keys_now, values_now], axis=-1).astype(jnp.float32)
    local_memory = exact_product("bthn,bthd->bhnd", local_weights, pair_rows)
    flags = starts[:, 0].astype(jnp.float32)
    forward_identity = (
        jnp.zeros_like(flags),
        jnp.full_like(block_max, -HUGE_VALUE),
        jnp.zeros_like(local_total),
        jnp.zeros_like(local_memory),
    )
    prefix = carried_in(
        (flags, block_max, local_total, local_memory), "seq", advance, forward_identity, False
    )
    prior_max = prefix[1]
    keeping = (1.0 - flags)[:, None, None]
    ceiling = jnp.maximum(prior_max, block_max)
    carried = keeping * jnp.exp(prior_max - ceiling)
    prior_total = carried * prefix[2]
    prior_memory = (carried[..., None] * prefix[3]).astype(jnp.bfloat16)
    prior_keys = prior_memory[..., :head_size]
    prior_values = prior_memory[..., head_size:]
    weights_now = jnp.exp(control - ceiling[:, None])
    causal = (
        lax.broadcasted_iota(jnp.int32, (length, length), 0)
        >= lax.broadcasted_iota(jnp.int32, (length, length), 1)
    ).astype(jnp.float32)
    totals = prior_total[:, None] + running_sum("ts,bshn->bthn", causal, weights_now)
    weights_low = weights_now.astype(jnp.bfloat16)
    scores = (product("bthd,bshd->bhts", queries, keys_now) * causal).astype(jnp.bfloat16)
    numerator = product("bthd,bhnd->bthn", queries, prior_keys) + product(
        "bhts,bshn->bthn", scores, weights_low
    )
    logits = numerator / totals
    probabilities = jax.nn.softmax(logits, axis=-1)
    shares = (probabilities / totals).astype(jnp.bfloat16)
    mixing = (product("bthn,bshn->bhts", shares, weights_low) * causal).astype(jnp.bfloat16)
    attended = product("bthn,bhnd->bthd", shares, prior_values) + product(
        "bhts,bshd->bthd", mixing, values_now
    )
    writes = jnp.sum(weights_now / totals, axis=(0, 1))
    mixed = attended.reshape(row_count, width).astype(jnp.bfloat16)
    hidden = tokens + jnp.dot(mixed, output_weight, preferred_element_type=jnp.float32)
    normed_ffn, scaled_two, inverse_two = norm_forward(hidden, ffn_gain, ffn_shift)
    normed_ffn_low = normed_ffn.astype(jnp.bfloat16)
    raised = jnp.dot(normed_ffn_low, up_weight, preferred_element_type=jnp.float32) + up_bias
    activated, gelu_pull = jax.vjp(jax.nn.gelu, raised)
    activated_low = activated.astype(jnp.bfloat16)
    result = (
        hidden + jnp.dot(activated_low, down_weight, preferred_element_type=jnp.float32) + down_bias
    )
    upstream = cotangent.reshape(row_count, width)
    upstream_wide = upstream.astype(jnp.float32)
    down_bias_grad = jnp.sum(upstream_wide, axis=0)
    down_weight_grad = contract_rows(activated_low, upstream)
    activated_grad = against_rows(upstream, down_weight)
    raised_grad = gelu_pull(activated_grad)[0].astype(jnp.bfloat16)
    up_weight_grad = contract_rows(normed_ffn_low, raised_grad)
    up_bias_grad = jnp.sum(raised_grad.astype(jnp.float32), axis=0)
    hidden_part, ffn_gain_grad, ffn_shift_grad = norm_backward(
        against_rows(raised_grad, up_weight), scaled_two, inverse_two, ffn_gain
    )
    hidden_grad = upstream_wide + hidden_part
    branch_grad = hidden_grad.astype(jnp.bfloat16)
    output_weight_grad = contract_rows(mixed, branch_grad)
    ffn_summed = lax.psum(
        (
            output_weight_grad,
            ffn_gain_grad,
            ffn_shift_grad,
            up_weight_grad,
            up_bias_grad,
            down_weight_grad,
            down_bias_grad,
            writes,
        ),
        ("dp", "seq"),
    )
    attended_grad = (
        against_rows(branch_grad, output_weight)
        .astype(jnp.bfloat16)
        .reshape(streams, length, heads, head_size)
    )
    mixing_grad = (product("bthd,bshd->bhts", attended_grad, values_now) * causal).astype(
        jnp.bfloat16
    )
    share_grad = product("bthd,bhnd->bthn", attended_grad, prior_values) + product(
        "bhts,bshn->bthn", mixing_grad, weights_low
    )
    prior_values_grad = product("bthn,bthd->bhnd", shares, attended_grad)
    values_grad = product("bhts,bthd->bshd", mixing, attended_grad)
    weights_grad = product("bhts,bthn->bshn", mixing_grad, shares)
    prob_grad = share_grad / totals
    logit_grad = probabilities * (
        prob_grad - jnp.sum(probabilities * prob_grad, axis=-1, keepdims=True)
    )
    totals_grad = -share_grad * probabilities / (totals * totals) - logit_grad * logits / totals
    numerator_grad = (logit_grad / totals).astype(jnp.bfloat16)
    scores_grad = (product("bthn,bshn->bhts", numerator_grad, weights_low) * causal).astype(
        jnp.bfloat16
    )
    queries_grad = product("bthn,bhnd->bthd", numerator_grad, prior_keys) + product(
        "bhts,bshd->bthd", scores_grad, keys_now
    )
    keys_grad = product("bhts,bthd->bshd", scores_grad, queries)
    prior_keys_grad = product("bthn,bthd->bhnd", numerator_grad, queries)
    weights_grad = (
        weights_grad
        + product("bhts,bthn->bshn", scores, numerator_grad)
        + running_sum("ts,bthn->bshn", causal, totals_grad)
    )
    prior_total_grad = jnp.sum(totals_grad, axis=1)
    memory_grad = jnp.concatenate([prior_keys_grad, prior_values_grad], axis=-1)
    backward_identity = (
        jnp.zeros_like(flags),
        jnp.full_like(ceiling, HUGE_VALUE),
        jnp.zeros_like(prior_total_grad),
        jnp.zeros_like(memory_grad),
    )
    suffix = carried_in(
        (flags, ceiling, keeping * prior_total_grad, keeping[..., None] * memory_grad),
        "seq",
        retreat,
        backward_identity,
        True,
    )
    reach = jnp.exp(block_max - suffix[1])
    local_total_grad = reach * suffix[2]
    local_memory_grad = reach[..., None] * suffix[3]
    local_weights_grad = (
        exact_product("bhnd,bthd->bthn", local_memory_grad, pair_rows) + local_total_grad[:, None]
    )
    pair_rows_grad = exact_product("bthn,bhnd->bthd", local_weights, local_memory_grad)
    control_grad = weights_grad * weights_now + local_weights_grad * local_weights
    queries_low = queries_grad.astype(jnp.bfloat16).reshape(row_count, width)
    keys_low = (
        (keys_grad + pair_rows_grad[..., :head_size]).astype(jnp.bfloat16).reshape(row_count, width)
    )
    values_low = (
        (values_grad + pair_rows_grad[..., head_size:])
        .astype(jnp.bfloat16)
        .reshape(row_count, width)
    )
    control_low = control_grad.astype(jnp.bfloat16).reshape(row_count, heads * slot_count)
    query_weight_grad = contract_rows(normed_low, queries_low)
    key_weight_grad = contract_rows(normed_low, keys_low)
    value_weight_grad = contract_rows(normed_low, values_low)
    control_weight_grad = contract_rows(normed_low, control_low)
    normed_grad = (
        against_rows(queries_low, query_weight)
        + against_rows(keys_low, key_weight)
        + against_rows(values_low, value_weight)
        + against_rows(control_low, control_weight)
    )
    token_part, attn_gain_grad, attn_shift_grad = norm_backward(
        normed_grad, scaled_one, inverse_one, attn_gain
    )
    input_grad = (hidden_grad + token_part).reshape(streams, length, width)
    attn_summed = lax.psum(
        (
            attn_gain_grad,
            attn_shift_grad,
            query_weight_grad,
            key_weight_grad,
            value_weight_grad,
            control_weight_grad,
        ),
        ("dp", "seq"),
    )
    new_means = 0.9 * slot_means + 0.1 * ffn_summed[7] / (streams * lax.axis_size("dp"))
    return (
        result.reshape(streams, length, width).astype(jnp.bfloat16),
        input_grad,
        attn_summed[0],
        attn_summed[1],
        attn_summed[2],
        attn_summed[3],
        attn_summed[4],
        attn_summed[5],
        ffn_summed[0],
        ffn_summed[1],
        ffn_summed[2],
        ffn_summed[3],
        ffn_summed[4],
        ffn_summed[5],
        ffn_summed[6],
        new_means,
    )


def solution(mesh):
    return jax.shard_map(
        shards,
        mesh=mesh,
        in_specs=(
            P("dp", "seq", None),
            P("dp", "seq"),
            P(),
            P(),
            P(),
            P(),
            P(),
            P(),
            P(),
            P(),
            P(),
            P(),
            P(),
            P(),
            P(),
            P(),
            P("dp", "seq", None),
        ),
        out_specs=(
            P("dp", "seq", None),
            P("dp", "seq", None),
            P(),
            P(),
            P(),
            P(),
            P(),
            P(),
            P(),
            P(),
            P(),
            P(),
            P(),
            P(),
            P(),
            P(),
        ),
        check_vma=False,
    )
```

```python
import functools

import jax
import jax.numpy as jnp
from jax import lax
from jax.experimental import pallas as pl
from jax.experimental.pallas import tpu as pltpu
from jax.sharding import PartitionSpec as P

HEADS = 8
HEAD = 64
SLOTS = 64
EPSILON = 1e-05
HUGE_VALUE = 1e30
MESH = pl.DeviceIdType.MESH
F32 = jnp.float32
BF16 = jnp.bfloat16
LANES = 128
HALF = 256


def mm(left, right):
    return lax.dot_general(left, right, (((1,), (0,)), ((), ())), preferred_element_type=F32)


def mm_lanes(left, right):
    return lax.dot_general(left, right, (((1,), (1,)), ((), ())), preferred_element_type=F32)


def mm_rows(left, right):
    return lax.dot_general(left, right, (((0,), (0,)), ((), ())), preferred_element_type=F32)


def iota(shape, axis):
    return lax.broadcasted_iota(jnp.int32, shape, axis)


def first_head(shape):
    return iota(shape, len(shape) - 1) < HEAD


def only_head(values, head):
    keep = first_head(values.shape) if head == 0 else jnp.logical_not(first_head(values.shape))
    return jnp.where(keep, values, jnp.zeros_like(values))


def both_blocks(rows):
    doubled = jnp.concatenate([rows, rows], axis=0)
    inside = (iota(doubled.shape, 0) < HEAD) == first_head(doubled.shape)
    return jnp.where(inside, doubled, jnp.zeros_like(doubled))


def one_block(square):
    return jnp.where(first_head((HEAD, LANES)), square[:HEAD], square[HEAD:])


def lower(shape=(HALF, HALF)):
    return iota(shape, 0) >= iota(shape, 1)


def upper(shape=(HALF, HALF)):
    return iota(shape, 0) <= iota(shape, 1)


def head_reduce(values, operation, empty):
    here = first_head(values.shape)
    one = operation(jnp.where(here, values, empty), axis=1, keepdims=True)
    two = operation(jnp.where(here, empty, values), axis=1, keepdims=True)
    return jnp.where(here, one, two)


def parts_of(values):
    high = values.astype(BF16)
    return jnp.concatenate([high, (values - high.astype(F32)).astype(BF16)], axis=1)


def add_parts(product):
    return product[:, :LANES] + product[:, LANES:]


def normalized(values):
    centre = values - jnp.mean(values, axis=-1, keepdims=True)
    inverse = lax.rsqrt(jnp.mean(centre * centre, axis=-1, keepdims=True) + EPSILON)
    return centre * inverse, inverse


HIGHEST = lax.Precision.HIGHEST
class Exchange:
    def __init__(self, size, sent, landed, send_sem, recv_sem):
        self.size, self.sent, self.landed = size, sent, landed
        self.send_sem, self.recv_sem = send_sem, recv_sem
        self.me = lax.axis_index("seq")

    def copy(self, to, slot):
        return pltpu.make_async_remote_copy(
            src_ref=self.sent.at[to],
            dst_ref=self.landed.at[slot],
            send_sem=self.send_sem.at[to],
            recv_sem=self.recv_sem.at[slot],
            device_id={"seq": to},
            device_id_type=MESH,
        )

    def send(self, to):
        @pl.when(to != self.me)
        def _():
            self.copy(to, self.me).start()

        @pl.when(to == self.me)
        def _():
            self.landed[self.me] = self.sent[self.me]

    def receive(self, slot):
        @pl.when(slot != self.me)
        def _():
            self.copy(slot, slot).wait_recv()

    def finish(self):
        def one(to, unused):
            @pl.when(to != self.me)
            def _():
                self.copy(to, self.me).wait_send()

            return unused

        lax.fori_loop(0, self.size, one, 0)


def greet(dp, seq):
    barrier = pltpu.get_barrier_semaphore()
    me = lax.axis_index("seq")
    for step in range(1, seq):
        pl.semaphore_signal(
            barrier, inc=1, device_id={"seq": lax.rem(me + step, seq)}, device_id_type=MESH
        )
    pl.semaphore_wait(barrier, seq - 1)


def block_of(combo):
    stream, pair = combo // 4, lax.rem(combo, 4)
    return (
        pl.multiple_of(stream * 512, 512),
        pl.multiple_of(pair * LANES, LANES),
    )


def forward_kernel(
    seq,
    tokens,
    flags,
    attn_gain,
    attn_shift,
    wq,
    wk,
    wv,
    wc,
    normed,
    queries,
    keys,
    values,
    local,
    weights,
    inverse_totals,
    logits,
    chances,
    shares,
    mixed,
    prior,
    notes,
    writes,
    numerators,
    sums,
    out_one,
    land_one,
    out_two,
    land_two,
    send_one,
    recv_one,
    send_two,
    recv_two,
):
    groups = seq // 8
    part = LANES // groups
    greet(4, seq)
    there = Exchange(seq, out_one, land_one, send_one, recv_one)
    back = Exchange(seq, out_two, land_two, send_two, recv_two)
    me = there.me

    def project(step, unused):
        rows = pl.ds(pl.multiple_of(step * HALF, HALF), HALF)
        scaled, _ = normalized(tokens[rows, :].astype(F32))
        low = (scaled * attn_gain[...] + attn_shift[...]).astype(BF16)
        normed[rows, :] = low
        local[rows, :] = mm(low, wc[...])
        keys[rows, :] = mm(low, wk[...]).astype(BF16)
        values[rows, :] = mm(low, wv[...]).astype(BF16)
        return unused

    def summarize(combo, unused):
        row, col = block_of(combo)
        rows, cols = pl.ds(row, 512), pl.ds(col, LANES)
        control = local[rows, cols]
        block_max = jnp.floor(jnp.max(control, axis=0, keepdims=True))
        spread = jnp.exp(control - block_max)
        local[rows, cols] = spread
        pair_rows = jnp.concatenate([keys[rows, cols], values[rows, cols]], axis=1)
        memory = add_parts(mm_rows(pair_rows, parts_of(spread)))
        memory = jnp.concatenate([one_block(memory[:LANES]), one_block(memory[LANES:])], axis=0)
        total = jnp.sum(spread, axis=0, keepdims=True)
        flag = flags[pl.ds(combo // 4, 1), :]
        line = iota((8, LANES), 0)
        small = jnp.where(line == 0, block_max, jnp.where(line == 1, total, flag))
        notes[combo] = small
        for group in range(groups):
            to = combo * groups + group
            out_one[to, :part] = memory[group * part : (group + 1) * part]
            out_one[to, part:] = small
            there.send(to)
        return unused

    for stream in range(2):
        lax.fori_loop(2 * stream, 2 * stream + 2, project, 0)
        lax.fori_loop(4 * stream, 4 * stream + 4, summarize, 0)

    def project_query(step, unused):
        rows = pl.ds(pl.multiple_of(step * HALF, HALF), HALF)
        queries[rows, :] = mm(normed[rows, :], wq[...]).astype(BF16)
        return unused

    lax.fori_loop(0, 4, project_query, 0)

    def inside(combo, unused):
        row, col = block_of(combo)
        cols = pl.ds(col, LANES)
        spread = local[pl.ds(row, 512), cols]
        low = spread.astype(BF16)
        triangle = lower()
        ones = jnp.where(triangle, 1.0, 0.0).astype(BF16)
        first = add_parts(mm(ones, parts_of(spread[:HALF])))
        second = add_parts(mm(ones, parts_of(spread[HALF:]))) + first[HALF - 1 :]
        sums[pl.ds(row, HALF), cols] = first
        sums[pl.ds(row + HALF, HALF), cols] = second
        for at in range(2):
            rows = pl.ds(row + at * HALF, HALF)
            width = (at + 1) * HALF
            total = None
            for head in range(2):
                query = only_head(queries[rows, cols], head)
                found = []
                for other in range(at + 1):
                    score = mm_lanes(query, keys[pl.ds(row + other * HALF, HALF), cols])
                    if other == at:
                        score = jnp.where(triangle, score, 0.0)
                    found.append(score.astype(BF16))
                score = found[0] if at == 0 else jnp.concatenate(found, axis=1)
                term = mm(score, only_head(low[:width], head))
                total = term if total is None else total + term
            numerators[rows, cols] = total
        return unused

    lax.fori_loop(0, 4, inside, 0)

    prior_max = jnp.full((1, LANES), -HUGE_VALUE, F32)
    raw_total = jnp.zeros((1, LANES), F32)
    raw_memory = jnp.zeros((part, LANES), F32)
    for source in range(seq):
        out_two[source, :part] = raw_memory
        line = iota((8, LANES), 0)
        out_two[source, part:] = jnp.where(line == 0, prior_max, raw_total)
        back.send(source)
        if source == seq - 1:
            there.receive(source)
            break
        there.receive(source)
        block_max = land_one[source, part : part + 1]
        total = land_one[source, part + 1 : part + 2]
        flag = land_one[source, part + 2 : part + 3]
        ceiling = jnp.maximum(prior_max, block_max)
        old = (1.0 - flag) * jnp.exp(prior_max - ceiling)
        new = jnp.exp(block_max - ceiling)
        raw_total = old * raw_total + new * total
        raw_memory = old * raw_memory + new * land_one[source, :part]
        prior_max = ceiling

    lax.fori_loop(4, 8, inside, 0)

    def attend(combo, unused):
        row, col = block_of(combo)
        cols = pl.ds(col, LANES)
        for group in range(groups):
            back.receive(combo * groups + group)
        if groups == 1:
            memory = land_two[combo, :LANES]
        else:
            memory = jnp.concatenate(
                [land_two[combo * groups + group, :part] for group in range(groups)], axis=0
            )
        past_max = land_two[combo * groups, part : part + 1]
        past_total = land_two[combo * groups, part + 1 : part + 2]
        block_max = notes[combo, 0:1]
        flag = notes[combo, 2:3]
        ceiling = jnp.maximum(past_max, block_max)
        carried = (1.0 - flag) * jnp.exp(past_max - ceiling)
        factor = jnp.exp(block_max - ceiling)
        notes[combo, 1:2] = ceiling
        memory = (carried * memory).astype(BF16)
        prior[combo] = memory
        prior_keys = both_blocks(memory[:HEAD])
        prior_values = both_blocks(memory[HEAD:])
        triangle = lower()
        written = jnp.zeros((1, LANES), F32)
        for at in range(2):
            rows = pl.ds(row + at * HALF, HALF)
            weight = local[rows, cols] * factor
            weights[rows, cols] = weight.astype(BF16)
            inverse = 1.0 / (carried * past_total + factor * sums[rows, cols])
            inverse_totals[rows, cols] = inverse
            written = written + jnp.sum(weight * inverse, axis=0, keepdims=True)
            logit = (mm(queries[rows, cols], prior_keys) + factor * numerators[rows, cols]) * inverse
            logits[rows, cols] = logit
            top = head_reduce(logit, jnp.max, -HUGE_VALUE)
            raised = jnp.exp(logit - top)
            chance = raised / head_reduce(raised, jnp.sum, 0.0)
            chances[rows, cols] = chance
            share = (chance * inverse).astype(BF16)
            shares[rows, cols] = share
            attended = mm_lanes(share, prior_values)
            for head in range(2):
                own = only_head(share, head)
                for other in range(at + 1):
                    these = pl.ds(row + other * HALF, HALF)
                    mixing = mm_lanes(own, weights[these, cols])
                    if other == at:
                        mixing = jnp.where(triangle, mixing, 0.0)
                    attended = attended + mm(
                        mixing.astype(BF16), only_head(values[these, cols], head)
                    )
            mixed[rows, cols] = attended.astype(BF16)
        writes[combo] = jnp.broadcast_to(written, (8, LANES))
        return unused

    lax.fori_loop(0, 8, attend, 0)
    there.finish()
    back.finish()


def vmem():
    return pl.BlockSpec(memory_space=pltpu.VMEM)


def forward_call(seq, tokens, flags, attn_gain, attn_shift, wq, wk, wv, wc):
    rows, width = tokens.shape
    part = LANES // (seq // 8)
    wide = jax.ShapeDtypeStruct((rows, width), F32)
    slim = jax.ShapeDtypeStruct((rows, width), BF16)
    small = jax.ShapeDtypeStruct((8, 8, LANES), F32)
    blocks = pltpu.VMEM((seq, part + 8, LANES), F32)
    outs = [slim, slim, slim, slim, wide, slim, wide, wide, wide, slim, slim]
    outs += [jax.ShapeDtypeStruct((8, LANES, LANES), BF16), small, small]
    return pl.pallas_call(
        functools.partial(forward_kernel, seq),
        out_shape=outs,
        in_specs=[vmem()] * 8,
        out_specs=[vmem()] * len(outs),
        scratch_shapes=[
            pltpu.VMEM((rows, width), F32),
            pltpu.VMEM((rows, width), F32),
            blocks,
            blocks,
            blocks,
            blocks,
        ]
        + [pltpu.SemaphoreType.DMA((seq,))] * 4,
        compiler_params=pltpu.CompilerParams(
            collective_id=1, has_side_effects=True, vmem_limit_bytes=60 * 2**20
        ),
        name="forward",
    )(tokens, flags, attn_gain, attn_shift, wq, wk, wv, wc)


def carried_in(part, axis, combine, identity, reverse):
    count = lax.axis_size(axis)
    place = lax.axis_index(axis)
    ahead = count - 1 - place if reverse else place
    gathered = jax.tree.map(lambda a: lax.all_gather(a, axis), part)
    state = jax.tree.map(lambda a, e: jnp.zeros_like(a) + jnp.asarray(e, a.dtype), part, identity)

    def one(step, state):
        source = count - 1 - step if reverse else step
        return combine(
            state, jax.tree.map(lambda a: lax.dynamic_index_in_dim(a, source, 0, False), gathered)
        )

    return lax.fori_loop(0, ahead, one, state)


def product(form, left, right):
    return jnp.einsum(form, left, right, preferred_element_type=jnp.float32)


def exact_product(form, left, right):
    return jnp.einsum(form, left, right, precision=HIGHEST, preferred_element_type=jnp.float32)


def running_sum(form, mask, values):
    high = values.astype(jnp.bfloat16)
    rest = (values - high.astype(jnp.float32)).astype(jnp.bfloat16)
    mask = mask.astype(jnp.bfloat16)
    return product(form, mask, high) + product(form, mask, rest)


def contract_rows(left, right):
    return lax.dot_general(
        left, right, (((0,), (0,)), ((), ())), preferred_element_type=jnp.float32
    )


def against_rows(left, right):
    return lax.dot_general(
        left, right, (((1,), (1,)), ((), ())), preferred_element_type=jnp.float32
    )


def norm_forward(values, gain, shift):
    centre = values - jnp.mean(values, axis=-1, keepdims=True)
    inverse = lax.rsqrt(jnp.mean(centre * centre, axis=-1, keepdims=True) + EPSILON)
    scaled = centre * inverse
    return (scaled * gain + shift, scaled, inverse)


def norm_backward(upstream, scaled, inverse, gain):
    inside = upstream * gain
    first = jnp.mean(inside, axis=-1, keepdims=True)
    second = jnp.mean(inside * scaled, axis=-1, keepdims=True)
    return (
        inverse * (inside - first - scaled * second),
        jnp.sum(upstream * scaled, axis=0),
        jnp.sum(upstream, axis=0),
    )


def advance(earlier, later):
    flag_old, max_old, total_old, memory_old = earlier
    flag_new, max_new, total_new, memory_new = later
    ceiling = jnp.maximum(max_old, max_new)
    old_factor = (1.0 - flag_new)[:, None, None] * jnp.exp(max_old - ceiling)
    new_factor = jnp.exp(max_new - ceiling)
    flagged = flag_old + flag_new - flag_old * flag_new
    return (
        flagged,
        ceiling,
        old_factor * total_old + new_factor * total_new,
        old_factor[..., None] * memory_old + new_factor[..., None] * memory_new,
    )


def retreat(earlier, later):
    flag_high, floor_high, total_high, memory_high = earlier
    flag_near, floor_near, total_near, memory_near = later
    lowest = jnp.minimum(floor_high, floor_near)
    near_factor = jnp.exp(lowest - floor_near)
    far_factor = (1.0 - flag_near)[:, None, None] * jnp.exp(lowest - floor_high)
    flagged = flag_near + flag_high - flag_near * flag_high
    return (
        flagged,
        lowest,
        near_factor * total_near + far_factor * total_high,
        near_factor[..., None] * memory_near + far_factor[..., None] * memory_high,
    )


def shards(
    inputs,
    starts,
    attn_gain,
    attn_shift,
    query_weight,
    key_weight,
    value_weight,
    control_weight,
    output_weight,
    ffn_gain,
    ffn_shift,
    up_weight,
    up_bias,
    down_weight,
    down_bias,
    slot_means,
    cotangent,
):
    streams, length, width = inputs.shape
    heads, head_size, slot_count = (HEADS, HEAD, SLOTS)
    row_count = streams * length
    tokens_low = inputs.reshape(row_count, width)
    tokens = tokens_low.astype(jnp.float32)
    flags = starts[:, 0].astype(jnp.float32)
    (normed_low, queries, keys_now, values_now, local_weights, weights_low, inverse_totals, logits, probabilities, shares, mixed, prior, notes, writes) = forward_call(
        lax.axis_size("seq"), tokens_low, jnp.broadcast_to(flags[:, None], (2, LANES)), attn_gain[None], attn_shift[None],
        query_weight, key_weight, value_weight, control_weight)
    _, scaled_one, inverse_one = norm_forward(tokens, attn_gain, attn_shift)
    def split(a): return a.reshape(streams, length, heads, head_size)
    queries, keys_now, values_now, local_weights, weights_low, inverse_totals, logits, probabilities, shares = [split(a) for a in (queries, keys_now, values_now, local_weights, weights_low, inverse_totals, logits, probabilities, shares)]
    totals = 1.0 / inverse_totals
    def row(i): return notes[:, i].reshape(streams, heads, slot_count)
    block_max, ceiling = row(0), row(1)
    keeping = (1.0 - flags)[:, None, None]
    weights_now = local_weights * jnp.exp(block_max - ceiling)[:, None]
    prior = prior.reshape(streams, 4, 2, head_size, 2, slot_count)
    prior = jnp.transpose(prior, (2, 0, 1, 4, 5, 3)).reshape(2, streams, heads, slot_count, head_size)
    prior_keys, prior_values = prior[0], prior[1]
    writes = jnp.sum(writes[:, 0].reshape(streams, heads, slot_count), axis=0)
    pair_rows = jnp.concatenate([keys_now, values_now], axis=-1).astype(jnp.float32)
    causal = (
        lax.broadcasted_iota(jnp.int32, (length, length), 0)
        >= lax.broadcasted_iota(jnp.int32, (length, length), 1)
    ).astype(jnp.float32)
    scores = (product("bthd,bshd->bhts", queries, keys_now) * causal).astype(jnp.bfloat16)
    mixing = (product("bthn,bshn->bhts", shares, weights_low) * causal).astype(jnp.bfloat16)
    hidden = tokens + jnp.dot(mixed, output_weight, preferred_element_type=jnp.float32)
    normed_ffn, scaled_two, inverse_two = norm_forward(hidden, ffn_gain, ffn_shift)
    normed_ffn_low = normed_ffn.astype(jnp.bfloat16)
    raised = jnp.dot(normed_ffn_low, up_weight, preferred_element_type=jnp.float32) + up_bias
    activated, gelu_pull = jax.vjp(jax.nn.gelu, raised)
    activated_low = activated.astype(jnp.bfloat16)
    result = (
        hidden + jnp.dot(activated_low, down_weight, preferred_element_type=jnp.float32) + down_bias
    )
    upstream = cotangent.reshape(row_count, width)
    upstream_wide = upstream.astype(jnp.float32)
    down_bias_grad = jnp.sum(upstream_wide, axis=0)
    down_weight_grad = contract_rows(activated_low, upstream)
    activated_grad = against_rows(upstream, down_weight)
    raised_grad = gelu_pull(activated_grad)[0].astype(jnp.bfloat16)
    up_weight_grad = contract_rows(normed_ffn_low, raised_grad)
    up_bias_grad = jnp.sum(raised_grad.astype(jnp.float32), axis=0)
    hidden_part, ffn_gain_grad, ffn_shift_grad = norm_backward(
        against_rows(raised_grad, up_weight), scaled_two, inverse_two, ffn_gain
    )
    hidden_grad = upstream_wide + hidden_part
    branch_grad = hidden_grad.astype(jnp.bfloat16)
    output_weight_grad = contract_rows(mixed, branch_grad)
    ffn_summed = lax.psum(
        (
            output_weight_grad,
            ffn_gain_grad,
            ffn_shift_grad,
            up_weight_grad,
            up_bias_grad,
            down_weight_grad,
            down_bias_grad,
            writes,
        ),
        ("dp", "seq"),
    )
    attended_grad = (
        against_rows(branch_grad, output_weight)
        .astype(jnp.bfloat16)
        .reshape(streams, length, heads, head_size)
    )
    mixing_grad = (product("bthd,bshd->bhts", attended_grad, values_now) * causal).astype(
        jnp.bfloat16
    )
    share_grad = product("bthd,bhnd->bthn", attended_grad, prior_values) + product(
        "bhts,bshn->bthn", mixing_grad, weights_low
    )
    prior_values_grad = product("bthn,bthd->bhnd", shares, attended_grad)
    values_grad = product("bhts,bthd->bshd", mixing, attended_grad)
    weights_grad = product("bhts,bthn->bshn", mixing_grad, shares)
    prob_grad = share_grad / totals
    logit_grad = probabilities * (
        prob_grad - jnp.sum(probabilities * prob_grad, axis=-1, keepdims=True)
    )
    totals_grad = -share_grad * probabilities / (totals * totals) - logit_grad * logits / totals
    numerator_grad = (logit_grad / totals).astype(jnp.bfloat16)
    scores_grad = (product("bthn,bshn->bhts", numerator_grad, weights_low) * causal).astype(
        jnp.bfloat16
    )
    queries_grad = product("bthn,bhnd->bthd", numerator_grad, prior_keys) + product(
        "bhts,bshd->bthd", scores_grad, keys_now
    )
    keys_grad = product("bhts,bthd->bshd", scores_grad, queries)
    prior_keys_grad = product("bthn,bthd->bhnd", numerator_grad, queries)
    weights_grad = (
        weights_grad
        + product("bhts,bthn->bshn", scores, numerator_grad)
        + running_sum("ts,bthn->bshn", causal, totals_grad)
    )
    prior_total_grad = jnp.sum(totals_grad, axis=1)
    memory_grad = jnp.concatenate([prior_keys_grad, prior_values_grad], axis=-1)
    backward_identity = (
        jnp.zeros_like(flags),
        jnp.full_like(ceiling, HUGE_VALUE),
        jnp.zeros_like(prior_total_grad),
        jnp.zeros_like(memory_grad),
    )
    suffix = carried_in(
        (flags, ceiling, keeping * prior_total_grad, keeping[..., None] * memory_grad),
        "seq",
        retreat,
        backward_identity,
        True,
    )
    reach = jnp.exp(block_max - suffix[1])
    local_total_grad = reach * suffix[2]
    local_memory_grad = reach[..., None] * suffix[3]
    local_weights_grad = (
        exact_product("bhnd,bthd->bthn", local_memory_grad, pair_rows) + local_total_grad[:, None]
    )
    pair_rows_grad = exact_product("bthn,bhnd->bthd", local_weights, local_memory_grad)
    control_grad = weights_grad * weights_now + local_weights_grad * local_weights
    queries_low = queries_grad.astype(jnp.bfloat16).reshape(row_count, width)
    keys_low = (
        (keys_grad + pair_rows_grad[..., :head_size]).astype(jnp.bfloat16).reshape(row_count, width)
    )
    values_low = (
        (values_grad + pair_rows_grad[..., head_size:])
        .astype(jnp.bfloat16)
        .reshape(row_count, width)
    )
    control_low = control_grad.astype(jnp.bfloat16).reshape(row_count, heads * slot_count)
    query_weight_grad = contract_rows(normed_low, queries_low)
    key_weight_grad = contract_rows(normed_low, keys_low)
    value_weight_grad = contract_rows(normed_low, values_low)
    control_weight_grad = contract_rows(normed_low, control_low)
    normed_grad = (
        against_rows(queries_low, query_weight)
        + against_rows(keys_low, key_weight)
        + against_rows(values_low, value_weight)
        + against_rows(control_low, control_weight)
    )
    token_part, attn_gain_grad, attn_shift_grad = norm_backward(
        normed_grad, scaled_one, inverse_one, attn_gain
    )
    input_grad = (hidden_grad + token_part).reshape(streams, length, width)
    attn_summed = lax.psum(
        (
            attn_gain_grad,
            attn_shift_grad,
            query_weight_grad,
            key_weight_grad,
            value_weight_grad,
            control_weight_grad,
        ),
        ("dp", "seq"),
    )
    new_means = 0.9 * slot_means + 0.1 * ffn_summed[7] / (streams * lax.axis_size("dp"))
    return (
        result.reshape(streams, length, width).astype(jnp.bfloat16),
        input_grad,
        attn_summed[0],
        attn_summed[1],
        attn_summed[2],
        attn_summed[3],
        attn_summed[4],
        attn_summed[5],
        ffn_summed[0],
        ffn_summed[1],
        ffn_summed[2],
        ffn_summed[3],
        ffn_summed[4],
        ffn_summed[5],
        ffn_summed[6],
        new_means,
    )


def solution(mesh):
    return jax.shard_map(
        shards,
        mesh=mesh,
        in_specs=(
            P("dp", "seq", None),
            P("dp", "seq"),
            P(),
            P(),
            P(),
            P(),
            P(),
            P(),
            P(),
            P(),
            P(),
            P(),
            P(),
            P(),
            P(),
            P(),
            P("dp", "seq", None),
        ),
        out_specs=(
            P("dp", "seq", None),
            P("dp", "seq", None),
            P(),
            P(),
            P(),
            P(),
            P(),
            P(),
            P(),
            P(),
            P(),
            P(),
            P(),
            P(),
            P(),
            P(),
        ),
        check_vma=False,
    )
```

```python
import types

import jax
import jax.numpy as jnp
from jax import lax
from jax.experimental import pallas as pl
from jax.experimental.pallas import tpu as pltpu
from jax.sharding import PartitionSpec as P

HEADS = 8
HEAD = 64
SLOTS = 64
EPSILON = 1e-05
HUGE_VALUE = 1e30
MESH = pl.DeviceIdType.MESH
F32 = jnp.float32
BF16 = jnp.bfloat16
LANES = 128
HALF = 256
DP, SEQ = "dp", "seq"
CORE, LINE, NEAR, FAR = range(4)


def mm(left, right):
    return lax.dot_general(left, right, (((1,), (0,)), ((), ())), preferred_element_type=F32)


def mm_lanes(left, right):
    return lax.dot_general(left, right, (((1,), (1,)), ((), ())), preferred_element_type=F32)


def mm_rows(left, right):
    return lax.dot_general(left, right, (((0,), (0,)), ((), ())), preferred_element_type=F32)


def iota(shape, axis):
    return lax.broadcasted_iota(jnp.int32, shape, axis)


def first_head(shape):
    return iota(shape, len(shape) - 1) < HEAD


def only_head(values, head):
    keep = first_head(values.shape) if head == 0 else jnp.logical_not(first_head(values.shape))
    return jnp.where(keep, values, jnp.zeros_like(values))


def both_blocks(rows):
    doubled = jnp.concatenate([rows, rows], axis=0)
    inside = (iota(doubled.shape, 0) < HEAD) == first_head(doubled.shape)
    return jnp.where(inside, doubled, jnp.zeros_like(doubled))


def one_block(square):
    return jnp.where(first_head((HEAD, LANES)), square[:HEAD], square[HEAD:])


def lower(shape=(HALF, HALF)):
    return iota(shape, 0) >= iota(shape, 1)


def upper(shape=(HALF, HALF)):
    return iota(shape, 0) <= iota(shape, 1)


def head_reduce(values, operation, empty):
    here = first_head(values.shape)
    one = operation(jnp.where(here, values, empty), axis=1, keepdims=True)
    two = operation(jnp.where(here, empty, values), axis=1, keepdims=True)
    return jnp.where(here, one, two)


def parts_of(values):
    high = values.astype(BF16)
    return jnp.concatenate([high, (values - high.astype(F32)).astype(BF16)], axis=1)


def add_parts(product):
    return product[:, :LANES] + product[:, LANES:]


def normalized(values):
    centre = values - jnp.mean(values, axis=-1, keepdims=True)
    inverse = lax.rsqrt(jnp.mean(centre * centre, axis=-1, keepdims=True) + EPSILON)
    return centre * inverse, inverse


class Exchange:
    def __init__(self, size, sent, landed, send_sem, recv_sem):
        self.size, self.sent, self.landed = size, sent, landed
        self.send_sem, self.recv_sem = send_sem, recv_sem
        self.me = lax.axis_index(SEQ)

    def copy(self, source, target, to):
        return pltpu.make_async_remote_copy(
            src_ref=source,
            dst_ref=target,
            send_sem=self.send_sem,
            recv_sem=self.recv_sem,
            device_id={SEQ: to},
            device_id_type=MESH,
        )

    def send(self, to):
        @pl.when(to != self.me)
        def _():
            self.copy(self.sent.at[to], self.landed.at[self.me], to).start()

        @pl.when(to == self.me)
        def _():
            self.landed[self.me] = self.sent[self.me]

    def send_all(self):
        self.landed[self.me] = self.sent[self.me]
        for step in range(1, self.size):
            to = lax.rem(self.me + step, self.size)
            self.copy(self.sent.at[to], self.landed.at[self.me], to).start()

    def receive(self):
        others = self.landed.at[pl.ds(0, self.size - 1)]
        self.copy(others, others, lax.rem(self.me + 1, self.size)).wait_recv()

    def finish(self):
        others = self.sent.at[pl.ds(0, self.size - 1)]
        self.copy(others, others, lax.rem(self.me + 1, self.size)).wait_send()


class Reduction:
    def __init__(self, dp, seq, held, landed, full, send_sem, recv_sem, keep_sem):
        self.held, self.landed, self.full = held, landed, full
        self.send_sem, self.recv_sem, self.keep_sem = send_sem, recv_sem, keep_sem
        dp_at, seq_at = lax.axis_index(DP), lax.axis_index(SEQ)
        slow, fast = 4, seq // 4
        core, line = lax.rem(dp_at, 2), dp_at // 2
        near, far = lax.rem(seq_at, fast), seq_at // fast
        self.groups = {
            CORE: (2, core, lambda m: {DP: line * 2 + m}),
            LINE: (dp // 2, line, lambda m: {DP: m * 2 + core}),
            NEAR: (fast, near, lambda m: {SEQ: far * fast + m}),
            FAR: (slow, far, lambda m: {SEQ: m * fast + near}),
        }
        self.ways = dp // 2 * fast * slow

    def orders(self, rows, index):
        half = rows // 2
        ways = [(LINE, NEAR, FAR), (NEAR, LINE, FAR)]
        if half % (2 * self.ways * 8) == 0:
            return [(0, half // 2, ways[0]), (half // 2, half // 2, ways[1])]
        return [(0, half, ways[index % 2])]

    def steps(self, chunk, level):
        base, rows, land, index = chunk
        core = self.groups[CORE][1]
        if level == 0:
            return [(base, rows // 2, CORE, land)], rows // 2
        orders = self.orders(rows, index)
        place = land + rows // 2
        sizes = [size for _, size, _ in orders]
        starts = [base + core * (rows // 2) + offset for offset, _, _ in orders]
        for depth in range(level):
            found = []
            first = place
            for at, (_, _, axes) in enumerate(orders):
                name = axes[depth]
                count, mine, _ = self.groups[name]
                sizes[at] //= count
                found.append((starts[at], sizes[at], name, place))
                starts[at] = starts[at] + mine * sizes[at]
                place = place + sizes[at] * (count - 1)
        return found, sum(size * (self.groups[name][0] - 1) for _, size, name, _ in found)

    def rows_sent(self, chunk):
        return 2 * sum(self.steps(chunk, level)[1] for level in range(4))

    def copy(self, chunk, slot, source, target, device):
        return pltpu.make_async_remote_copy(
            src_ref=source,
            dst_ref=target,
            send_sem=self.send_sem.at[chunk[3]],
            recv_sem=self.recv_sem.at[chunk[3], slot],
            device_id=device,
            device_id_type=MESH,
        )

    def start(self, chunk, level, gather):
        for start, size, name, land in self.steps(chunk, level)[0]:
            count, at, device = self.groups[name]
            for k in range(1, count):
                to = lax.rem(at + k, count)
                if gather:
                    rows = pl.ds(pl.multiple_of(start + at * size, 8), size)
                    source = (self.held if level == 3 else self.full).at[rows]
                    target = self.full.at[rows]
                else:
                    source = self.held.at[pl.ds(pl.multiple_of(start + to * size, 8), size)]
                    target = self.landed.at[pl.ds(pl.multiple_of(land + (k - 1) * size, 8), size)]
                self.copy(chunk, level + 4 * gather, source, target, device(to)).start()
            if gather and level == 3:
                rows = pl.ds(pl.multiple_of(start + at * size, 8), size)
                pltpu.make_async_copy(
                    self.held.at[rows], self.full.at[rows], self.keep_sem.at[chunk[3]]
                ).start()

    def wait(self, chunk, level, gather):
        steps, rows = self.steps(chunk, level)
        at = pl.ds(chunk[0], rows) if gather else pl.ds(steps[0][3], rows)
        ref = (self.full if gather else self.landed).at[at]
        self.copy(chunk, level + 4 * gather, ref, ref, self.groups[CORE][2](0)).wait_recv()
        if gather and level == 3:
            at = pl.ds(chunk[0], sum(size for _, size, _, _ in steps))
            pltpu.make_async_copy(
                self.held.at[at], self.full.at[at], self.keep_sem.at[chunk[3]]
            ).wait()

    def finish(self, chunk):
        ref = self.held.at[pl.ds(0, self.rows_sent(chunk))]
        self.copy(chunk, 0, ref, ref, self.groups[CORE][2](0)).wait_send()

    def add(self, chunk, level):
        for start, size, name, land in self.steps(chunk, level)[0]:
            count, at, _ = self.groups[name]
            block = min(size, 512)

            def one(step, unused, start=start, size=size, land=land, at=at, count=count, block=block):
                rows = pl.ds(pl.multiple_of(start + at * size + step * block, 8), block)
                total = self.held[rows]
                for k in range(1, count):
                    found = pl.ds(pl.multiple_of(land + (k - 1) * size + step * block, 8), block)
                    total = total + self.landed[found]
                self.held[rows] = total
                return unused

            if size == block:
                one(0, 0)
            else:
                lax.fori_loop(0, size // block, one, 0)

    def stage(self, chunk, number):
        if number:
            level, gather = (number - 1, False) if number <= 4 else (8 - number, True)
            self.wait(chunk, level, gather)
            if not gather:
                self.add(chunk, level)
        if number < 8:
            self.start(chunk, *((number, False) if number < 4 else (7 - number, True)))


def timetable(costs, begins):
    line = {0: (0, 0.9), 1: (1, 2.9), 2: (1, 1.5), 3: (2, 2.9)}
    now, free, ready, following = 0.0, [0.0] * 3, {}, {}
    table = [[] for _ in costs] + [[]]

    def take(chunk, number, place):
        nonlocal now
        now += EVENT
        place.append((chunk, number))
        following[chunk] = number + 1
        if number == 8:
            del following[chunk], ready[chunk]
            return
        link, cost = line[min(number, 7 - number)]
        free[link] = max(now, free[link]) + (cost if chunk < 13 else cost / 4)
        ready[chunk] = free[link] + LATENCY

    for moment, cost in enumerate(costs):
        now += cost
        for chunk, begin in enumerate(begins):
            if begin == moment:
                take(chunk, 0, table[moment])
        while True:
            able = [chunk for chunk in following if ready[chunk] <= now]
            if not able:
                break
            take(min(able), following[min(able)], table[moment])
    while following:
        chunk = min(following, key=lambda at: (ready[at], at))
        now = max(now, ready[chunk])
        take(chunk, following[chunk], table[-1])
    return table


def block_of(combo):
    stream, pair = combo // 4, lax.rem(combo, 4)
    return (
        pl.multiple_of(stream * 512, 512),
        pl.multiple_of(pair * LANES, LANES),
    )


def gelu_parts(raised):
    root = 0.7978845608028654
    square = raised * raised
    bent = jnp.tanh(root * raised * (1.0 + 0.044715 * square))
    half = 0.5 * (1.0 + bent)
    slope = half + (0.5 * root) * raised * (1.0 - bent * bent) * (1.0 + 0.134145 * square)
    return raised * half, slope


def norm_pull(upstream, scaled, inverse, gain):
    inside = upstream * gain
    first = jnp.mean(inside, axis=-1, keepdims=True)
    second = jnp.mean(inside * scaled, axis=-1, keepdims=True)
    return inverse * (inside - first - scaled * second)


def column_sum(values):
    return jnp.sum(values, axis=0, keepdims=True)


LOADS = 8
ATTN_GAIN, ATTN_SHIFT, FFN_GAIN, FFN_SHIFT, DOWN_BIAS, WRITES, UP_BIAS = range(0, 28, 4)
CHUNK = 2048
EVENT = 0.2
LATENCY = 3.0
COSTS = [0.85] * 24 + [0.5] * 4 + [0.8, 1.0] + [1.7, 1.7, 1.2, 1.2, 0.4, 0.1] * 3
COSTS += [1.7, 1.7, 1.2, 1.2, 1.6, 0.1, 1.7, 1.7, 1.2, 1.2, 0.4, 0.1] * 2
COSTS += [1.7, 1.7, 1.2, 1.2, 1.6, 0.1] + [0.0, 1.0, 0.0, 1.6] + [1.0] * 4 + [0.3]
BEGINS = [4, 5, 10, 11, 16, 17, 22, 23, 28, 52, 64, 76, 81, 86]
TABLE = timetable(COSTS, BEGINS)


class Sizes:
    def __init__(self, dp, seq):
        self.dp, self.seq = dp, seq
        self.groups = seq // 8
        self.part = LANES // self.groups
        self.tiny = max(512, dp // 2 * seq * 16)
        self.rows = 13 * CHUNK + self.tiny
        self.landing = 9 * CHUNK

    def chunk(self, index):
        land = index - 9 * (index >= 9) if isinstance(index, int) else jnp.where(index >= 9, index - 9, index)
        return (index * CHUNK, CHUNK, land * CHUNK, index)

    def last(self):
        return (13 * CHUNK, self.tiny, 4 * CHUNK, 13)


def layer_kernel(sizes, refs):
    r = refs
    seq, groups, part = sizes.seq, sizes.groups, sizes.part
    dp_at, me = lax.axis_index(DP), lax.axis_index(SEQ)

    sources = (r.in_tokens, r.in_wc, r.in_wk, r.in_wv, r.in_wq, r.in_wo, r.in_down, r.in_pull)
    targets = (r.tokens, r.wc, r.wk, r.wv, r.wq, r.wo, r.down, r.pull)
    loads = [
        pltpu.make_async_copy(source, target, r.load_sem.at[at])
        for at, (source, target) in enumerate(zip(sources, targets))
    ]
    for copy in loads:
        copy.start()
    early_loads, load_wq, load_wo, load_down, load_pull = loads[:4], *loads[4:]
    up_loads = [
        pltpu.make_async_copy(
            r.in_up.at[:, pl.ds(512 * at, 512)], r.up.at[at], r.up_sem.at[at]
        )
        for at in range(4)
    ]
    for copy in up_loads:
        copy.start()

    barrier = pltpu.get_barrier_semaphore()
    count = 0
    for step in range(1, seq):
        pl.semaphore_signal(
            barrier, inc=1, device_id={SEQ: lax.rem(me + step, seq)}, device_id_type=MESH
        )
        count += 1
    core, line = lax.rem(dp_at, 2), dp_at // 2
    pl.semaphore_signal(
        barrier, inc=1, device_id={DP: line * 2 + 1 - core}, device_id_type=MESH
    )
    count += 1
    for step in range(1, sizes.dp // 2):
        other = lax.rem(line + step, sizes.dp // 2) * 2 + core
        pl.semaphore_signal(barrier, inc=1, device_id={DP: other}, device_id_type=MESH)
        count += 1

    tokens, normed, queries, keys, values = (
        r.tokens, r.normed, r.queries, r.keys, r.values
    )
    local, weights, sums, logits, chances, shares, mixed = (
        r.local, r.weights, r.sums, r.logits, r.chances, r.shares, r.mixed
    )
    notes, prior, hidden, held, small = r.notes, r.prior, r.hidden, r.held, r.small
    there = Exchange(seq, r.box0, r.box1, r.box_sem.at[0], r.box_sem.at[1])
    back = Exchange(seq, r.box2, r.box3, r.box_sem.at[2], r.box_sem.at[3])
    theres = [
        Exchange(seq, r.box4.at[at], r.box5.at[at], r.pair_sem.at[0, at], r.pair_sem.at[1, at])
        for at in range(4)
    ]
    backs = [
        Exchange(seq, r.box6.at[at], r.box7.at[at], r.pair_sem.at[2, at], r.pair_sem.at[3, at])
        for at in range(4)
    ]
    reduction = Reduction(
        sizes.dp, seq, held, r.landed, r.out_full, r.reduce_send, r.reduce_recv, r.keep_sem
    )

    def chunk_of(index):
        return sizes.last() if index == 13 else sizes.chunk(index)

    def events(moment):
        for index, number in TABLE[moment]:
            reduction.stage(chunk_of(index), number)

    def events_in(moments, *at):
        for indices, moment in moments.items():
            if TABLE[moment]:
                here = at[0] == indices[0]
                for index, value in zip(at[1:], indices[1:]):
                    here = here & (index == value)
                pl.when(here)(lambda moment=moment: events(moment))

    def put_small(at, values):
        for column in range(values.shape[1] // LANES):
            row = pl.ds(at + column, 1)
            small[row, :] = small[row, :] + values[:, column * LANES : (column + 1) * LANES]

    small[...] = jnp.zeros_like(small)

    for copy in early_loads:
        copy.wait()

    def project(step, unused):
        rows = pl.ds(pl.multiple_of(step * HALF, HALF), HALF)
        scaled, _ = normalized(tokens[rows, :].astype(F32))
        low = (scaled * r.attn_gain[...] + r.attn_shift[...]).astype(BF16)
        normed[rows, :] = low
        local[rows, :] = mm(low, r.wc[...])
        keys[rows, :] = mm(low, r.wk[...]).astype(BF16)
        values[rows, :] = mm(low, r.wv[...]).astype(BF16)
        return unused

    def summarize(combo, unused):
        row, col = block_of(combo)
        rows, cols = pl.ds(row, 512), pl.ds(col, LANES)
        control = local[rows, cols]
        block_max = jnp.floor(jnp.max(control, axis=0, keepdims=True))
        spread = jnp.exp(control - block_max)
        local[rows, cols] = spread
        pair_rows = jnp.concatenate([keys[rows, cols], values[rows, cols]], axis=1)
        memory = add_parts(mm_rows(pair_rows, parts_of(spread)))
        memory = jnp.concatenate([one_block(memory[:LANES]), one_block(memory[LANES:])], axis=0)
        total = column_sum(spread)
        flag = jnp.broadcast_to(r.starts[pl.ds(combo // 4, 1), :].astype(F32), (1, LANES))
        line = iota((8, LANES), 0)
        notes[combo] = jnp.where(line == 0, block_max, jnp.where(line == 1, total, flag))
        for group in range(groups):
            to = combo * groups + group
            there.sent[to, :part] = memory[group * part : (group + 1) * part]
            there.sent[to, part:] = notes[combo]
            there.send(to)
        return unused

    for stream in range(2):
        lax.fori_loop(2 * stream, 2 * stream + 2, project, 0)
        if stream == 0:
            pl.semaphore_wait(barrier, count)
        lax.fori_loop(4 * stream, 4 * stream + 4, summarize, 0)

    load_wq.wait()

    def project_query(step, unused):
        rows = pl.ds(pl.multiple_of(step * HALF, HALF), HALF)
        queries[rows, :] = mm(normed[rows, :], r.wq[...]).astype(BF16)
        return unused

    lax.fori_loop(0, 4, project_query, 0)

    def inside(combo, unused):
        row, col = block_of(combo)
        cols = pl.ds(col, LANES)
        spread = local[pl.ds(row, 512), cols]
        low = spread.astype(BF16)
        triangle = lower()
        ones = jnp.where(triangle, 1.0, 0.0).astype(BF16)
        first = add_parts(mm(ones, parts_of(spread[:HALF])))
        second = add_parts(mm(ones, parts_of(spread[HALF:]))) + first[HALF - 1 :]
        sums[pl.ds(row, HALF), cols] = first
        sums[pl.ds(row + HALF, HALF), cols] = second
        for at in range(2):
            rows = pl.ds(row + at * HALF, HALF)
            width = (at + 1) * HALF
            total = None
            for head in range(2):
                query = only_head(queries[rows, cols], head)
                found = []
                for other in range(at + 1):
                    score = mm_lanes(query, keys[pl.ds(row + other * HALF, HALF), cols])
                    if other == at:
                        score = jnp.where(triangle, score, 0.0)
                    found.append(score.astype(BF16))
                score = found[0] if at == 0 else jnp.concatenate(found, axis=1)
                term = mm(score, only_head(low[:width], head))
                total = term if total is None else total + term
            logits[rows, cols] = total
        return unused

    lax.fori_loop(0, 4, inside, 0)

    prior_max = jnp.full((1, LANES), -HUGE_VALUE, F32)
    raw_total = jnp.zeros((1, LANES), F32)
    raw_memory = jnp.zeros((part, LANES), F32)
    line = iota((8, LANES), 0)
    there.receive()
    for source in range(seq):
        back.sent[source, :part] = raw_memory
        back.sent[source, part:] = jnp.where(line == 0, prior_max, raw_total)
        back.send(source)
        if source < seq - 1:
            block_max = there.landed[source, part : part + 1]
            total = there.landed[source, part + 1 : part + 2]
            flag = there.landed[source, part + 2 : part + 3]
            ceiling = jnp.maximum(prior_max, block_max)
            old = (1.0 - flag) * jnp.exp(prior_max - ceiling)
            new = jnp.exp(block_max - ceiling)
            raw_total = old * raw_total + new * total
            raw_memory = old * raw_memory + new * there.landed[source, :part]
            prior_max = ceiling

    lax.fori_loop(4, 8, inside, 0)

    def returned(exchange, combo):
        pieces = [exchange.landed[combo * groups + group, :part] for group in range(groups)]
        memory = pieces[0] if groups == 1 else jnp.concatenate(pieces, axis=0)
        first = combo * groups
        return (
            memory,
            exchange.landed[first, part : part + 1],
            exchange.landed[first, part + 1 : part + 2],
        )

    def attend(combo, unused):
        row, col = block_of(combo)
        cols = pl.ds(col, LANES)
        memory, past_max, past_total = returned(back, combo)
        block_max = notes[combo, 0:1]
        flag = notes[combo, 2:3]
        ceiling = jnp.maximum(past_max, block_max)
        carried = (1.0 - flag) * jnp.exp(past_max - ceiling)
        factor = jnp.exp(block_max - ceiling)
        notes[combo, 1:2] = ceiling
        notes[combo, 3:4] = factor
        memory = (carried * memory).astype(BF16)
        prior[combo] = memory
        prior_keys = both_blocks(memory[:HEAD])
        prior_values = both_blocks(memory[HEAD:])
        triangle = lower()
        written = jnp.zeros((1, LANES), F32)
        for at in range(2):
            rows = pl.ds(row + at * HALF, HALF)
            weight = local[rows, cols] * factor
            weights[rows, cols] = weight.astype(BF16)
            inverse = 1.0 / (carried * past_total + factor * sums[rows, cols])
            sums[rows, cols] = inverse
            written = written + column_sum(weight * inverse)
            logit = (mm(queries[rows, cols], prior_keys) + factor * logits[rows, cols]) * inverse
            logits[rows, cols] = logit
            top = head_reduce(logit, jnp.max, -HUGE_VALUE)
            raised = jnp.exp(logit - top)
            chance = raised / head_reduce(raised, jnp.sum, 0.0)
            chances[rows, cols] = chance
            share = (chance * inverse).astype(BF16)
            shares[rows, cols] = share
            attended = mm_lanes(share, prior_values)
            for head in range(2):
                own = only_head(share, head)
                for other in range(at + 1):
                    these = pl.ds(row + other * HALF, HALF)
                    mixing = mm_lanes(own, weights[these, cols])
                    if other == at:
                        mixing = jnp.where(triangle, mixing, 0.0)
                    attended = attended + mm(
                        mixing.astype(BF16), only_head(values[these, cols], head)
                    )
            mixed[rows, cols] = attended.astype(BF16)
        place = pl.ds(WRITES + lax.rem(combo, 4), 1)
        small[place, :] = small[place, :] + written
        return unused

    back.receive()
    lax.fori_loop(0, 8, attend, 0)

    load_wo.wait()
    load_pull.wait()
    pull, branch, turned = r.pull, r.branch, r.turned

    def project_out(step, unused):
        rows = pl.ds(pl.multiple_of(step * HALF, HALF), HALF)
        wide = tokens[rows, :].astype(F32) + mm(mixed[rows, :], r.wo[...])
        hidden[rows, :] = wide
        scaled, _ = normalized(wide)
        low = (scaled * r.ffn_gain[...] + r.ffn_shift[...]).astype(BF16)
        branch[rows, :] = low
        turned[:, rows] = low.T
        put_small(DOWN_BIAS, column_sum(pull[rows, :].astype(F32)))
        return unused

    lax.fori_loop(0, 4, project_out, 0)

    load_down.wait()
    for copy in up_loads:
        copy.wait()
    up, down, active, pushed = r.up, r.down, r.active, r.pushed
    after = 9 * CHUNK

    def running(base, rows_at, values, first):
        for column in range(4):
            place = pl.ds(pl.multiple_of(base + column * 1024 + rows_at, 8), HALF)
            block = values[:, column * LANES : (column + 1) * LANES]
            held[place] = jnp.where(first, block, held[place] + block)

    def collected(base, rows_at):
        return jnp.concatenate(
            [
                held[pl.ds(pl.multiple_of(base + column * 1024 + rows_at, 8), HALF)]
                for column in range(4)
            ],
            axis=1,
        )

    def store_block(base, square, rows_at):
        for column in range(square.shape[1] // LANES):
            place = pl.ds(pl.multiple_of(base + column * 512 + rows_at, 8), square.shape[0])
            held[place] = square[:, column * LANES : (column + 1) * LANES]

    def feed_forward(part_at, unused):
        base = part_at * 2 * CHUNK

        def rows_of(step, unused):
            rows_at = pl.multiple_of(step * HALF, HALF)
            rows = pl.ds(rows_at, HALF)
            raised = mm(branch[rows, :], up[part_at]) + r.up_bias[:, pl.ds(pl.multiple_of(part_at * 512, 512), 512)]
            value, slope = gelu_parts(raised)
            low = value.astype(BF16)
            active[rows, :] = low
            along = pl.ds(pl.multiple_of(part_at * 512, 512), 512)
            grad = (mm_lanes(pull[rows, :], down[along, :]) * slope).astype(BF16)
            pushed[rows, :] = grad
            running(after, rows_at, mm(low, down[along, :]), part_at == 0)
            running(after + 4096, rows_at, mm_lanes(grad, up[part_at]), part_at == 0)
            total = column_sum(grad.astype(F32))
            for column in range(4):
                place = pl.ds(UP_BIAS + part_at * 4 + column, 1)
                small[place, :] = small[place, :] + total[:, column * LANES : (column + 1) * LANES]
            events_in(
                {(p, q): 6 * p + q for p in range(4) for q in range(4)}, part_at, step
            )
            return unused

        lax.fori_loop(0, 4, rows_of, 0)
        for block in range(2):
            wide = mm_rows(active[:, block * HALF : (block + 1) * HALF], pull[...])
            store_block(base, wide, block * HALF)
        events_in({(p,): 6 * p + 4 for p in range(4)}, part_at)
        for block in range(2):
            wide = mm(turned[block * HALF : (block + 1) * HALF, :], pushed[...])
            store_block(base + CHUNK, wide, block * HALF)
        events_in({(p,): 6 * p + 5 for p in range(4)}, part_at)
        return unused

    lax.fori_loop(0, 4, feed_forward, 0)

    def finish_rows(step, unused):
        rows_at = pl.multiple_of(step * HALF, HALF)
        rows = pl.ds(rows_at, HALF)
        wide = hidden[rows, :]
        r.result[rows, :] = (wide + collected(after, rows_at) + r.down_bias[...]).astype(BF16)
        scaled, inverse = normalized(wide)
        upstream = collected(after + 4096, rows_at)
        put_small(FFN_GAIN, column_sum(upstream * scaled))
        put_small(FFN_SHIFT, column_sum(upstream))
        grad = pull[rows, :].astype(F32) + norm_pull(upstream, scaled, inverse, r.ffn_gain[...])
        hidden[rows, :] = grad
        branch[rows, :] = grad.astype(BF16)
        events_in({(q,): 24 + q for q in range(4)}, step)
        return unused

    lax.fori_loop(0, 4, finish_rows, 0)
    result_copy = pltpu.make_async_copy(r.result, r.out_result, r.load_sem.at[LOADS])
    result_copy.start()
    for block in range(2):
        wide = mm_rows(mixed[:, block * HALF : (block + 1) * HALF], branch[...])
        store_block(8 * CHUNK, wide, block * HALF)
    events(28)

    def into_attention(step, unused):
        rows = pl.ds(pl.multiple_of(step * HALF, HALF), HALF)
        mixed[rows, :] = mm_lanes(branch[rows, :], r.wo[...]).astype(BF16)
        turned[:, rows] = normed[rows, :].T
        return unused

    lax.fori_loop(0, 4, into_attention, 0)
    events(29)

    late, outgoing = 256 // seq, r.box4
    pulled, near_grad, total_grad, query_low = mixed, r.near_grad, r.total_grad, active

    def backward(combo, step):
        row, col = block_of(combo)
        cols = pl.ds(col, LANES)
        memory = prior[combo]
        prior_keys = both_blocks(memory[:HEAD])
        prior_values = both_blocks(memory[HEAD:])
        triangle = lower()
        early = upper()
        all_rows = [pl.ds(row, HALF), pl.ds(row + HALF, HALF)]
        for at in range(2):
            rows = all_rows[at]
            pulls = pulled[rows, cols]
            share_grad = mm(pulls, prior_values)
            for head in range(2):
                own = only_head(pulls, head)
                for other in range(at + 1):
                    these = all_rows[other]
                    grad = mm_lanes(own, values[these, cols])
                    if other == at:
                        grad = jnp.where(triangle, grad, 0.0)
                    share_grad = share_grad + mm(
                        grad.astype(BF16), only_head(weights[these, cols], head)
                    )
            inverse, chance = sums[rows, cols], chances[rows, cols]
            chance_grad = share_grad * inverse
            middle = head_reduce(chance * chance_grad, jnp.sum, 0.0)
            logit_grad = chance * (chance_grad - middle)
            number_grad = logit_grad * inverse
            total_grad[pl.ds(at * HALF, HALF), :] = -(
                chance_grad * chance * inverse + number_grad * logits[rows, cols]
            )
            low = number_grad.astype(BF16)
            near_grad[pl.ds(at * HALF, HALF), :] = low
            query_grad = mm_lanes(low, prior_keys)
            for head in range(2):
                own = only_head(low, head)
                for other in range(at + 1):
                    these = all_rows[other]
                    grad = mm_lanes(own, weights[these, cols])
                    if other == at:
                        grad = jnp.where(triangle, grad, 0.0)
                    query_grad = query_grad + mm(
                        grad.astype(BF16), only_head(keys[these, cols], head)
                    )
            query_low[rows, cols] = query_grad.astype(BF16)
            events_in({(q,): 30 + 6 * q + at for q in range(8)}, step)
        ones = jnp.where(early, 1.0, 0.0).astype(BF16)
        late_sum = add_parts(mm(ones, parts_of(total_grad[HALF:, :])))
        early_sum = add_parts(mm(ones, parts_of(total_grad[:HALF, :]))) + late_sum[:1]
        prior_total_grad = early_sum[:1]
        for at in range(2):
            rows = all_rows[at]
            weight_grad = early_sum if at == 0 else late_sum
            key_grad = value_grad = None
            for head in range(2):
                own_value = only_head(values[rows, cols], head)
                own_weight = only_head(weights[rows, cols], head)
                own_key = only_head(keys[rows, cols], head)
                for other in range(at, 2):
                    these = all_rows[other]
                    near = near_grad[pl.ds(other * HALF, HALF), :]

                    def masked(square, other=other):
                        if other == at:
                            square = jnp.where(early, square, 0.0)
                        return square.astype(BF16)

                    pulls = pulled[these, cols]
                    share = shares[these, cols]
                    query = queries[these, cols]
                    weight_grad = weight_grad + mm(
                        masked(mm_lanes(own_value, pulls)), only_head(share, head)
                    )
                    weight_grad = weight_grad + mm(
                        masked(mm_lanes(own_key, query)), only_head(near, head)
                    )
                    term = mm(masked(mm_lanes(own_weight, share)), only_head(pulls, head))
                    value_grad = term if value_grad is None else value_grad + term
                    term = mm(masked(mm_lanes(own_weight, near)), only_head(query, head))
                    key_grad = term if key_grad is None else key_grad + term
            sums[rows, cols] = weight_grad * (local[rows, cols] * notes[combo, 3:4])
            logits[rows, cols] = key_grad
            chances[rows, cols] = value_grad
            if at == 0:
                events_in({(q,): 32 + 6 * q for q in range(8)}, step)
        whole = pl.ds(row, 512)
        key_memory = mm_rows(queries[whole, cols], near_grad[...])
        value_memory = mm_rows(pulled[whole, cols], shares[whole, cols])
        keep = 1.0 - notes[combo, 2:3]
        memory = keep * jnp.concatenate([one_block(key_memory), one_block(value_memory)], axis=0)
        line = iota((8, LANES), 0)
        extra = jnp.where(
            line == 0,
            notes[combo, 1:2],
            jnp.where(line == 1, keep * prior_total_grad, notes[combo, 2:3]),
        )
        stream = combo // 4
        for group in range(seq // 2):
            to = stream * (seq // 2) + group
            outgoing[step // 2, to, :late] = memory[group * late : (group + 1) * late]
            outgoing[step // 2, to, late:] = extra

    def handle(pair):
        arrived, answers = theres[pair], backs[pair]
        arrived.receive()
        floor = jnp.full((1, LANES), HUGE_VALUE, F32)
        total = jnp.zeros((1, LANES), F32)
        memory = jnp.zeros((late, LANES), F32)
        line = iota((8, LANES), 0)
        for source in reversed(range(seq)):
            answers.sent[source, :late] = memory
            answers.sent[source, late:] = jnp.where(line == 0, floor, total)
            if source > 0:
                ceiling = arrived.landed[source, late : late + 1]
                flag = arrived.landed[source, late + 2 : late + 3]
                lowest = jnp.minimum(floor, ceiling)
                near = jnp.exp(lowest - ceiling)
                far = (1.0 - flag) * jnp.exp(lowest - floor)
                total = near * arrived.landed[source, late + 1 : late + 2] + far * total
                memory = near * arrived.landed[source, :late] + far * memory
                floor = lowest
        answers.send_all()

    def for_pair(pair, act):
        for at in range(4):
            pl.when(pair == at)(lambda at=at: act(at))

    def finalize(pair):
        if isinstance(pair, int):
            backs[pair].receive()
        else:
            for_pair(pair, lambda at: backs[at].receive())

        def one(stream, unused):
            combo = stream * 4 + pair
            row, col = block_of(combo)
            cols = pl.ds(col, LANES)
            first = stream * (seq // 2)
            memory = jnp.concatenate(
                [r.box7[pair, first + group, :late] for group in range(seq // 2)], axis=0
            )
            floor = r.box7[pair, first, late : late + 1]
            total = r.box7[pair, first, late + 1 : late + 2]
            reach = jnp.exp(notes[combo, 0:1] - floor)
            total = reach * total
            memory = (reach * memory).astype(BF16)
            key_memory, value_memory = both_blocks(memory[:HEAD]), both_blocks(memory[HEAD:])
            for at in range(2):
                rows = pl.ds(row + at * HALF, HALF)
                spread = local[rows, cols]
                low = spread.astype(BF16)
                inner = mm(keys[rows, cols], key_memory) + mm(values[rows, cols], value_memory)
                weights[rows, cols] = (sums[rows, cols] + spread * (inner + total)).astype(BF16)
                key_grad = logits[rows, cols] + mm_lanes(low, key_memory)
                value_grad = chances[rows, cols] + mm_lanes(low, value_memory)
                keys[rows, cols] = key_grad.astype(BF16)
                values[rows, cols] = value_grad.astype(BF16)
            return unused

        lax.fori_loop(0, 2, one, 0)
        cols = pl.ds(pl.multiple_of(pair * LANES, LANES), LANES)
        base = (9 + pair) * CHUNK
        for at, (left, right) in enumerate(((query_low, keys), (values, weights))):
            both = jnp.concatenate([left[:, cols], right[:, cols]], axis=1)
            for block in range(2):
                wide = mm(turned[block * HALF : (block + 1) * HALF, :], both)
                store_block(base + at * 1024, wide, block * HALF)

    def iteration(step, unused):
        backward((lax.rem(step, 2)) * 4 + step // 2, step)
        events_in({(q,): 33 + 6 * q for q in range(8)}, step)

        @pl.when(lax.rem(step, 2) == 1)
        def _():
            for_pair(step // 2, lambda at: theres[at].send_all())

        @pl.when((step >= 2) & (lax.rem(step, 2) == 0))
        def _():
            for_pair(step // 2 - 1, handle)

        @pl.when((step >= 3) & (lax.rem(step, 2) == 1))
        def _():
            finalize((step - 3) // 2)

        events_in({(q,): 34 + 6 * q for q in range(8)}, step)
        events_in({(q,): 35 + 6 * q for q in range(8)}, step)
        return unused

    lax.fori_loop(0, 8, iteration, 0)
    events(78)

    handle(3)
    events(79)
    events(80)
    finalize(3)
    events(81)

    def input_rows(step, unused):
        rows = pl.ds(pl.multiple_of(step * HALF, HALF), HALF)
        upstream = mm_lanes(query_low[rows, :], r.wq[...])
        upstream = upstream + mm_lanes(keys[rows, :], r.wk[...])
        upstream = upstream + mm_lanes(values[rows, :], r.wv[...])
        upstream = upstream + mm_lanes(weights[rows, :], r.wc[...])
        scaled, inverse = normalized(tokens[rows, :].astype(F32))
        put_small(ATTN_GAIN, column_sum(upstream * scaled))
        put_small(ATTN_SHIFT, column_sum(upstream))
        hidden[rows, :] = hidden[rows, :] + norm_pull(
            upstream, scaled, inverse, r.attn_gain[...]
        )
        events_in({(q,): 82 + q for q in range(4)}, step)
        return unused

    lax.fori_loop(0, 4, input_rows, 0)
    grad_copy = pltpu.make_async_copy(
        hidden, r.out_input_grad, r.load_sem.at[LOADS + 1]
    )
    grad_copy.start()
    last = sizes.last()
    held[pl.ds(last[0], last[1])] = jnp.zeros((last[1], LANES), F32)
    held[pl.ds(last[0], small.shape[0])] = small[...]
    events(86)
    events(87)
    for copy in (result_copy, grad_copy):
        copy.wait()
    for exchange in (there, back, *theres, *backs):
        exchange.finish()
    for index in range(14):
        reduction.finish(chunk_of(index))


def deliver_kernel(full, result, input_grad, slot_means, count, *outs):
    (
        out_result, out_input_grad, attn_gain, attn_shift, wq, wk, wv, wc, wo,
        ffn_gain, ffn_shift, up, up_bias, down, down_bias, means, held, held_result, held_grad, in_sem, out_sem,
    ) = outs
    loads = [
        pltpu.make_async_copy(full.at[rows], held.at[rows], in_sem.at[at])
        for at, rows in enumerate(
            [pl.ds(13 * CHUNK, 40)] + [pl.ds(at * CHUNK, CHUNK) for at in range(13)]
        )
    ]
    loads.append(pltpu.make_async_copy(result, held_result, in_sem.at[14]))
    loads.append(pltpu.make_async_copy(input_grad, held_grad, in_sem.at[15]))
    for copy in loads:
        copy.start()
    stores = []

    def store(source, target):
        copy = pltpu.make_async_copy(source, target, out_sem.at[len(stores)])
        copy.start()
        stores.append(copy)

    for index in range(13):
        loads[1 + index].wait()
        for column in range(4):
            lanes = pl.ds(column * LANES, LANES)
            source = held.at[pl.ds(index * CHUNK + column * 512, 512)]
            if index == 8:
                store(source, wo.at[:, lanes])
            elif index > 8:
                store(source, (wq, wk, wv, wc)[column].at[:, pl.ds((index - 9) * LANES, LANES)])
            elif index % 2:
                store(source, up.at[:, pl.ds(index // 2 * 512 + column * LANES, LANES)])
            else:
                store(source, down.at[pl.ds(index // 2 * 512, 512), lanes])
    loads[14].wait()
    store(held_result, out_result)
    loads[15].wait()
    store(held_grad, out_input_grad)
    loads[0].wait()
    small = held.at[pl.ds(13 * CHUNK, 40)]
    for at, target in (
        (ATTN_GAIN, attn_gain),
        (ATTN_SHIFT, attn_shift),
        (FFN_GAIN, ffn_gain),
        (FFN_SHIFT, ffn_shift),
        (DOWN_BIAS, down_bias),
        (UP_BIAS, up_bias),
    ):
        for column in range(target.shape[1] // LANES):
            row = pl.ds(at + column, 1)
            target[:, column * LANES : (column + 1) * LANES] = small[row, :]
    for pair in range(4):
        row = small[pl.ds(WRITES + pair, 1), :]
        for head in range(2):
            line = pl.ds(2 * pair + head, 1)
            written = row[:, head * SLOTS : (head + 1) * SLOTS]
            means[line, :] = 0.9 * slot_means[line, :] + 0.1 * written / count
    for copy in stores:
        copy.wait()


def deliver_call(count, full, result, input_grad, slot_means):
    square = jax.ShapeDtypeStruct((512, 512), F32)
    vector = jax.ShapeDtypeStruct((1, 512), F32)
    long = jax.ShapeDtypeStruct((1, 2048), F32)
    shapes = [result, input_grad, vector, vector, square, square, square, square, square]
    shapes += [vector, vector, jax.ShapeDtypeStruct((512, 2048), F32), long]
    shapes += [jax.ShapeDtypeStruct((2048, 512), F32), vector, slot_means]
    anywhere = pl.BlockSpec(memory_space=pl.ANY)
    near = pl.BlockSpec(memory_space=pltpu.VMEM)

    def kernel(full, result, input_grad, slot_means, *outs):
        deliver_kernel(full, result, input_grad, slot_means, count, *outs)

    return pl.pallas_call(
        kernel,
        out_shape=[jax.ShapeDtypeStruct(shape.shape, shape.dtype) for shape in shapes],
        in_specs=[anywhere, anywhere, anywhere, near],
        out_specs=[near if shape is vector or shape is long or shape is slot_means else anywhere for shape in shapes],
        scratch_shapes=[
            pltpu.VMEM((13 * CHUNK + 40, LANES), F32),
            pltpu.VMEM(result.shape, BF16),
            pltpu.VMEM(input_grad.shape, F32),
            pltpu.SemaphoreType.DMA((16,)),
            pltpu.SemaphoreType.DMA((54,)),
        ],
        compiler_params=pltpu.CompilerParams(vmem_limit_bytes=60 * 2**20),
        name="deliver",
    )(full, result, input_grad, slot_means)


def layer_call(sizes, **arrays):
    rows, width, hidden = 1024, 512, 2048
    outputs = dict(
        out_result=jax.ShapeDtypeStruct((rows, width), BF16),
        out_input_grad=jax.ShapeDtypeStruct((rows, width), F32),
        out_full=jax.ShapeDtypeStruct((sizes.rows, LANES), F32),
    )
    low, wide = pltpu.VMEM((rows, width), BF16), pltpu.VMEM((rows, width), F32)
    weight = pltpu.VMEM((width, width), BF16)
    box = pltpu.VMEM((sizes.seq, sizes.part + 8, LANES), F32)
    pair_box = pltpu.VMEM((4, sizes.seq, 256 // sizes.seq + 8, LANES), F32)
    semaphores = pltpu.SemaphoreType.DMA
    scratch = dict(
        tokens=low, wc=weight, wk=weight, wv=weight, wq=weight, wo=weight,
        up=pltpu.VMEM((4, width, 512), BF16), down=pltpu.VMEM((hidden, width), BF16), pull=low,
        normed=low, queries=low, keys=low, values=low, local=wide, weights=low,
        sums=wide, logits=wide, chances=wide, shares=low, mixed=low, hidden=wide,
        branch=low, turned=pltpu.VMEM((width, rows), BF16), active=low, pushed=low, result=low,
        near_grad=pltpu.VMEM((512, LANES), BF16), total_grad=pltpu.VMEM((512, LANES), F32),
        prior=pltpu.VMEM((8, LANES, LANES), BF16), notes=pltpu.VMEM((8, 8, LANES), F32),
        small=pltpu.VMEM((40, LANES), F32),
        held=pltpu.VMEM((sizes.rows, LANES), F32), landed=pltpu.VMEM((sizes.landing, LANES), F32),
        box0=box, box1=box, box2=box, box3=box, box4=pair_box, box5=pair_box, box6=pair_box, box7=pair_box,
        box_sem=semaphores((4,)), pair_sem=semaphores((4, 4)), load_sem=semaphores((LOADS + 2,)), up_sem=semaphores((4,)),
        keep_sem=semaphores((14,)), reduce_send=semaphores((14,)),
        reduce_recv=semaphores((14, 8)),
    )
    names = list(arrays) + list(outputs) + list(scratch)

    def kernel(*refs):
        layer_kernel(sizes, types.SimpleNamespace(**dict(zip(names, refs, strict=True))))

    anywhere = pl.BlockSpec(memory_space=pl.ANY)
    near = pl.BlockSpec(memory_space=pltpu.VMEM)
    found = pl.pallas_call(
        kernel,
        out_shape=list(outputs.values()),
        in_specs=[anywhere if name.startswith("in_") else near for name in arrays],
        out_specs=[anywhere] * len(outputs),
        scratch_shapes=list(scratch.values()),
        compiler_params=pltpu.CompilerParams(
            collective_id=1, has_side_effects=True, vmem_limit_bytes=63 * 2**20
        ),
        name="layer",
    )(*arrays.values())
    return types.SimpleNamespace(**dict(zip(outputs, found, strict=True)))


def solution(mesh):
    sizes = Sizes(mesh.shape[DP], mesh.shape[SEQ])

    def shards(
        inputs, starts, attn_gain, attn_shift, query_weight, key_weight, value_weight, control_weight, output_weight,
        ffn_gain, ffn_shift, up_weight, up_bias, down_weight, down_bias, slot_means, cotangent,
    ):
        streams, length, width = inputs.shape
        rows = streams * length
        found = layer_call(
            sizes,
            in_tokens=inputs.reshape(rows, width),
            in_wc=control_weight,
            in_wk=key_weight,
            in_wv=value_weight,
            in_wq=query_weight,
            in_wo=output_weight,
            in_up=up_weight,
            in_down=down_weight,
            in_pull=cotangent.reshape(rows, width),
            starts=starts,
            attn_gain=attn_gain[None],
            attn_shift=attn_shift[None],
            ffn_gain=ffn_gain[None],
            ffn_shift=ffn_shift[None],
            up_bias=up_bias[None],
            down_bias=down_bias[None],
        )
        outs = list(deliver_call(
            streams * sizes.dp, found.out_full, found.out_result, found.out_input_grad, slot_means)
        )
        outs[0], outs[1] = outs[0].reshape(inputs.shape), outs[1].reshape(inputs.shape)
        for at in (2, 3, 9, 10, 12, 14):
            outs[at] = outs[at].reshape(-1)
        return tuple(outs)

    split = P(DP, SEQ, None)
    return jax.shard_map(
        shards,
        mesh=mesh,
        in_specs=(split, P(DP, SEQ)) + (P(),) * 14 + (split,),
        out_specs=(split, split) + (P(),) * 14,
        check_vma=False,
    )
```

```python
import functools
import types

import jax
import jax.numpy as jnp
from jax import lax
from jax.experimental import pallas as pl
from jax.experimental.pallas import tpu as pltpu
from jax.sharding import PartitionSpec as P

HEADS = 8
HEAD = 64
SLOTS = 64
EPSILON = 1e-05
HUGE_VALUE = 1e30
MESH = pl.DeviceIdType.MESH
F32 = jnp.float32
BF16 = jnp.bfloat16
LANES = 128
HALF = 256
SHARE = 8
DP, SEQ = "dp", "seq"
CORE, LINE, NEAR, LOW, HIGH = range(5)
LEVELS = 5


def mm(left, right):
    return lax.dot_general(left, right, (((1,), (0,)), ((), ())), preferred_element_type=F32)


def mm_lanes(left, right):
    return lax.dot_general(left, right, (((1,), (1,)), ((), ())), preferred_element_type=F32)


def mm_rows(left, right):
    return lax.dot_general(left, right, (((0,), (0,)), ((), ())), preferred_element_type=F32)


def iota(shape, axis):
    return lax.broadcasted_iota(jnp.int32, shape, axis)


def first_head(shape):
    return iota(shape, len(shape) - 1) < HEAD


def only_head(values, head):
    keep = first_head(values.shape) if head == 0 else jnp.logical_not(first_head(values.shape))
    return jnp.where(keep, values, jnp.zeros_like(values))


def both_blocks(rows):
    doubled = jnp.concatenate([rows, rows], axis=0)
    inside = (iota(doubled.shape, 0) < HEAD) == first_head(doubled.shape)
    return jnp.where(inside, doubled, jnp.zeros_like(doubled))


def one_block(square):
    return jnp.where(first_head((HEAD, LANES)), square[:HEAD], square[HEAD:])


def stacked(values):
    return jnp.concatenate([only_head(values, 0), only_head(values, 1)], axis=0)


def masked(square, earlier):
    row = iota(square.shape, 0)
    column = jnp.bitwise_and(iota(square.shape, 1), LANES - 1)
    keep = row >= column if earlier else row <= column
    return jnp.where(keep, square, 0.0).astype(BF16)


def own_blocks(square):
    inside = (iota(square.shape, 0) < HEAD) == first_head(square.shape)
    return jnp.where(inside, square, 0.0)


def triangle(earlier):
    row, column = iota((LANES, LANES), 0), iota((LANES, LANES), 1)
    return jnp.where(row >= column if earlier else row <= column, 1.0, 0.0).astype(BF16)


def head_reduce(values, operation, empty):
    here = first_head(values.shape)
    one = operation(jnp.where(here, values, empty), axis=1, keepdims=True)
    two = operation(jnp.where(here, empty, values), axis=1, keepdims=True)
    return jnp.where(here, one, two)


def parts_of(values):
    high = values.astype(BF16)
    return jnp.concatenate([high, (values - high.astype(F32)).astype(BF16)], axis=1)


def add_parts(product):
    return product[:, :LANES] + product[:, LANES:]


def normalized(values):
    centre = values - jnp.mean(values, axis=-1, keepdims=True)
    inverse = lax.rsqrt(jnp.mean(centre * centre, axis=-1, keepdims=True) + EPSILON)
    return centre * inverse, inverse


class Exchange:
    def __init__(self, size, sent, landed, send_sem, recv_sem):
        self.size, self.sent, self.landed = size, sent, landed
        self.send_sem, self.recv_sem = send_sem, recv_sem
        self.me = lax.axis_index(SEQ)

    def copy(self, source, target, to):
        return pltpu.make_async_remote_copy(
            src_ref=source,
            dst_ref=target,
            send_sem=self.send_sem,
            recv_sem=self.recv_sem,
            device_id={SEQ: to},
            device_id_type=MESH,
        )

    def send(self, to):
        @pl.when(to != self.me)
        def _():
            self.copy(self.sent.at[to], self.landed.at[self.me], to).start()

        @pl.when(to == self.me)
        def _():
            self.landed[self.me] = self.sent[self.me]

    def send_all(self):
        self.landed[self.me] = self.sent[self.me]
        for step in range(1, self.size):
            to = lax.rem(self.me + step, self.size)
            self.copy(self.sent.at[to], self.landed.at[self.me], to).start()

    def receive(self):
        others = self.landed.at[pl.ds(0, self.size - 1)]
        self.copy(others, others, lax.rem(self.me + 1, self.size)).wait_recv()

    def finish(self):
        others = self.sent.at[pl.ds(0, self.size - 1)]
        self.copy(others, others, lax.rem(self.me + 1, self.size)).wait_send()


class Reduction:
    def __init__(self, dp, seq, held, landed, full, send_sem, recv_sem, keep_sem):
        self.held, self.landed, self.full = held, landed, full
        self.send_sem, self.recv_sem, self.keep_sem = send_sem, recv_sem, keep_sem
        dp_at, seq_at = lax.axis_index(DP), lax.axis_index(SEQ)
        slow, fast = 4, seq // 4
        core, line = lax.rem(dp_at, 2), dp_at // 2
        near, far = lax.rem(seq_at, fast), seq_at // fast
        self.groups = {
            CORE: (2, core, lambda m: {DP: line * 2 + m}),
            LINE: (dp // 2, line, lambda m: {DP: m * 2 + core}),
            NEAR: (fast, near, lambda m: {SEQ: far * fast + m}),
            LOW: (2, lax.rem(far, 2), lambda m: {SEQ: (far // 2 * 2 + m) * fast + near}),
            HIGH: (2, far // 2, lambda m: {SEQ: (m * 2 + lax.rem(far, 2)) * fast + near}),
        }
        self.ways = dp // 2 * fast * slow

    def orders(self, rows, index):
        half = rows // 2
        least = self.ways * 8
        if half >= 2 * least:
            first = max(half // least * SHARE // 16, 1) * least
            return [(0, first, (LINE, NEAR, LOW, HIGH)), (first, half - first, (NEAR, LINE, LOW, HIGH))]
        return [(0, half, (LINE, NEAR, LOW, HIGH))]

    def steps(self, chunk, level):
        base, rows, land, index = chunk
        core = self.groups[CORE][1]
        if level == 0:
            return [(base, rows // 2, CORE, land)], rows // 2
        orders = self.orders(rows, index)
        place = land + rows // 2
        sizes = [size for _, size, _ in orders]
        starts = [base + core * (rows // 2) + offset for offset, _, _ in orders]
        for depth in range(level):
            found = []
            first = place
            for at, (_, _, axes) in enumerate(orders):
                name = axes[depth]
                count, mine, _ = self.groups[name]
                sizes[at] //= count
                found.append((starts[at], sizes[at], name, place))
                starts[at] = starts[at] + mine * sizes[at]
                place = place + sizes[at] * (count - 1)
        return found, sum(size * (self.groups[name][0] - 1) for _, size, name, _ in found)

    def rows_sent(self, chunk):
        return 2 * sum(self.steps(chunk, level)[1] for level in range(LEVELS))

    def copy(self, chunk, slot, source, target, device):
        return pltpu.make_async_remote_copy(
            src_ref=source,
            dst_ref=target,
            send_sem=self.send_sem.at[chunk[3]],
            recv_sem=self.recv_sem.at[chunk[3], slot],
            device_id=device,
            device_id_type=MESH,
        )

    def start(self, chunk, level, gather):
        for start, size, name, land in self.steps(chunk, level)[0]:
            count, at, device = self.groups[name]
            for k in range(1, count):
                to = lax.rem(at + k, count)
                if gather:
                    rows = pl.ds(pl.multiple_of(start + at * size, 8), size)
                    source = (self.held if level == LEVELS - 1 else self.full).at[rows]
                    target = self.full.at[rows]
                else:
                    source = self.held.at[pl.ds(pl.multiple_of(start + to * size, 8), size)]
                    target = self.landed.at[pl.ds(pl.multiple_of(land + (k - 1) * size, 8), size)]
                self.copy(chunk, level + LEVELS * gather, source, target, device(to)).start()
            if gather and level == LEVELS - 1:
                rows = pl.ds(pl.multiple_of(start + at * size, 8), size)
                pltpu.make_async_copy(
                    self.held.at[rows], self.full.at[rows], self.keep_sem.at[chunk[3]]
                ).start()

    def wait(self, chunk, level, gather):
        steps, rows = self.steps(chunk, level)
        at = pl.ds(chunk[0], rows) if gather else pl.ds(steps[0][3], rows)
        ref = (self.full if gather else self.landed).at[at]
        self.copy(chunk, level + LEVELS * gather, ref, ref, self.groups[CORE][2](0)).wait_recv()
        if gather and level == LEVELS - 1:
            at = pl.ds(chunk[0], sum(size for _, size, _, _ in steps))
            pltpu.make_async_copy(
                self.held.at[at], self.full.at[at], self.keep_sem.at[chunk[3]]
            ).wait()

    def finish(self, chunk):
        ref = self.held.at[pl.ds(0, self.rows_sent(chunk))]
        self.copy(chunk, 0, ref, ref, self.groups[CORE][2](0)).wait_send()

    def add(self, chunk, level):
        for start, size, name, land in self.steps(chunk, level)[0]:
            count, at, _ = self.groups[name]
            block = min(size, 512)

            def one(step, unused, start=start, size=size, land=land, at=at, count=count, block=block):
                rows = pl.ds(pl.multiple_of(start + at * size + step * block, 8), block)
                total = self.held[rows]
                for k in range(1, count):
                    found = pl.ds(pl.multiple_of(land + (k - 1) * size + step * block, 8), block)
                    total = total + self.landed[found]
                self.held[rows] = total
                return unused

            if size == block:
                one(0, 0)
            else:
                lax.fori_loop(0, size // block, one, 0)

    def stage(self, chunk, number):
        if number:
            summing = number <= LEVELS
            level = number - 1 if summing else 2 * LEVELS - number
            self.wait(chunk, level, not summing)
            if summing:
                self.add(chunk, level)
        if number < LEVELS:
            self.start(chunk, number, False)
        elif number < 2 * LEVELS:
            self.start(chunk, 2 * LEVELS - 1 - number, True)


def timetable(costs, begins):
    line = [(0, 0.9), (1, 2.9), (1, 1.5), (2, 1.5), (2, 1.5)]
    now, free, ready, following = 0.0, [0.0] * 3, {}, {}
    table = [[] for _ in costs] + [[]]

    def take(chunk, number, place):
        nonlocal now
        now += EVENT
        place.append((chunk, number))
        following[chunk] = number + 1
        if number == 2 * LEVELS:
            del following[chunk], ready[chunk]
            return
        link, cost = line[min(number, 2 * LEVELS - 1 - number)]
        free[link] = max(now, free[link]) + (cost if chunk < 13 else cost / 4)
        ready[chunk] = free[link] + LATENCY

    for moment, cost in enumerate(costs):
        now += cost
        for chunk, begin in enumerate(begins):
            if begin == moment:
                take(chunk, 0, table[moment])
        while True:
            able = [chunk for chunk in following if ready[chunk] <= now]
            if not able:
                break
            take(min(able), following[min(able)], table[moment])
    while following:
        chunk = min(following, key=lambda at: (ready[at], at))
        now = max(now, ready[chunk])
        take(chunk, following[chunk], table[-1])
    return table


def block_of(combo):
    stream, pair = combo // 4, lax.rem(combo, 4)
    return (
        pl.multiple_of(stream * 512, 512),
        pl.multiple_of(pair * LANES, LANES),
    )


def gelu_parts(raised):
    root = 0.7978845608028654
    square = raised * raised
    bent = jnp.tanh(root * raised * (1.0 + 0.044715 * square))
    half = 0.5 * (1.0 + bent)
    slope = half + (0.5 * root) * raised * (1.0 - bent * bent) * (1.0 + 0.134145 * square)
    return raised * half, slope


def norm_pull(upstream, scaled, inverse, gain):
    inside = upstream * gain
    first = jnp.mean(inside, axis=-1, keepdims=True)
    second = jnp.mean(inside * scaled, axis=-1, keepdims=True)
    return inverse * (inside - first - scaled * second)


def quarters(values):
    return [values[at * LANES : (at + 1) * LANES] for at in range(4)]


def running(blocks):
    sums = [blocks[0]]
    for block in blocks[1:]:
        sums.append(sums[-1] + block)
    return sums


def column_sum(values):
    return jnp.sum(values, axis=0, keepdims=True)


LOADS = 8
ATTN_GAIN, ATTN_SHIFT, FFN_GAIN, FFN_SHIFT, DOWN_BIAS, WRITES, UP_BIAS = range(0, 28, 4)
CHUNK = 2048
EVENT = 0.35
LATENCY = 3.0
COSTS = [0.85] * 24 + [0.5] * 4 + [0.8, 1.0] + [0.9, 0.9, 1.1, 0.7, 0.3, 0.0] * 8
COSTS += [0.9, 0.8, 0.8, 0.8, 1.0, 1.8, 0.9, 0.9] + [1.0] * 4 + [0.3]
BEGINS = [4, 5, 10, 11, 16, 17, 22, 23, 28, 78, 83, 84, 85, 90]
TABLE = timetable(COSTS, BEGINS)


class Sizes:
    def __init__(self, dp, seq):
        self.dp, self.seq = dp, seq
        self.tiny = max(512, dp // 2 * seq * 16)
        self.rows = 13 * CHUNK + self.tiny
        self.landing = 9 * CHUNK

    def chunk(self, index):
        land = index - 9 * (index >= 9) if isinstance(index, int) else jnp.where(index >= 9, index - 9, index)
        return (index * CHUNK, CHUNK, land * CHUNK, index)

    def last(self):
        return (13 * CHUNK, self.tiny, 4 * CHUNK, 13)


def layer_kernel(sizes, refs):
    r = refs
    seq = sizes.seq
    dp_at, me = lax.axis_index(DP), lax.axis_index(SEQ)

    sources = (r.in_tokens, r.in_wc, r.in_wk, r.in_wv, r.in_wq, r.in_wo, r.in_down, r.in_pull)
    targets = (r.tokens, r.wc, r.wk, r.wv, r.wq, r.wo, r.down, r.pull)
    loads = [
        pltpu.make_async_copy(source, target, r.load_sem.at[at])
        for at, (source, target) in enumerate(zip(sources, targets))
    ]
    for copy in loads:
        copy.start()
    early_loads, load_wq, load_wo, load_down, load_pull = loads[:4], *loads[4:]
    up_loads = [
        pltpu.make_async_copy(
            r.in_up.at[:, pl.ds(512 * at, 512)], r.up.at[at], r.up_sem.at[at]
        )
        for at in range(4)
    ]
    for copy in up_loads:
        copy.start()

    barrier = pltpu.get_barrier_semaphore()
    count = 0
    for step in range(1, seq):
        pl.semaphore_signal(
            barrier, inc=1, device_id={SEQ: lax.rem(me + step, seq)}, device_id_type=MESH
        )
        count += 1
    core, line = lax.rem(dp_at, 2), dp_at // 2
    pl.semaphore_signal(
        barrier, inc=1, device_id={DP: line * 2 + 1 - core}, device_id_type=MESH
    )
    count += 1
    for step in range(1, sizes.dp // 2):
        other = lax.rem(line + step, sizes.dp // 2) * 2 + core
        pl.semaphore_signal(barrier, inc=1, device_id={DP: other}, device_id_type=MESH)
        count += 1

    tokens, normed, queries, keys, values = (
        r.tokens, r.normed, r.queries, r.keys, r.values
    )
    local, weights, sums, logits, chances, shares, mixed = (
        r.local, r.weights, r.sums, r.logits, r.chances, r.shares, r.mixed
    )
    notes, prior, hidden, held, small = r.notes, r.prior, r.hidden, r.held, r.small
    early = 512 // seq
    there = [
        Exchange(seq, r.box0.at[at], r.box1.at[at], r.box_sem.at[0, at], r.box_sem.at[1, at])
        for at in range(2)
    ]
    back = [
        Exchange(seq, r.box2.at[at], r.box3.at[at], r.box_sem.at[2, at], r.box_sem.at[3, at])
        for at in range(2)
    ]
    theres = [
        Exchange(seq, r.box4.at[at], r.box5.at[at], r.pair_sem.at[0, at], r.pair_sem.at[1, at])
        for at in range(4)
    ]
    backs = [
        Exchange(seq, r.box6.at[at], r.box7.at[at], r.pair_sem.at[2, at], r.pair_sem.at[3, at])
        for at in range(4)
    ]
    reduction = Reduction(
        sizes.dp, seq, held, r.landed, r.out_full, r.reduce_send, r.reduce_recv, r.keep_sem
    )

    def chunk_of(index):
        return sizes.last() if index == 13 else sizes.chunk(index)

    def events(moment):
        for index, number in TABLE[moment]:
            reduction.stage(chunk_of(index), number)

    def events_in(moments, *at):
        for indices, moment in moments.items():
            if TABLE[moment]:
                here = at[0] == indices[0]
                for index, value in zip(at[1:], indices[1:]):
                    here = here & (index == value)
                pl.when(here)(lambda moment=moment: events(moment))

    def put_small(at, values):
        for column in range(values.shape[1] // LANES):
            row = pl.ds(at + column, 1)
            small[row, :] = small[row, :] + values[:, column * LANES : (column + 1) * LANES]

    small[...] = jnp.zeros_like(small)
    pull, down = r.pull, r.down

    for copy in early_loads:
        copy.wait()

    def project(step, unused):
        rows = pl.ds(pl.multiple_of(step * HALF, HALF), HALF)
        scaled, _ = normalized(tokens[rows, :].astype(F32))
        low = (scaled * r.attn_gain[...] + r.attn_shift[...]).astype(BF16)
        normed[rows, :] = low
        local[rows, :] = mm(low, r.wc[...])
        keys[rows, :] = mm(low, r.wk[...]).astype(BF16)
        values[rows, :] = mm(low, r.wv[...]).astype(BF16)
        return unused

    def summarize(stream, pair, unused):
        combo = 4 * stream + pair
        row, col = block_of(combo)
        rows, cols = pl.ds(row, 512), pl.ds(col, LANES)
        control = local[rows, cols]
        block_max = jnp.floor(jnp.max(control, axis=0, keepdims=True))
        spread = jnp.exp(control - block_max)
        local[rows, cols] = spread
        pair_rows = jnp.concatenate([keys[rows, cols], values[rows, cols]], axis=1)
        memory = add_parts(mm_rows(pair_rows, parts_of(spread)))
        memory = jnp.concatenate([one_block(memory[:LANES]), one_block(memory[LANES:])], axis=0)
        total = column_sum(spread)
        flag = jnp.broadcast_to(r.starts[stream : stream + 1, :].astype(F32), (1, LANES))
        line = iota((8, LANES), 0)
        notes[combo] = jnp.where(line == 0, block_max, jnp.where(line == 1, total, flag))
        for group in range(seq // 4):
            to = pair * (seq // 4) + group
            there[stream].sent[to, :early] = memory[group * early : (group + 1) * early]
            there[stream].sent[to, early:] = notes[combo]
            there[stream].send(to)
        return unused

    for stream in range(2):
        lax.fori_loop(2 * stream, 2 * stream + 2, project, 0)
        if stream == 0:
            pl.semaphore_wait(barrier, count)
        lax.fori_loop(0, 4, functools.partial(summarize, stream), 0)

    load_wq.wait()

    def project_query(step, unused):
        rows = pl.ds(pl.multiple_of(step * HALF, HALF), HALF)
        queries[rows, :] = mm(normed[rows, :], r.wq[...]).astype(BF16)
        return unused

    lax.fori_loop(0, 4, project_query, 0)

    def accumulate(base, rows_at, values, first):
        for column in range(4):
            place = pl.ds(pl.multiple_of(base + column * 1024 + rows_at, 8), HALF)
            block = values[:, column * LANES : (column + 1) * LANES]
            held[place] = jnp.where(first, block, held[place] + block)

    def collected(base, rows_at):
        return jnp.concatenate(
            [
                held[pl.ds(pl.multiple_of(base + column * 1024 + rows_at, 8), HALF)]
                for column in range(4)
            ],
            axis=1,
        )

    def store_block(base, square, rows_at):
        for column in range(square.shape[1] // LANES):
            place = pl.ds(pl.multiple_of(base + column * 512 + rows_at, 8), square.shape[0])
            held[place] = square[:, column * LANES : (column + 1) * LANES]

    def inside(combo, unused):
        row, col = block_of(combo)
        rows, cols = pl.ds(row, 512), pl.ds(col, LANES)
        spread = local[rows, cols]
        low = quarters(spread.astype(BF16))
        query, key = quarters(queries[rows, cols]), quarters(keys[rows, cols])
        ones = triangle(True)
        totals = [add_parts(mm(ones, part)) for part in quarters(parts_of(spread))]
        scores = [mm_lanes(query[at], stacked(key[at])) for at in range(4)]
        added = [own_blocks(mm_rows(key[at], low[at])) for at in range(3)]
        scores = [masked(score, True) for score in scores]
        numbers = [mm(scores[at], stacked(low[at])) for at in range(4)]
        memories = [memory.astype(BF16) for memory in running(added)]
        for at in range(1, 4):
            numbers[at] = numbers[at] + mm(query[at], memories[at - 1])
            totals[at] = totals[at] + totals[at - 1][LANES - 1 :]
        sums[rows, cols] = jnp.concatenate(totals, axis=0)
        logits[rows, cols] = jnp.concatenate(numbers, axis=0)
        return unused

    def hand_out(stream):
        arrived, answers = there[stream], back[stream]
        arrived.receive()
        prior_max = jnp.full((1, LANES), -HUGE_VALUE, F32)
        raw_total = jnp.zeros((1, LANES), F32)
        raw_memory = jnp.zeros((early, LANES), F32)
        line = iota((8, LANES), 0)
        for source in range(seq):
            answers.sent[source, :early] = raw_memory
            answers.sent[source, early:] = jnp.where(line == 0, prior_max, raw_total)
            if source < seq - 1:
                block_max = arrived.landed[source, early : early + 1]
                total = arrived.landed[source, early + 1 : early + 2]
                flag = arrived.landed[source, early + 2 : early + 3]
                ceiling = jnp.maximum(prior_max, block_max)
                old = (1.0 - flag) * jnp.exp(prior_max - ceiling)
                new = jnp.exp(block_max - ceiling)
                raw_total = old * raw_total + new * total
                raw_memory = old * raw_memory + new * arrived.landed[source, :early]
                prior_max = ceiling
        answers.send_all()

    def pull_back(step, unused):
        rows_at = pl.multiple_of(lax.rem(step, 4) * HALF, HALF)
        along = pl.ds(pl.multiple_of(step // 4 * 512, 512), 512)
        grad = mm_lanes(pull[pl.ds(rows_at, HALF), :], down[along, :])
        accumulate(step // 4 * 2 * CHUNK, rows_at, grad, True)
        return unused

    lax.fori_loop(0, 4, inside, 0)
    hand_out(0)
    lax.fori_loop(4, 8, inside, 0)
    load_pull.wait()
    load_down.wait()
    lax.fori_loop(0, 8, pull_back, 0)
    hand_out(1)
    lax.fori_loop(8, 16, pull_back, 0)

    def attend(combo, unused):
        row, col = block_of(combo)
        cols = pl.ds(col, LANES)
        stream, first = combo // 4, lax.rem(combo, 4) * (seq // 4)
        memory = jnp.concatenate(
            [r.box3[stream, first + group, :early] for group in range(seq // 4)], axis=0
        )
        past_max = r.box3[stream, first, early : early + 1]
        past_total = r.box3[stream, first, early + 1 : early + 2]
        block_max = notes[combo, 0:1]
        flag = notes[combo, 2:3]
        ceiling = jnp.maximum(past_max, block_max)
        carried = (1.0 - flag) * jnp.exp(past_max - ceiling)
        factor = jnp.exp(block_max - ceiling)
        notes[combo, 1:2] = ceiling
        notes[combo, 3:4] = factor
        memory = (carried * memory).astype(BF16)
        prior[combo] = memory
        prior_keys = both_blocks(memory[:HEAD])
        prior_values = both_blocks(memory[HEAD:])
        rows = pl.ds(row, 512)
        weight = local[rows, cols] * factor
        low = weight.astype(BF16)
        weights[rows, cols] = low
        inverse = 1.0 / (carried * past_total + factor * sums[rows, cols])
        sums[rows, cols] = inverse
        written = column_sum(weight * inverse)
        logit = (mm(queries[rows, cols], prior_keys) + factor * logits[rows, cols]) * inverse
        logits[rows, cols] = logit
        top = head_reduce(logit, jnp.max, -HUGE_VALUE)
        raised = jnp.exp(logit - top)
        chance = raised / head_reduce(raised, jnp.sum, 0.0)
        chances[rows, cols] = chance
        share = (chance * inverse).astype(BF16)
        shares[rows, cols] = share
        attended = quarters(mm_lanes(share, prior_values))
        share, low, value = quarters(share), quarters(low), quarters(values[rows, cols])
        mixing = [mm_lanes(share[at], stacked(low[at])) for at in range(4)]
        added = [own_blocks(mm_rows(value[at], low[at])) for at in range(3)]
        mixing = [masked(square, True) for square in mixing]
        memories = [memory.astype(BF16) for memory in running(added)]
        for at in range(4):
            attended[at] = attended[at] + mm(mixing[at], stacked(value[at]))
            if at:
                attended[at] = attended[at] + mm_lanes(share[at], memories[at - 1])
        mixed[rows, cols] = jnp.concatenate(attended, axis=0).astype(BF16)
        place = pl.ds(WRITES + lax.rem(combo, 4), 1)
        small[place, :] = small[place, :] + written
        return unused

    for stream in range(2):
        back[stream].receive()
        lax.fori_loop(4 * stream, 4 * stream + 4, attend, 0)

    load_wo.wait()
    branch, turned = r.branch, r.turned

    def project_out(step, unused):
        rows = pl.ds(pl.multiple_of(step * HALF, HALF), HALF)
        wide = tokens[rows, :].astype(F32) + mm(mixed[rows, :], r.wo[...])
        hidden[rows, :] = wide
        scaled, _ = normalized(wide)
        low = (scaled * r.ffn_gain[...] + r.ffn_shift[...]).astype(BF16)
        branch[rows, :] = low
        turned[:, rows] = low.T
        put_small(DOWN_BIAS, column_sum(pull[rows, :].astype(F32)))
        return unused

    lax.fori_loop(0, 4, project_out, 0)

    for copy in up_loads:
        copy.wait()
    up, active, pushed = r.up, r.active, r.pushed
    after = 9 * CHUNK

    def feed_forward(part_at, unused):
        base = part_at * 2 * CHUNK

        def rows_of(step, unused):
            rows_at = pl.multiple_of(step * HALF, HALF)
            rows = pl.ds(rows_at, HALF)
            raised = mm(branch[rows, :], up[part_at]) + r.up_bias[:, pl.ds(pl.multiple_of(part_at * 512, 512), 512)]
            value, slope = gelu_parts(raised)
            low = value.astype(BF16)
            active[rows, :] = low
            along = pl.ds(pl.multiple_of(part_at * 512, 512), 512)
            grad = (collected(base, rows_at) * slope).astype(BF16)
            pushed[rows, :] = grad
            accumulate(after, rows_at, mm(low, down[along, :]), part_at == 0)
            accumulate(after + 4096, rows_at, mm_lanes(grad, up[part_at]), part_at == 0)
            total = column_sum(grad.astype(F32))
            for column in range(4):
                place = pl.ds(UP_BIAS + part_at * 4 + column, 1)
                small[place, :] = small[place, :] + total[:, column * LANES : (column + 1) * LANES]
            events_in(
                {(p, q): 6 * p + q for p in range(4) for q in range(4)}, part_at, step
            )
            return unused

        lax.fori_loop(0, 4, rows_of, 0)
        for block in range(2):
            wide = mm_rows(active[:, block * HALF : (block + 1) * HALF], pull[...])
            store_block(base, wide, block * HALF)
        events_in({(p,): 6 * p + 4 for p in range(4)}, part_at)
        for block in range(2):
            wide = mm(turned[block * HALF : (block + 1) * HALF, :], pushed[...])
            store_block(base + CHUNK, wide, block * HALF)
        events_in({(p,): 6 * p + 5 for p in range(4)}, part_at)
        return unused

    lax.fori_loop(0, 4, feed_forward, 0)

    def finish_rows(step, unused):
        rows_at = pl.multiple_of(step * HALF, HALF)
        rows = pl.ds(rows_at, HALF)
        wide = hidden[rows, :]
        pushed[rows, :] = (wide + collected(after, rows_at) + r.down_bias[...]).astype(BF16)
        scaled, inverse = normalized(wide)
        upstream = collected(after + 4096, rows_at)
        put_small(FFN_GAIN, column_sum(upstream * scaled))
        put_small(FFN_SHIFT, column_sum(upstream))
        grad = pull[rows, :].astype(F32) + norm_pull(upstream, scaled, inverse, r.ffn_gain[...])
        hidden[rows, :] = grad
        branch[rows, :] = grad.astype(BF16)
        events_in({(q,): 24 + q for q in range(4)}, step)
        return unused

    lax.fori_loop(0, 4, finish_rows, 0)
    result_copy = pltpu.make_async_copy(pushed, r.out_result, r.load_sem.at[LOADS])
    result_copy.start()
    for block in range(2):
        wide = mm_rows(mixed[:, block * HALF : (block + 1) * HALF], branch[...])
        store_block(8 * CHUNK, wide, block * HALF)
    events(28)

    def into_attention(step, unused):
        rows = pl.ds(pl.multiple_of(step * HALF, HALF), HALF)
        mixed[rows, :] = mm_lanes(branch[rows, :], r.wo[...]).astype(BF16)
        turned[:, rows] = normed[rows, :].T
        return unused

    lax.fori_loop(0, 4, into_attention, 0)
    events(29)

    late, outgoing = 256 // seq, r.box4
    pulled, near_grad, total_grad, query_low = mixed, r.near_grad, r.total_grad, active

    def backward(combo, step):
        row, col = block_of(combo)
        cols = pl.ds(col, LANES)
        memory = prior[combo]
        prior_keys = both_blocks(memory[:HEAD])
        prior_values = both_blocks(memory[HEAD:])
        rows = pl.ds(row, 512)
        inverse, chance = sums[rows, cols], chances[rows, cols]
        weight, share = quarters(weights[rows, cols]), quarters(shares[rows, cols])
        pulls, query = quarters(pulled[rows, cols]), quarters(queries[rows, cols])
        key, value = quarters(keys[rows, cols]), quarters(values[rows, cols])
        wide_weight = [stacked(block) for block in weight]
        squares = [mm_lanes(pulls[at], stacked(value[at])) for at in range(4)]
        added = [own_blocks(mm_rows(value[at], weight[at])) for at in range(3)]
        squares = [masked(square, True) for square in squares]
        inner = [memory.astype(BF16) for memory in running(added)]
        grads = [mm(pulls[at], prior_values) + mm(squares[at], wide_weight[at]) for at in range(4)]
        for at in range(1, 4):
            grads[at] = grads[at] + mm(pulls[at], inner[at - 1])
        events_in({(q,): 30 + 6 * q for q in range(8)}, step)
        chance_grad = jnp.concatenate(grads, axis=0) * inverse
        middle = head_reduce(chance * chance_grad, jnp.sum, 0.0)
        number_grad = chance * (chance_grad - middle) * inverse
        total_grad[...] = -(chance_grad * chance * inverse + number_grad * logits[rows, cols])
        low = number_grad.astype(BF16)
        near_grad[...] = low
        near = quarters(low)
        squares = [mm_lanes(near[at], wide_weight[at]) for at in range(4)]
        added = [own_blocks(mm_rows(key[at], weight[at])) for at in range(3)]
        squares = [masked(square, True) for square in squares]
        inner = [memory.astype(BF16) for memory in running(added)]
        grads = [mm_lanes(near[at], prior_keys) + mm(squares[at], stacked(key[at])) for at in range(4)]
        for at in range(1, 4):
            grads[at] = grads[at] + mm_lanes(near[at], inner[at - 1])
        query_low[rows, cols] = jnp.concatenate(grads, axis=0).astype(BF16)
        events_in({(q,): 31 + 6 * q for q in range(8)}, step)

        near = quarters(near_grad[...])
        wide_share, wide_near = [stacked(block) for block in share], [stacked(block) for block in near]
        wide_pulls, wide_query = [stacked(block) for block in pulls], [stacked(block) for block in query]
        added = [own_blocks(mm_rows(query[at], near[at])) for at in reversed(range(4))]
        later_keys = running(added)
        added = [own_blocks(mm_rows(pulls[at], share[at])) for at in reversed(range(4))]
        later_values = running(added)
        key_memory, value_memory = later_keys[3], later_values[3]
        later_keys = [memory.astype(BF16) for memory in reversed(later_keys[:3])]
        later_values = [memory.astype(BF16) for memory in reversed(later_values[:3])]
        ones = triangle(False)
        totals = [add_parts(mm(ones, part)) for part in quarters(parts_of(total_grad[...]))]
        for at in reversed(range(3)):
            totals[at] = totals[at] + totals[at + 1][:1]
        carry = totals[0][:1]
        one = [masked(mm_lanes(value[at], wide_pulls[at]), False) for at in range(4)]
        two = [masked(mm_lanes(key[at], wide_query[at]), False) for at in range(4)]
        for at in range(4):
            totals[at] = totals[at] + mm(one[at], wide_share[at]) + mm(two[at], wide_near[at])
            if at < 3:
                totals[at] = totals[at] + mm(value[at], later_values[at]) + mm(key[at], later_keys[at])
        sums[rows, cols] = jnp.concatenate(totals, axis=0) * (local[rows, cols] * notes[combo, 3:4])
        events_in({(q,): 32 + 6 * q for q in range(8)}, step)
        one = [masked(mm_lanes(weight[at], wide_share[at]), False) for at in range(4)]
        two = [masked(mm_lanes(weight[at], wide_near[at]), False) for at in range(4)]
        one = [mm(one[at], wide_pulls[at]) for at in range(4)]
        two = [mm(two[at], wide_query[at]) for at in range(4)]
        for at in range(3):
            one[at] = one[at] + mm_lanes(weight[at], later_values[at])
            two[at] = two[at] + mm_lanes(weight[at], later_keys[at])
        logits[rows, cols] = jnp.concatenate(two, axis=0)
        chances[rows, cols] = jnp.concatenate(one, axis=0)
        prior_total_grad = carry
        keep = 1.0 - notes[combo, 2:3]
        memory = keep * jnp.concatenate([one_block(key_memory), one_block(value_memory)], axis=0)
        line = iota((8, LANES), 0)
        extra = jnp.where(
            line == 0,
            notes[combo, 1:2],
            jnp.where(line == 1, keep * prior_total_grad, notes[combo, 2:3]),
        )
        stream = combo // 4
        for group in range(seq // 2):
            to = stream * (seq // 2) + group
            outgoing[step // 2, to, :late] = memory[group * late : (group + 1) * late]
            outgoing[step // 2, to, late:] = extra

    def handle(pair):
        arrived, answers = theres[pair], backs[pair]
        arrived.receive()
        floor = jnp.full((1, LANES), HUGE_VALUE, F32)
        total = jnp.zeros((1, LANES), F32)
        memory = jnp.zeros((late, LANES), F32)
        line = iota((8, LANES), 0)
        for source in reversed(range(seq)):
            answers.sent[source, :late] = memory
            answers.sent[source, late:] = jnp.where(line == 0, floor, total)
            if source > 0:
                ceiling = arrived.landed[source, late : late + 1]
                flag = arrived.landed[source, late + 2 : late + 3]
                lowest = jnp.minimum(floor, ceiling)
                near = jnp.exp(lowest - ceiling)
                far = (1.0 - flag) * jnp.exp(lowest - floor)
                total = near * arrived.landed[source, late + 1 : late + 2] + far * total
                memory = near * arrived.landed[source, :late] + far * memory
                floor = lowest
        answers.send_all()

    def for_pair(pair, act):
        for at in range(4):
            pl.when(pair == at)(lambda at=at: act(at))

    def finalize(pair):
        backs[pair].receive()

        def one(stream, unused):
            combo = stream * 4 + pair
            row, col = block_of(combo)
            rows, cols = pl.ds(row, 512), pl.ds(col, LANES)
            first = stream * (seq // 2)
            memory = jnp.concatenate(
                [r.box7[pair, first + group, :late] for group in range(seq // 2)], axis=0
            )
            floor = r.box7[pair, first, late : late + 1]
            total = r.box7[pair, first, late + 1 : late + 2]
            reach = jnp.exp(notes[combo, 0:1] - floor)
            total = reach * total
            memory = (reach * memory).astype(BF16)
            key_memory, value_memory = both_blocks(memory[:HEAD]), both_blocks(memory[HEAD:])
            spread = local[rows, cols]
            low = spread.astype(BF16)
            inner = mm(keys[rows, cols], key_memory) + mm(values[rows, cols], value_memory)
            weights[rows, cols] = (sums[rows, cols] + spread * (inner + total)).astype(BF16)
            key_grad = logits[rows, cols] + mm_lanes(low, key_memory)
            value_grad = chances[rows, cols] + mm_lanes(low, value_memory)
            queries[rows, cols] = key_grad.astype(BF16)
            shares[rows, cols] = value_grad.astype(BF16)
            return unused

        lax.fori_loop(0, 2, one, 0)

    def weight_grad(index, right):
        for block in range(2):
            wide = mm(turned[block * HALF : (block + 1) * HALF, :], right[...])
            store_block(index * CHUNK, wide, block * HALF)

    def iteration(step, unused):
        backward((lax.rem(step, 2)) * 4 + step // 2, step)
        events_in({(q,): 33 + 6 * q for q in range(8)}, step)

        @pl.when(lax.rem(step, 2) == 1)
        def _():
            for_pair(step // 2, lambda at: theres[at].send_all())

        @pl.when((step >= 3) & (lax.rem(step, 2) == 1))
        def _():
            for_pair(step // 2 - 1, handle)

        events_in({(q,): 34 + 6 * q for q in range(8)}, step)
        events_in({(q,): 35 + 6 * q for q in range(8)}, step)
        return unused

    lax.fori_loop(0, 8, iteration, 0)
    weight_grad(9, query_low)
    events(78)
    for pair in range(3):
        finalize(pair)
        events(79 + pair)
    handle(3)
    events(82)
    finalize(3)
    key_low, value_low, control_low = queries, shares, weights
    for index, right in ((10, key_low), (11, value_low), (12, control_low)):
        weight_grad(index, right)
        events(73 + index)

    def input_rows(step, unused):
        rows = pl.ds(pl.multiple_of(step * HALF, HALF), HALF)
        upstream = mm_lanes(query_low[rows, :], r.wq[...])
        upstream = upstream + mm_lanes(key_low[rows, :], r.wk[...])
        upstream = upstream + mm_lanes(value_low[rows, :], r.wv[...])
        upstream = upstream + mm_lanes(control_low[rows, :], r.wc[...])
        scaled, inverse = normalized(tokens[rows, :].astype(F32))
        put_small(ATTN_GAIN, column_sum(upstream * scaled))
        put_small(ATTN_SHIFT, column_sum(upstream))
        hidden[rows, :] = hidden[rows, :] + norm_pull(
            upstream, scaled, inverse, r.attn_gain[...]
        )
        events_in({(q,): 86 + q for q in range(4)}, step)
        return unused

    lax.fori_loop(0, 4, input_rows, 0)
    grad_copy = pltpu.make_async_copy(
        hidden, r.out_input_grad, r.load_sem.at[LOADS + 1]
    )
    grad_copy.start()
    last = sizes.last()
    held[pl.ds(last[0], last[1])] = jnp.zeros((last[1], LANES), F32)
    held[pl.ds(last[0], small.shape[0])] = small[...]
    events(90)
    events(91)
    for copy in (result_copy, grad_copy):
        copy.wait()
    for exchange in (*there, *back, *theres, *backs):
        exchange.finish()
    for index in range(14):
        reduction.finish(chunk_of(index))


def deliver_kernel(full, result, input_grad, slot_means, count, *outs):
    (
        out_result, out_input_grad, attn_gain, attn_shift, wq, wk, wv, wc, wo,
        ffn_gain, ffn_shift, up, up_bias, down, down_bias, means, held, held_result, held_grad, in_sem, out_sem,
    ) = outs
    loads = [
        pltpu.make_async_copy(full.at[rows], held.at[rows], in_sem.at[at])
        for at, rows in enumerate(
            [pl.ds(13 * CHUNK, 40)] + [pl.ds(at * CHUNK, CHUNK) for at in range(13)]
        )
    ]
    loads.append(pltpu.make_async_copy(result, held_result, in_sem.at[14]))
    loads.append(pltpu.make_async_copy(input_grad, held_grad, in_sem.at[15]))
    for copy in loads:
        copy.start()
    stores = []

    def store(source, target):
        copy = pltpu.make_async_copy(source, target, out_sem.at[len(stores)])
        copy.start()
        stores.append(copy)

    for index in range(13):
        loads[1 + index].wait()
        for column in range(4):
            lanes = pl.ds(column * LANES, LANES)
            source = held.at[pl.ds(index * CHUNK + column * 512, 512)]
            if index >= 8:
                store(source, (wo, wq, wk, wv, wc)[index - 8].at[:, lanes])
            elif index % 2:
                store(source, up.at[:, pl.ds(index // 2 * 512 + column * LANES, LANES)])
            else:
                store(source, down.at[pl.ds(index // 2 * 512, 512), lanes])
    loads[14].wait()
    store(held_result, out_result)
    loads[15].wait()
    store(held_grad, out_input_grad)
    loads[0].wait()
    small = held.at[pl.ds(13 * CHUNK, 40)]
    for at, target in (
        (ATTN_GAIN, attn_gain),
        (ATTN_SHIFT, attn_shift),
        (FFN_GAIN, ffn_gain),
        (FFN_SHIFT, ffn_shift),
        (DOWN_BIAS, down_bias),
        (UP_BIAS, up_bias),
    ):
        for column in range(target.shape[1] // LANES):
            row = pl.ds(at + column, 1)
            target[:, column * LANES : (column + 1) * LANES] = small[row, :]
    for pair in range(4):
        row = small[pl.ds(WRITES + pair, 1), :]
        for head in range(2):
            line = pl.ds(2 * pair + head, 1)
            written = row[:, head * SLOTS : (head + 1) * SLOTS]
            means[line, :] = 0.9 * slot_means[line, :] + 0.1 * written / count
    for copy in stores:
        copy.wait()


def deliver_call(count, full, result, input_grad, slot_means):
    square = jax.ShapeDtypeStruct((512, 512), F32)
    vector = jax.ShapeDtypeStruct((1, 512), F32)
    long = jax.ShapeDtypeStruct((1, 2048), F32)
    shapes = [result, input_grad, vector, vector, square, square, square, square, square]
    shapes += [vector, vector, jax.ShapeDtypeStruct((512, 2048), F32), long]
    shapes += [jax.ShapeDtypeStruct((2048, 512), F32), vector, slot_means]
    anywhere = pl.BlockSpec(memory_space=pl.ANY)
    near = pl.BlockSpec(memory_space=pltpu.VMEM)

    def kernel(full, result, input_grad, slot_means, *outs):
        deliver_kernel(full, result, input_grad, slot_means, count, *outs)

    return pl.pallas_call(
        kernel,
        out_shape=[jax.ShapeDtypeStruct(shape.shape, shape.dtype) for shape in shapes],
        in_specs=[anywhere, anywhere, anywhere, near],
        out_specs=[near if shape is vector or shape is long or shape is slot_means else anywhere for shape in shapes],
        scratch_shapes=[
            pltpu.VMEM((13 * CHUNK + 40, LANES), F32),
            pltpu.VMEM(result.shape, BF16),
            pltpu.VMEM(input_grad.shape, F32),
            pltpu.SemaphoreType.DMA((16,)),
            pltpu.SemaphoreType.DMA((54,)),
        ],
        compiler_params=pltpu.CompilerParams(vmem_limit_bytes=60 * 2**20),
        name="deliver",
    )(full, result, input_grad, slot_means)


def layer_call(sizes, **arrays):
    rows, width, hidden = 1024, 512, 2048
    outputs = dict(
        out_result=jax.ShapeDtypeStruct((rows, width), BF16),
        out_input_grad=jax.ShapeDtypeStruct((rows, width), F32),
        out_full=jax.ShapeDtypeStruct((sizes.rows, LANES), F32),
    )
    low, wide = pltpu.VMEM((rows, width), BF16), pltpu.VMEM((rows, width), F32)
    weight = pltpu.VMEM((width, width), BF16)
    box = pltpu.VMEM((2, sizes.seq, 512 // sizes.seq + 8, LANES), F32)
    pair_box = pltpu.VMEM((4, sizes.seq, 256 // sizes.seq + 8, LANES), F32)
    semaphores = pltpu.SemaphoreType.DMA
    scratch = dict(
        tokens=low, wc=weight, wk=weight, wv=weight, wq=weight, wo=weight,
        up=pltpu.VMEM((4, width, 512), BF16), down=pltpu.VMEM((hidden, width), BF16), pull=low,
        normed=low, queries=low, keys=low, values=low, local=wide, weights=low,
        sums=wide, logits=wide, chances=wide, shares=low, mixed=low, hidden=wide,
        branch=low, turned=pltpu.VMEM((width, rows), BF16), active=low, pushed=low,
        near_grad=pltpu.VMEM((512, LANES), BF16), total_grad=pltpu.VMEM((512, LANES), F32),
        prior=pltpu.VMEM((8, LANES, LANES), BF16), notes=pltpu.VMEM((8, 8, LANES), F32),
        small=pltpu.VMEM((40, LANES), F32),
        held=pltpu.VMEM((sizes.rows, LANES), F32), landed=pltpu.VMEM((sizes.landing, LANES), F32),
        box0=box, box1=box, box2=box, box3=box, box4=pair_box, box5=pair_box, box6=pair_box, box7=pair_box,
        box_sem=semaphores((4, 2)), pair_sem=semaphores((4, 4)), load_sem=semaphores((LOADS + 2,)), up_sem=semaphores((4,)),
        keep_sem=semaphores((14,)), reduce_send=semaphores((14,)),
        reduce_recv=semaphores((14, 2 * LEVELS)),
    )
    names = list(arrays) + list(outputs) + list(scratch)

    def kernel(*refs):
        layer_kernel(sizes, types.SimpleNamespace(**dict(zip(names, refs, strict=True))))

    anywhere = pl.BlockSpec(memory_space=pl.ANY)
    near = pl.BlockSpec(memory_space=pltpu.VMEM)
    found = pl.pallas_call(
        kernel,
        out_shape=list(outputs.values()),
        in_specs=[anywhere if name.startswith("in_") else near for name in arrays],
        out_specs=[anywhere] * len(outputs),
        scratch_shapes=list(scratch.values()),
        compiler_params=pltpu.CompilerParams(
            collective_id=1, has_side_effects=True, vmem_limit_bytes=63 * 2**20
        ),
        name="layer",
    )(*arrays.values())
    return types.SimpleNamespace(**dict(zip(outputs, found, strict=True)))


def solution(mesh):
    sizes = Sizes(mesh.shape[DP], mesh.shape[SEQ])

    def shards(
        inputs, starts, attn_gain, attn_shift, query_weight, key_weight, value_weight, control_weight, output_weight,
        ffn_gain, ffn_shift, up_weight, up_bias, down_weight, down_bias, slot_means, cotangent,
    ):
        streams, length, width = inputs.shape
        rows = streams * length
        found = layer_call(
            sizes,
            in_tokens=inputs.reshape(rows, width),
            in_wc=control_weight,
            in_wk=key_weight,
            in_wv=value_weight,
            in_wq=query_weight,
            in_wo=output_weight,
            in_up=up_weight,
            in_down=down_weight,
            in_pull=cotangent.reshape(rows, width),
            starts=starts,
            attn_gain=attn_gain[None],
            attn_shift=attn_shift[None],
            ffn_gain=ffn_gain[None],
            ffn_shift=ffn_shift[None],
            up_bias=up_bias[None],
            down_bias=down_bias[None],
        )
        outs = list(deliver_call(
            streams * sizes.dp, found.out_full, found.out_result, found.out_input_grad, slot_means)
        )
        outs[0], outs[1] = outs[0].reshape(inputs.shape), outs[1].reshape(inputs.shape)
        for at in (2, 3, 9, 10, 12, 14):
            outs[at] = outs[at].reshape(-1)
        return tuple(outs)

    split = P(DP, SEQ, None)
    return jax.shard_map(
        shards,
        mesh=mesh,
        in_specs=(split, P(DP, SEQ)) + (P(),) * 14 + (split,),
        out_specs=(split, split) + (P(),) * 14,
        check_vma=False,
    )
```

```python
import functools
import types

import jax
import jax.numpy as jnp
from jax import lax
from jax.experimental import pallas as pl
from jax.experimental.pallas import tpu as pltpu
from jax.sharding import PartitionSpec as P

HEADS = 8
HEAD = 64
SLOTS = 64
EPSILON = 1e-05
HUGE_VALUE = 1e30
MESH = pl.DeviceIdType.MESH
F32 = jnp.float32
BF16 = jnp.bfloat16
LANES = 128
HALF = 256
DP, SEQ = "dp", "seq"
CORE, LINE, NEAR, FAR = range(4)


def mm(left, right):
    return lax.dot_general(left, right, (((1,), (0,)), ((), ())), preferred_element_type=F32)


def mm_lanes(left, right):
    return lax.dot_general(left, right, (((1,), (1,)), ((), ())), preferred_element_type=F32)


def mm_rows(left, right):
    return lax.dot_general(left, right, (((0,), (0,)), ((), ())), preferred_element_type=F32)


def iota(shape, axis):
    return lax.broadcasted_iota(jnp.int32, shape, axis)


def first_head(shape):
    return iota(shape, len(shape) - 1) < HEAD


def only_head(values, head):
    keep = first_head(values.shape) if head == 0 else jnp.logical_not(first_head(values.shape))
    return jnp.where(keep, values, jnp.zeros_like(values))


def both_blocks(rows):
    doubled = jnp.concatenate([rows, rows], axis=0)
    inside = (iota(doubled.shape, 0) < HEAD) == first_head(doubled.shape)
    return jnp.where(inside, doubled, jnp.zeros_like(doubled))


def one_block(square):
    return jnp.where(first_head((HEAD, LANES)), square[:HEAD], square[HEAD:])


def stacked(values):
    return jnp.concatenate([only_head(values, 0), only_head(values, 1)], axis=0)


def masked(square, earlier):
    row = iota(square.shape, 0)
    column = jnp.bitwise_and(iota(square.shape, 1), LANES - 1)
    keep = row >= column if earlier else row <= column
    return jnp.where(keep, square, 0.0).astype(BF16)


def own_blocks(square):
    inside = (iota(square.shape, 0) < HEAD) == first_head(square.shape)
    return jnp.where(inside, square, 0.0)


def triangle(earlier):
    row, column = iota((LANES, LANES), 0), iota((LANES, LANES), 1)
    return jnp.where(row >= column if earlier else row <= column, 1.0, 0.0).astype(BF16)


def head_reduce(values, operation, empty):
    here = first_head(values.shape)
    one = operation(jnp.where(here, values, empty), axis=1, keepdims=True)
    two = operation(jnp.where(here, empty, values), axis=1, keepdims=True)
    return jnp.where(here, one, two)


def parts_of(values):
    high = values.astype(BF16)
    return jnp.concatenate([high, (values - high.astype(F32)).astype(BF16)], axis=1)


def add_parts(product):
    return product[:, :LANES] + product[:, LANES:]


def normalized(values):
    centre = values - jnp.mean(values, axis=-1, keepdims=True)
    inverse = lax.rsqrt(jnp.mean(centre * centre, axis=-1, keepdims=True) + EPSILON)
    return centre * inverse, inverse


class Exchange:
    def __init__(self, size, sent, landed, send_sem, recv_sem):
        self.size, self.sent, self.landed = size, sent, landed
        self.send_sem, self.recv_sem = send_sem, recv_sem
        self.me = lax.axis_index(SEQ)

    def copy(self, source, target, to):
        return pltpu.make_async_remote_copy(
            src_ref=source,
            dst_ref=target,
            send_sem=self.send_sem,
            recv_sem=self.recv_sem,
            device_id={SEQ: to},
            device_id_type=MESH,
        )

    def send(self, to):
        @pl.when(to != self.me)
        def _():
            self.copy(self.sent.at[to], self.landed.at[self.me], to).start()

        @pl.when(to == self.me)
        def _():
            self.landed[self.me] = self.sent[self.me]

    def send_all(self):
        self.landed[self.me] = self.sent[self.me]
        for step in range(1, self.size):
            to = lax.rem(self.me + step, self.size)
            self.copy(self.sent.at[to], self.landed.at[self.me], to).start()

    def receive(self):
        others = self.landed.at[pl.ds(0, self.size - 1)]
        self.copy(others, others, lax.rem(self.me + 1, self.size)).wait_recv()

    def finish(self):
        others = self.sent.at[pl.ds(0, self.size - 1)]
        self.copy(others, others, lax.rem(self.me + 1, self.size)).wait_send()


class Reduction:
    def __init__(self, dp, seq, held, landed, full, send_sem, recv_sem, keep_sem):
        self.held, self.landed, self.full = held, landed, full
        self.send_sem, self.recv_sem, self.keep_sem = send_sem, recv_sem, keep_sem
        dp_at, seq_at = lax.axis_index(DP), lax.axis_index(SEQ)
        slow, fast = 4, seq // 4
        core, line = lax.rem(dp_at, 2), dp_at // 2
        near, far = lax.rem(seq_at, fast), seq_at // fast
        self.groups = {
            CORE: (2, core, lambda m: {DP: line * 2 + m}),
            LINE: (dp // 2, line, lambda m: {DP: m * 2 + core}),
            NEAR: (fast, near, lambda m: {SEQ: far * fast + m}),
            FAR: (slow, far, lambda m: {SEQ: m * fast + near}),
        }
        self.ways = dp // 2 * fast * slow

    def orders(self, rows):
        half = rows // 2
        if half % (2 * self.ways * 8) == 0:
            return [(0, half // 2, (LINE, NEAR, FAR)), (half // 2, half // 2, (NEAR, LINE, FAR))]
        return [(0, half, (LINE, NEAR, FAR))]

    def steps(self, chunk, level):
        base, rows, land, _ = chunk
        core = self.groups[CORE][1]
        if level == 0:
            return [(base, rows // 2, CORE, land)], rows // 2
        orders = self.orders(rows)
        place = land + rows // 2
        sizes = [size for _, size, _ in orders]
        starts = [base + core * (rows // 2) + offset for offset, _, _ in orders]
        for depth in range(level):
            found = []
            first = place
            for at, (_, _, axes) in enumerate(orders):
                name = axes[depth]
                count, mine, _ = self.groups[name]
                sizes[at] //= count
                found.append((starts[at], sizes[at], name, place))
                starts[at] = starts[at] + mine * sizes[at]
                place = place + sizes[at] * (count - 1)
        return found, sum(size * (self.groups[name][0] - 1) for _, size, name, _ in found)

    def rows_sent(self, chunk):
        return 2 * sum(self.steps(chunk, level)[1] for level in range(4))

    def copy(self, chunk, slot, source, target, device):
        return pltpu.make_async_remote_copy(
            src_ref=source,
            dst_ref=target,
            send_sem=self.send_sem.at[chunk[3]],
            recv_sem=self.recv_sem.at[chunk[3], slot],
            device_id=device,
            device_id_type=MESH,
        )

    def start(self, chunk, level, gather):
        for start, size, name, land in self.steps(chunk, level)[0]:
            count, at, device = self.groups[name]
            for k in range(1, count):
                to = lax.rem(at + k, count)
                if gather:
                    rows = pl.ds(pl.multiple_of(start + at * size, 8), size)
                    source = (self.held if level == 3 else self.full).at[rows]
                    target = self.full.at[rows]
                else:
                    source = self.held.at[pl.ds(pl.multiple_of(start + to * size, 8), size)]
                    target = self.landed.at[pl.ds(pl.multiple_of(land + (k - 1) * size, 8), size)]
                self.copy(chunk, level + 4 * gather, source, target, device(to)).start()
            if gather and level == 3:
                rows = pl.ds(pl.multiple_of(start + at * size, 8), size)
                pltpu.make_async_copy(
                    self.held.at[rows], self.full.at[rows], self.keep_sem.at[chunk[3]]
                ).start()

    def wait(self, chunk, level, gather):
        steps, rows = self.steps(chunk, level)
        at = pl.ds(chunk[0], rows) if gather else pl.ds(steps[0][3], rows)
        ref = (self.full if gather else self.landed).at[at]
        self.copy(chunk, level + 4 * gather, ref, ref, self.groups[CORE][2](0)).wait_recv()
        if gather and level == 3:
            at = pl.ds(chunk[0], sum(size for _, size, _, _ in steps))
            pltpu.make_async_copy(
                self.held.at[at], self.full.at[at], self.keep_sem.at[chunk[3]]
            ).wait()

    def finish(self, chunk):
        ref = self.held.at[pl.ds(0, self.rows_sent(chunk))]
        self.copy(chunk, 0, ref, ref, self.groups[CORE][2](0)).wait_send()

    def add(self, chunk, level):
        for start, size, name, land in self.steps(chunk, level)[0]:
            count, at, _ = self.groups[name]
            block = min(size, 512)

            def one(step, unused, start=start, size=size, land=land, at=at, count=count, block=block):
                rows = pl.ds(pl.multiple_of(start + at * size + step * block, 8), block)
                total = self.held[rows]
                for k in range(1, count):
                    found = pl.ds(pl.multiple_of(land + (k - 1) * size + step * block, 8), block)
                    total = total + self.landed[found]
                self.held[rows] = total
                return unused

            if size == block:
                one(0, 0)
            else:
                lax.fori_loop(0, size // block, one, 0)

    def stage(self, chunk, number):
        if number:
            level, gather = (number - 1, False) if number <= 4 else (8 - number, True)
            self.wait(chunk, level, gather)
            if not gather:
                self.add(chunk, level)
        if number < 8:
            self.start(chunk, *((number, False) if number < 4 else (7 - number, True)))


def timetable(costs, begins):
    line = {0: (0, 0.9), 1: (1, 2.9), 2: (1, 1.5), 3: (2, 2.9)}
    now, free, ready, following = 0.0, [0.0] * 3, {}, {}
    table = [[] for _ in costs] + [[]]

    def take(chunk, number, place):
        nonlocal now
        now += EVENT
        place.append((chunk, number))
        following[chunk] = number + 1
        if number == 8:
            del following[chunk], ready[chunk]
            return
        link, cost = line[min(number, 7 - number)]
        free[link] = max(now, free[link]) + (cost * SCALES[chunk])
        ready[chunk] = free[link] + LATENCY

    for moment, cost in enumerate(costs):
        now += cost
        for chunk, begin in enumerate(begins):
            if begin == moment:
                take(chunk, 0, table[moment])
        while True:
            able = [chunk for chunk in following if ready[chunk] <= now]
            if not able:
                break
            take(min(able), following[min(able)], table[moment])
    while following:
        chunk = min(following, key=lambda at: (ready[at], at))
        now = max(now, ready[chunk])
        take(chunk, following[chunk], table[-1])
    order = [event for moment in table for event in moment]
    for early, late in ((0, 9), (1, 11), (2, 13), (3, 15), (4, 17)):
        assert order.index((early, 8)) < order.index((late, 0))
    return table


def block_of(combo):
    stream, pair = combo // 4, lax.rem(combo, 4)
    return (
        pl.multiple_of(stream * 512, 512),
        pl.multiple_of(pair * LANES, LANES),
    )


def gelu_parts(raised):
    root = 0.7978845608028654
    square = raised * raised
    bent = jnp.tanh(root * raised * (1.0 + 0.044715 * square))
    half = 0.5 * (1.0 + bent)
    slope = half + (0.5 * root) * raised * (1.0 - bent * bent) * (1.0 + 0.134145 * square)
    return raised * half, slope


def norm_pull(upstream, scaled, inverse, gain):
    inside = upstream * gain
    first = jnp.mean(inside, axis=-1, keepdims=True)
    second = jnp.mean(inside * scaled, axis=-1, keepdims=True)
    return inverse * (inside - first - scaled * second)


def quarters(values):
    return [values[at * LANES : (at + 1) * LANES] for at in range(4)]


def running(blocks):
    sums = [blocks[0]]
    for block in blocks[1:]:
        sums.append(sums[-1] + block)
    return sums


def column_sum(values):
    return jnp.sum(values, axis=0, keepdims=True)


LOADS = 8
ATTN_GAIN, ATTN_SHIFT, FFN_GAIN, FFN_SHIFT, DOWN_BIAS, WRITES, UP_BIAS = range(0, 28, 4)
CHUNK = 2048
EVENT = 0.35
LATENCY = 1.5
COSTS = [0.85] * 24 + [0.5] * 4 + [0.8, 1.0] + [0.9, 0.9, 1.1, 0.7, 0.3, 0.0] * 8
COSTS += [0.9, 0.8, 0.8, 0.8, 1.0, 1.8, 0.9, 0.9] + [1.0] * 4 + [0.3]
BEGINS = [4, 5, 10, 11, 16, 17, 22, 23, 28, 78, 78, 83, 83, 84, 84, 85, 85, 90]
SCALES = [1.0] * 9 + [0.5] * 8 + [0.25]
TABLE = timetable(COSTS, BEGINS)


class Sizes:
    def __init__(self, dp, seq):
        self.dp, self.seq = dp, seq
        ways = dp // 2 * seq
        self.halves = CHUNK // 4 % (ways * 8) == 0
        self.tiny = max(512, ways * 16)
        self.rows = 13 * CHUNK + self.tiny
        self.landing = 9 * CHUNK
        self.chunks = [at for at in range(18) if self.halves or at < 9 or at % 2]

    def chunk(self, index):
        if index < 9:
            return (index * CHUNK, CHUNK, index * CHUNK, index)
        if index == 17:
            return (13 * CHUNK, self.tiny, 4 * CHUNK, 17)
        first = (index - 9) * CHUNK // 2
        return (9 * CHUNK + first, CHUNK // 2 if self.halves else CHUNK, first, index)


def layer_kernel(sizes, refs):
    r = refs
    seq = sizes.seq
    dp_at, me = lax.axis_index(DP), lax.axis_index(SEQ)

    sources = (r.in_tokens, r.in_wc, r.in_wk, r.in_wv, r.in_wq, r.in_wo, r.in_down, r.in_pull)
    targets = (r.tokens, r.wc, r.wk, r.wv, r.wq, r.wo, r.down, r.pull)
    loads = [
        pltpu.make_async_copy(source, target, r.load_sem.at[at])
        for at, (source, target) in enumerate(zip(sources, targets))
    ]
    for copy in loads:
        copy.start()
    early_loads, load_wq, load_wo, load_down, load_pull = loads[:4], *loads[4:]
    up_loads = [
        pltpu.make_async_copy(
            r.in_up.at[:, pl.ds(512 * at, 512)], r.up.at[at], r.up_sem.at[at]
        )
        for at in range(4)
    ]
    for copy in up_loads:
        copy.start()

    barrier = pltpu.get_barrier_semaphore()
    count = 0
    for step in range(1, seq):
        pl.semaphore_signal(
            barrier, inc=1, device_id={SEQ: lax.rem(me + step, seq)}, device_id_type=MESH
        )
        count += 1
    core, line = lax.rem(dp_at, 2), dp_at // 2
    pl.semaphore_signal(
        barrier, inc=1, device_id={DP: line * 2 + 1 - core}, device_id_type=MESH
    )
    count += 1
    for step in range(1, sizes.dp // 2):
        other = lax.rem(line + step, sizes.dp // 2) * 2 + core
        pl.semaphore_signal(barrier, inc=1, device_id={DP: other}, device_id_type=MESH)
        count += 1

    tokens, normed, queries, keys, values = (
        r.tokens, r.normed, r.queries, r.keys, r.values
    )
    local, weights, sums, logits, chances, shares, mixed = (
        r.local, r.weights, r.sums, r.logits, r.chances, r.shares, r.mixed
    )
    notes, prior, hidden, held, small = r.notes, r.prior, r.hidden, r.held, r.small
    early = 512 // seq
    there = [
        Exchange(seq, r.box0.at[at], r.box1.at[at], r.box_sem.at[0, at], r.box_sem.at[1, at])
        for at in range(2)
    ]
    back = [
        Exchange(seq, r.box2.at[at], r.box3.at[at], r.box_sem.at[2, at], r.box_sem.at[3, at])
        for at in range(2)
    ]
    theres = [
        Exchange(seq, r.box4.at[at], r.box5.at[at], r.pair_sem.at[0, at], r.pair_sem.at[1, at])
        for at in range(4)
    ]
    backs = [
        Exchange(seq, r.box6.at[at], r.box7.at[at], r.pair_sem.at[2, at], r.pair_sem.at[3, at])
        for at in range(4)
    ]
    reduction = Reduction(
        sizes.dp, seq, held, r.landed, r.out_full, r.reduce_send, r.reduce_recv, r.keep_sem
    )

    def events(moment):
        for index, number in TABLE[moment]:
            if index in sizes.chunks:
                reduction.stage(sizes.chunk(index), number)

    def events_in(moments, *at):
        for indices, moment in moments.items():
            if TABLE[moment]:
                here = at[0] == indices[0]
                for index, value in zip(at[1:], indices[1:]):
                    here = here & (index == value)
                pl.when(here)(lambda moment=moment: events(moment))

    def put_small(at, values):
        for column in range(values.shape[1] // LANES):
            row = pl.ds(at + column, 1)
            small[row, :] = small[row, :] + values[:, column * LANES : (column + 1) * LANES]

    small[...] = jnp.zeros_like(small)
    pull, down = r.pull, r.down

    for copy in early_loads:
        copy.wait()

    def project(step, unused):
        rows = pl.ds(pl.multiple_of(step * HALF, HALF), HALF)
        scaled, _ = normalized(tokens[rows, :].astype(F32))
        low = (scaled * r.attn_gain[...] + r.attn_shift[...]).astype(BF16)
        normed[rows, :] = low
        local[rows, :] = mm(low, r.wc[...])
        keys[rows, :] = mm(low, r.wk[...]).astype(BF16)
        values[rows, :] = mm(low, r.wv[...]).astype(BF16)
        return unused

    def summarize(stream, pair, unused):
        combo = 4 * stream + pair
        row, col = block_of(combo)
        rows, cols = pl.ds(row, 512), pl.ds(col, LANES)
        control = local[rows, cols]
        block_max = jnp.floor(jnp.max(control, axis=0, keepdims=True))
        spread = jnp.exp(control - block_max)
        local[rows, cols] = spread
        pair_rows = jnp.concatenate([keys[rows, cols], values[rows, cols]], axis=1)
        memory = add_parts(mm_rows(pair_rows, parts_of(spread)))
        memory = jnp.concatenate([one_block(memory[:LANES]), one_block(memory[LANES:])], axis=0)
        total = column_sum(spread)
        flag = jnp.broadcast_to(r.starts[stream : stream + 1, :].astype(F32), (1, LANES))
        line = iota((8, LANES), 0)
        notes[combo] = jnp.where(line == 0, block_max, jnp.where(line == 1, total, flag))
        for group in range(seq // 4):
            to = pair * (seq // 4) + group
            there[stream].sent[to, :early] = memory[group * early : (group + 1) * early]
            there[stream].sent[to, early:] = notes[combo]
            there[stream].send(to)
        return unused

    for stream in range(2):
        lax.fori_loop(2 * stream, 2 * stream + 2, project, 0)
        if stream == 0:
            pl.semaphore_wait(barrier, count)
        lax.fori_loop(0, 4, functools.partial(summarize, stream), 0)

    load_wq.wait()

    def project_query(step, unused):
        rows = pl.ds(pl.multiple_of(step * HALF, HALF), HALF)
        queries[rows, :] = mm(normed[rows, :], r.wq[...]).astype(BF16)
        return unused

    lax.fori_loop(0, 4, project_query, 0)

    def accumulate(base, rows_at, values, first):
        for column in range(4):
            place = pl.ds(pl.multiple_of(base + column * 1024 + rows_at, 8), HALF)
            block = values[:, column * LANES : (column + 1) * LANES]
            held[place] = jnp.where(first, block, held[place] + block)

    def collected(base, rows_at):
        return jnp.concatenate(
            [
                held[pl.ds(pl.multiple_of(base + column * 1024 + rows_at, 8), HALF)]
                for column in range(4)
            ],
            axis=1,
        )

    def store_block(base, square, rows_at):
        for column in range(square.shape[1] // LANES):
            place = pl.ds(pl.multiple_of(base + column * 512 + rows_at, 8), square.shape[0])
            held[place] = square[:, column * LANES : (column + 1) * LANES]

    def inside(combo, unused):
        row, col = block_of(combo)
        rows, cols = pl.ds(row, 512), pl.ds(col, LANES)
        spread = local[rows, cols]
        low = quarters(spread.astype(BF16))
        query, key = quarters(queries[rows, cols]), quarters(keys[rows, cols])
        ones = triangle(True)
        totals = [add_parts(mm(ones, part)) for part in quarters(parts_of(spread))]
        scores = [mm_lanes(query[at], stacked(key[at])) for at in range(4)]
        added = [own_blocks(mm_rows(key[at], low[at])) for at in range(3)]
        scores = [masked(score, True) for score in scores]
        numbers = [mm(scores[at], stacked(low[at])) for at in range(4)]
        memories = [memory.astype(BF16) for memory in running(added)]
        for at in range(1, 4):
            numbers[at] = numbers[at] + mm(query[at], memories[at - 1])
            totals[at] = totals[at] + totals[at - 1][LANES - 1 :]
        sums[rows, cols] = jnp.concatenate(totals, axis=0)
        logits[rows, cols] = jnp.concatenate(numbers, axis=0)
        return unused

    def hand_out(stream):
        arrived, answers = there[stream], back[stream]
        arrived.receive()
        prior_max = jnp.full((1, LANES), -HUGE_VALUE, F32)
        raw_total = jnp.zeros((1, LANES), F32)
        raw_memory = jnp.zeros((early, LANES), F32)
        line = iota((8, LANES), 0)
        for source in range(seq):
            answers.sent[source, :early] = raw_memory
            answers.sent[source, early:] = jnp.where(line == 0, prior_max, raw_total)
            if source < seq - 1:
                block_max = arrived.landed[source, early : early + 1]
                total = arrived.landed[source, early + 1 : early + 2]
                flag = arrived.landed[source, early + 2 : early + 3]
                ceiling = jnp.maximum(prior_max, block_max)
                old = (1.0 - flag) * jnp.exp(prior_max - ceiling)
                new = jnp.exp(block_max - ceiling)
                raw_total = old * raw_total + new * total
                raw_memory = old * raw_memory + new * arrived.landed[source, :early]
                prior_max = ceiling
        answers.send_all()

    def pull_back(step, unused):
        rows_at = pl.multiple_of(lax.rem(step, 4) * HALF, HALF)
        along = pl.ds(pl.multiple_of(step // 4 * 512, 512), 512)
        grad = mm_lanes(pull[pl.ds(rows_at, HALF), :], down[along, :])
        accumulate(step // 4 * 2 * CHUNK, rows_at, grad, True)
        return unused

    lax.fori_loop(0, 4, inside, 0)
    hand_out(0)
    lax.fori_loop(4, 8, inside, 0)
    load_pull.wait()
    load_down.wait()
    lax.fori_loop(0, 8, pull_back, 0)
    hand_out(1)
    lax.fori_loop(8, 16, pull_back, 0)

    def attend(combo, unused):
        row, col = block_of(combo)
        cols = pl.ds(col, LANES)
        stream, first = combo // 4, lax.rem(combo, 4) * (seq // 4)
        memory = jnp.concatenate(
            [r.box3[stream, first + group, :early] for group in range(seq // 4)], axis=0
        )
        past_max = r.box3[stream, first, early : early + 1]
        past_total = r.box3[stream, first, early + 1 : early + 2]
        block_max = notes[combo, 0:1]
        flag = notes[combo, 2:3]
        ceiling = jnp.maximum(past_max, block_max)
        carried = (1.0 - flag) * jnp.exp(past_max - ceiling)
        factor = jnp.exp(block_max - ceiling)
        notes[combo, 1:2] = ceiling
        notes[combo, 3:4] = factor
        memory = (carried * memory).astype(BF16)
        prior[combo] = memory
        prior_keys = both_blocks(memory[:HEAD])
        prior_values = both_blocks(memory[HEAD:])
        rows = pl.ds(row, 512)
        weight = local[rows, cols] * factor
        low = weight.astype(BF16)
        weights[rows, cols] = low
        inverse = 1.0 / (carried * past_total + factor * sums[rows, cols])
        sums[rows, cols] = inverse
        written = column_sum(weight * inverse)
        logit = (mm(queries[rows, cols], prior_keys) + factor * logits[rows, cols]) * inverse
        logits[rows, cols] = logit
        top = head_reduce(logit, jnp.max, -HUGE_VALUE)
        raised = jnp.exp(logit - top)
        chance = raised / head_reduce(raised, jnp.sum, 0.0)
        chances[rows, cols] = chance
        share = (chance * inverse).astype(BF16)
        shares[rows, cols] = share
        attended = quarters(mm_lanes(share, prior_values))
        share, low, value = quarters(share), quarters(low), quarters(values[rows, cols])
        mixing = [mm_lanes(share[at], stacked(low[at])) for at in range(4)]
        added = [own_blocks(mm_rows(value[at], low[at])) for at in range(3)]
        mixing = [masked(square, True) for square in mixing]
        memories = [memory.astype(BF16) for memory in running(added)]
        for at in range(4):
            attended[at] = attended[at] + mm(mixing[at], stacked(value[at]))
            if at:
                attended[at] = attended[at] + mm_lanes(share[at], memories[at - 1])
        mixed[rows, cols] = jnp.concatenate(attended, axis=0).astype(BF16)
        place = pl.ds(WRITES + lax.rem(combo, 4), 1)
        small[place, :] = small[place, :] + written
        return unused

    for stream in range(2):
        back[stream].receive()
        lax.fori_loop(4 * stream, 4 * stream + 4, attend, 0)

    load_wo.wait()
    branch, turned = r.branch, r.turned

    def project_out(step, unused):
        rows = pl.ds(pl.multiple_of(step * HALF, HALF), HALF)
        wide = tokens[rows, :].astype(F32) + mm(mixed[rows, :], r.wo[...])
        hidden[rows, :] = wide
        scaled, _ = normalized(wide)
        low = (scaled * r.ffn_gain[...] + r.ffn_shift[...]).astype(BF16)
        branch[rows, :] = low
        turned[:, rows] = low.T
        put_small(DOWN_BIAS, column_sum(pull[rows, :].astype(F32)))
        return unused

    lax.fori_loop(0, 4, project_out, 0)

    for copy in up_loads:
        copy.wait()
    up, active, pushed = r.up, r.active, r.pushed
    after = 9 * CHUNK

    def feed_forward(part_at, unused):
        base = part_at * 2 * CHUNK

        def rows_of(step, unused):
            rows_at = pl.multiple_of(step * HALF, HALF)
            rows = pl.ds(rows_at, HALF)
            raised = mm(branch[rows, :], up[part_at]) + r.up_bias[:, pl.ds(pl.multiple_of(part_at * 512, 512), 512)]
            value, slope = gelu_parts(raised)
            low = value.astype(BF16)
            active[rows, :] = low
            along = pl.ds(pl.multiple_of(part_at * 512, 512), 512)
            grad = (collected(base, rows_at) * slope).astype(BF16)
            pushed[rows, :] = grad
            accumulate(after, rows_at, mm(low, down[along, :]), part_at == 0)
            accumulate(after + 4096, rows_at, mm_lanes(grad, up[part_at]), part_at == 0)
            total = column_sum(grad.astype(F32))
            for column in range(4):
                place = pl.ds(UP_BIAS + part_at * 4 + column, 1)
                small[place, :] = small[place, :] + total[:, column * LANES : (column + 1) * LANES]
            events_in(
                {(p, q): 6 * p + q for p in range(4) for q in range(4)}, part_at, step
            )
            return unused

        lax.fori_loop(0, 4, rows_of, 0)
        for block in range(2):
            wide = mm_rows(active[:, block * HALF : (block + 1) * HALF], pull[...])
            store_block(base, wide, block * HALF)
        events_in({(p,): 6 * p + 4 for p in range(4)}, part_at)
        for block in range(2):
            wide = mm(turned[block * HALF : (block + 1) * HALF, :], pushed[...])
            store_block(base + CHUNK, wide, block * HALF)
        events_in({(p,): 6 * p + 5 for p in range(4)}, part_at)
        return unused

    lax.fori_loop(0, 4, feed_forward, 0)

    def finish_rows(step, unused):
        rows_at = pl.multiple_of(step * HALF, HALF)
        rows = pl.ds(rows_at, HALF)
        wide = hidden[rows, :]
        pushed[rows, :] = (wide + collected(after, rows_at) + r.down_bias[...]).astype(BF16)
        scaled, inverse = normalized(wide)
        upstream = collected(after + 4096, rows_at)
        put_small(FFN_GAIN, column_sum(upstream * scaled))
        put_small(FFN_SHIFT, column_sum(upstream))
        grad = pull[rows, :].astype(F32) + norm_pull(upstream, scaled, inverse, r.ffn_gain[...])
        hidden[rows, :] = grad
        branch[rows, :] = grad.astype(BF16)
        events_in({(q,): 24 + q for q in range(4)}, step)
        return unused

    lax.fori_loop(0, 4, finish_rows, 0)
    result_copy = pltpu.make_async_copy(pushed, r.out_result, r.load_sem.at[LOADS])
    result_copy.start()
    for block in range(2):
        wide = mm_rows(mixed[:, block * HALF : (block + 1) * HALF], branch[...])
        store_block(8 * CHUNK, wide, block * HALF)
    events(28)

    def into_attention(step, unused):
        rows = pl.ds(pl.multiple_of(step * HALF, HALF), HALF)
        mixed[rows, :] = mm_lanes(branch[rows, :], r.wo[...]).astype(BF16)
        turned[:, rows] = normed[rows, :].T
        return unused

    lax.fori_loop(0, 4, into_attention, 0)
    events(29)

    late, outgoing = 256 // seq, r.box4
    pulled, near_grad, total_grad, query_low = mixed, r.near_grad, r.total_grad, active

    def backward(combo, step):
        row, col = block_of(combo)
        cols = pl.ds(col, LANES)
        memory = prior[combo]
        prior_keys = both_blocks(memory[:HEAD])
        prior_values = both_blocks(memory[HEAD:])
        rows = pl.ds(row, 512)
        inverse, chance = sums[rows, cols], chances[rows, cols]
        weight, share = quarters(weights[rows, cols]), quarters(shares[rows, cols])
        pulls, query = quarters(pulled[rows, cols]), quarters(queries[rows, cols])
        key, value = quarters(keys[rows, cols]), quarters(values[rows, cols])
        wide_weight = [stacked(block) for block in weight]
        squares = [mm_lanes(pulls[at], stacked(value[at])) for at in range(4)]
        added = [own_blocks(mm_rows(value[at], weight[at])) for at in range(3)]
        squares = [masked(square, True) for square in squares]
        inner = [memory.astype(BF16) for memory in running(added)]
        grads = [mm(pulls[at], prior_values) + mm(squares[at], wide_weight[at]) for at in range(4)]
        for at in range(1, 4):
            grads[at] = grads[at] + mm(pulls[at], inner[at - 1])
        events_in({(q,): 30 + 6 * q for q in range(8)}, step)
        chance_grad = jnp.concatenate(grads, axis=0) * inverse
        middle = head_reduce(chance * chance_grad, jnp.sum, 0.0)
        number_grad = chance * (chance_grad - middle) * inverse
        total_grad[...] = -(chance_grad * chance * inverse + number_grad * logits[rows, cols])
        low = number_grad.astype(BF16)
        near_grad[...] = low
        near = quarters(low)
        squares = [mm_lanes(near[at], wide_weight[at]) for at in range(4)]
        added = [own_blocks(mm_rows(key[at], weight[at])) for at in range(3)]
        squares = [masked(square, True) for square in squares]
        inner = [memory.astype(BF16) for memory in running(added)]
        grads = [mm_lanes(near[at], prior_keys) + mm(squares[at], stacked(key[at])) for at in range(4)]
        for at in range(1, 4):
            grads[at] = grads[at] + mm_lanes(near[at], inner[at - 1])
        query_low[rows, cols] = jnp.concatenate(grads, axis=0).astype(BF16)
        events_in({(q,): 31 + 6 * q for q in range(8)}, step)

        near = quarters(near_grad[...])
        wide_share, wide_near = [stacked(block) for block in share], [stacked(block) for block in near]
        wide_pulls, wide_query = [stacked(block) for block in pulls], [stacked(block) for block in query]
        added = [own_blocks(mm_rows(query[at], near[at])) for at in reversed(range(4))]
        later_keys = running(added)
        added = [own_blocks(mm_rows(pulls[at], share[at])) for at in reversed(range(4))]
        later_values = running(added)
        key_memory, value_memory = later_keys[3], later_values[3]
        later_keys = [memory.astype(BF16) for memory in reversed(later_keys[:3])]
        later_values = [memory.astype(BF16) for memory in reversed(later_values[:3])]
        ones = triangle(False)
        totals = [add_parts(mm(ones, part)) for part in quarters(parts_of(total_grad[...]))]
        for at in reversed(range(3)):
            totals[at] = totals[at] + totals[at + 1][:1]
        carry = totals[0][:1]
        one = [masked(mm_lanes(value[at], wide_pulls[at]), False) for at in range(4)]
        two = [masked(mm_lanes(key[at], wide_query[at]), False) for at in range(4)]
        for at in range(4):
            totals[at] = totals[at] + mm(one[at], wide_share[at]) + mm(two[at], wide_near[at])
            if at < 3:
                totals[at] = totals[at] + mm(value[at], later_values[at]) + mm(key[at], later_keys[at])
        sums[rows, cols] = jnp.concatenate(totals, axis=0) * (local[rows, cols] * notes[combo, 3:4])
        events_in({(q,): 32 + 6 * q for q in range(8)}, step)
        one = [masked(mm_lanes(weight[at], wide_share[at]), False) for at in range(4)]
        two = [masked(mm_lanes(weight[at], wide_near[at]), False) for at in range(4)]
        one = [mm(one[at], wide_pulls[at]) for at in range(4)]
        two = [mm(two[at], wide_query[at]) for at in range(4)]
        for at in range(3):
            one[at] = one[at] + mm_lanes(weight[at], later_values[at])
            two[at] = two[at] + mm_lanes(weight[at], later_keys[at])
        logits[rows, cols] = jnp.concatenate(two, axis=0)
        chances[rows, cols] = jnp.concatenate(one, axis=0)
        prior_total_grad = carry
        keep = 1.0 - notes[combo, 2:3]
        memory = keep * jnp.concatenate([one_block(key_memory), one_block(value_memory)], axis=0)
        line = iota((8, LANES), 0)
        extra = jnp.where(
            line == 0,
            notes[combo, 1:2],
            jnp.where(line == 1, keep * prior_total_grad, notes[combo, 2:3]),
        )
        stream = combo // 4
        for group in range(seq // 2):
            to = stream * (seq // 2) + group
            outgoing[step // 2, to, :late] = memory[group * late : (group + 1) * late]
            outgoing[step // 2, to, late:] = extra

    def handle(pair):
        arrived, answers = theres[pair], backs[pair]
        arrived.receive()
        floor = jnp.full((1, LANES), HUGE_VALUE, F32)
        total = jnp.zeros((1, LANES), F32)
        memory = jnp.zeros((late, LANES), F32)
        line = iota((8, LANES), 0)
        for source in reversed(range(seq)):
            answers.sent[source, :late] = memory
            answers.sent[source, late:] = jnp.where(line == 0, floor, total)
            if source > 0:
                ceiling = arrived.landed[source, late : late + 1]
                flag = arrived.landed[source, late + 2 : late + 3]
                lowest = jnp.minimum(floor, ceiling)
                near = jnp.exp(lowest - ceiling)
                far = (1.0 - flag) * jnp.exp(lowest - floor)
                total = near * arrived.landed[source, late + 1 : late + 2] + far * total
                memory = near * arrived.landed[source, :late] + far * memory
                floor = lowest
        answers.send_all()

    def for_pair(pair, act):
        for at in range(4):
            pl.when(pair == at)(lambda at=at: act(at))

    def finalize(pair):
        backs[pair].receive()

        def one(stream, unused):
            combo = stream * 4 + pair
            row, col = block_of(combo)
            rows, cols = pl.ds(row, 512), pl.ds(col, LANES)
            first = stream * (seq // 2)
            memory = jnp.concatenate(
                [r.box7[pair, first + group, :late] for group in range(seq // 2)], axis=0
            )
            floor = r.box7[pair, first, late : late + 1]
            total = r.box7[pair, first, late + 1 : late + 2]
            reach = jnp.exp(notes[combo, 0:1] - floor)
            total = reach * total
            memory = (reach * memory).astype(BF16)
            key_memory, value_memory = both_blocks(memory[:HEAD]), both_blocks(memory[HEAD:])
            spread = local[rows, cols]
            low = spread.astype(BF16)
            inner = mm(keys[rows, cols], key_memory) + mm(values[rows, cols], value_memory)
            weights[rows, cols] = (sums[rows, cols] + spread * (inner + total)).astype(BF16)
            key_grad = logits[rows, cols] + mm_lanes(low, key_memory)
            value_grad = chances[rows, cols] + mm_lanes(low, value_memory)
            queries[rows, cols] = key_grad.astype(BF16)
            shares[rows, cols] = value_grad.astype(BF16)
            return unused

        lax.fori_loop(0, 2, one, 0)

    def weight_grad(index, right):
        for block in range(2):
            wide = mm(turned[...], right[:, block * HALF : (block + 1) * HALF])
            store_block(index * CHUNK + block * 1024, wide, 0)

    def iteration(step, unused):
        backward((lax.rem(step, 2)) * 4 + step // 2, step)
        events_in({(q,): 33 + 6 * q for q in range(8)}, step)

        @pl.when(lax.rem(step, 2) == 1)
        def _():
            for_pair(step // 2, lambda at: theres[at].send_all())

        @pl.when((step >= 3) & (lax.rem(step, 2) == 1))
        def _():
            for_pair(step // 2 - 1, handle)

        events_in({(q,): 34 + 6 * q for q in range(8)}, step)
        events_in({(q,): 35 + 6 * q for q in range(8)}, step)
        return unused

    lax.fori_loop(0, 8, iteration, 0)
    weight_grad(9, query_low)
    events(78)
    for pair in range(3):
        finalize(pair)
        events(79 + pair)
    handle(3)
    events(82)
    finalize(3)
    key_low, value_low, control_low = queries, shares, weights
    for index, right in ((10, key_low), (11, value_low), (12, control_low)):
        weight_grad(index, right)
        events(73 + index)

    def input_rows(step, unused):
        rows = pl.ds(pl.multiple_of(step * HALF, HALF), HALF)
        upstream = mm_lanes(query_low[rows, :], r.wq[...])
        upstream = upstream + mm_lanes(key_low[rows, :], r.wk[...])
        upstream = upstream + mm_lanes(value_low[rows, :], r.wv[...])
        upstream = upstream + mm_lanes(control_low[rows, :], r.wc[...])
        scaled, inverse = normalized(tokens[rows, :].astype(F32))
        put_small(ATTN_GAIN, column_sum(upstream * scaled))
        put_small(ATTN_SHIFT, column_sum(upstream))
        hidden[rows, :] = hidden[rows, :] + norm_pull(
            upstream, scaled, inverse, r.attn_gain[...]
        )
        events_in({(q,): 86 + q for q in range(4)}, step)
        return unused

    lax.fori_loop(0, 4, input_rows, 0)
    grad_copy = pltpu.make_async_copy(
        hidden, r.out_input_grad, r.load_sem.at[LOADS + 1]
    )
    grad_copy.start()
    last = sizes.chunk(17)
    held[pl.ds(last[0], last[1])] = jnp.zeros((last[1], LANES), F32)
    held[pl.ds(last[0], small.shape[0])] = small[...]
    events(90)
    events(91)
    for copy in (result_copy, grad_copy):
        copy.wait()
    for exchange in (*there, *back, *theres, *backs):
        exchange.finish()
    for index in sizes.chunks:
        reduction.finish(sizes.chunk(index))


def deliver_kernel(full, result, input_grad, slot_means, count, *outs):
    (
        out_result, out_input_grad, attn_gain, attn_shift, wq, wk, wv, wc, wo,
        ffn_gain, ffn_shift, up, up_bias, down, down_bias, means, held, held_result, held_grad, in_sem, out_sem,
    ) = outs
    loads = [
        pltpu.make_async_copy(full.at[rows], held.at[rows], in_sem.at[at])
        for at, rows in enumerate(
            [pl.ds(13 * CHUNK, 40)] + [pl.ds(at * CHUNK, CHUNK) for at in range(13)]
        )
    ]
    loads.append(pltpu.make_async_copy(result, held_result, in_sem.at[14]))
    loads.append(pltpu.make_async_copy(input_grad, held_grad, in_sem.at[15]))
    for copy in loads:
        copy.start()
    stores = []

    def store(source, target):
        copy = pltpu.make_async_copy(source, target, out_sem.at[len(stores)])
        copy.start()
        stores.append(copy)

    for index in range(13):
        loads[1 + index].wait()
        for column in range(4):
            lanes = pl.ds(column * LANES, LANES)
            source = held.at[pl.ds(index * CHUNK + column * 512, 512)]
            if index >= 8:
                store(source, (wo, wq, wk, wv, wc)[index - 8].at[:, lanes])
            elif index % 2:
                store(source, up.at[:, pl.ds(index // 2 * 512 + column * LANES, LANES)])
            else:
                store(source, down.at[pl.ds(index // 2 * 512, 512), lanes])
    loads[14].wait()
    store(held_result, out_result)
    loads[15].wait()
    store(held_grad, out_input_grad)
    loads[0].wait()
    small = held.at[pl.ds(13 * CHUNK, 40)]
    for at, target in (
        (ATTN_GAIN, attn_gain),
        (ATTN_SHIFT, attn_shift),
        (FFN_GAIN, ffn_gain),
        (FFN_SHIFT, ffn_shift),
        (DOWN_BIAS, down_bias),
        (UP_BIAS, up_bias),
    ):
        for column in range(target.shape[1] // LANES):
            row = pl.ds(at + column, 1)
            target[:, column * LANES : (column + 1) * LANES] = small[row, :]
    for pair in range(4):
        row = small[pl.ds(WRITES + pair, 1), :]
        for head in range(2):
            line = pl.ds(2 * pair + head, 1)
            written = row[:, head * SLOTS : (head + 1) * SLOTS]
            means[line, :] = 0.9 * slot_means[line, :] + 0.1 * written / count
    for copy in stores:
        copy.wait()


def deliver_call(count, full, result, input_grad, slot_means):
    square = jax.ShapeDtypeStruct((512, 512), F32)
    vector = jax.ShapeDtypeStruct((1, 512), F32)
    long = jax.ShapeDtypeStruct((1, 2048), F32)
    shapes = [result, input_grad, vector, vector, square, square, square, square, square]
    shapes += [vector, vector, jax.ShapeDtypeStruct((512, 2048), F32), long]
    shapes += [jax.ShapeDtypeStruct((2048, 512), F32), vector, slot_means]
    anywhere = pl.BlockSpec(memory_space=pl.ANY)
    near = pl.BlockSpec(memory_space=pltpu.VMEM)

    def kernel(full, result, input_grad, slot_means, *outs):
        deliver_kernel(full, result, input_grad, slot_means, count, *outs)

    return pl.pallas_call(
        kernel,
        out_shape=[jax.ShapeDtypeStruct(shape.shape, shape.dtype) for shape in shapes],
        in_specs=[anywhere, anywhere, anywhere, near],
        out_specs=[near if shape is vector or shape is long or shape is slot_means else anywhere for shape in shapes],
        scratch_shapes=[
            pltpu.VMEM((13 * CHUNK + 40, LANES), F32),
            pltpu.VMEM(result.shape, BF16),
            pltpu.VMEM(input_grad.shape, F32),
            pltpu.SemaphoreType.DMA((16,)),
            pltpu.SemaphoreType.DMA((54,)),
        ],
        compiler_params=pltpu.CompilerParams(vmem_limit_bytes=60 * 2**20),
        name="deliver",
    )(full, result, input_grad, slot_means)


def layer_call(sizes, **arrays):
    rows, width, hidden = 1024, 512, 2048
    outputs = dict(
        out_result=jax.ShapeDtypeStruct((rows, width), BF16),
        out_input_grad=jax.ShapeDtypeStruct((rows, width), F32),
        out_full=jax.ShapeDtypeStruct((sizes.rows, LANES), F32),
    )
    low, wide = pltpu.VMEM((rows, width), BF16), pltpu.VMEM((rows, width), F32)
    weight = pltpu.VMEM((width, width), BF16)
    box = pltpu.VMEM((2, sizes.seq, 512 // sizes.seq + 8, LANES), F32)
    pair_box = pltpu.VMEM((4, sizes.seq, 256 // sizes.seq + 8, LANES), F32)
    semaphores = pltpu.SemaphoreType.DMA
    scratch = dict(
        tokens=low, wc=weight, wk=weight, wv=weight, wq=weight, wo=weight,
        up=pltpu.VMEM((4, width, 512), BF16), down=pltpu.VMEM((hidden, width), BF16), pull=low,
        normed=low, queries=low, keys=low, values=low, local=wide, weights=low,
        sums=wide, logits=wide, chances=wide, shares=low, mixed=low, hidden=wide,
        branch=low, turned=pltpu.VMEM((width, rows), BF16), active=low, pushed=low,
        near_grad=pltpu.VMEM((512, LANES), BF16), total_grad=pltpu.VMEM((512, LANES), F32),
        prior=pltpu.VMEM((8, LANES, LANES), BF16), notes=pltpu.VMEM((8, 8, LANES), F32),
        small=pltpu.VMEM((40, LANES), F32),
        held=pltpu.VMEM((sizes.rows, LANES), F32), landed=pltpu.VMEM((sizes.landing, LANES), F32),
        box0=box, box1=box, box2=box, box3=box, box4=pair_box, box5=pair_box, box6=pair_box, box7=pair_box,
        box_sem=semaphores((4, 2)), pair_sem=semaphores((4, 4)), load_sem=semaphores((LOADS + 2,)), up_sem=semaphores((4,)),
        keep_sem=semaphores((18,)), reduce_send=semaphores((18,)),
        reduce_recv=semaphores((18, 8)),
    )
    names = list(arrays) + list(outputs) + list(scratch)

    def kernel(*refs):
        layer_kernel(sizes, types.SimpleNamespace(**dict(zip(names, refs, strict=True))))

    anywhere = pl.BlockSpec(memory_space=pl.ANY)
    near = pl.BlockSpec(memory_space=pltpu.VMEM)
    found = pl.pallas_call(
        kernel,
        out_shape=list(outputs.values()),
        in_specs=[anywhere if name.startswith("in_") else near for name in arrays],
        out_specs=[anywhere] * len(outputs),
        scratch_shapes=list(scratch.values()),
        compiler_params=pltpu.CompilerParams(
            collective_id=1, has_side_effects=True, vmem_limit_bytes=63 * 2**20
        ),
        name="layer",
    )(*arrays.values())
    return types.SimpleNamespace(**dict(zip(outputs, found, strict=True)))


def solution(mesh):
    sizes = Sizes(mesh.shape[DP], mesh.shape[SEQ])

    def shards(
        inputs, starts, attn_gain, attn_shift, query_weight, key_weight, value_weight, control_weight, output_weight,
        ffn_gain, ffn_shift, up_weight, up_bias, down_weight, down_bias, slot_means, cotangent,
    ):
        streams, length, width = inputs.shape
        rows = streams * length
        found = layer_call(
            sizes,
            in_tokens=inputs.reshape(rows, width),
            in_wc=control_weight,
            in_wk=key_weight,
            in_wv=value_weight,
            in_wq=query_weight,
            in_wo=output_weight,
            in_up=up_weight,
            in_down=down_weight,
            in_pull=cotangent.reshape(rows, width),
            starts=starts,
            attn_gain=attn_gain[None],
            attn_shift=attn_shift[None],
            ffn_gain=ffn_gain[None],
            ffn_shift=ffn_shift[None],
            up_bias=up_bias[None],
            down_bias=down_bias[None],
        )
        outs = list(deliver_call(
            streams * sizes.dp, found.out_full, found.out_result, found.out_input_grad, slot_means)
        )
        outs[0], outs[1] = outs[0].reshape(inputs.shape), outs[1].reshape(inputs.shape)
        for at in (2, 3, 9, 10, 12, 14):
            outs[at] = outs[at].reshape(-1)
        return tuple(outs)

    split = P(DP, SEQ, None)
    return jax.shard_map(
        shards,
        mesh=mesh,
        in_specs=(split, P(DP, SEQ)) + (P(),) * 14 + (split,),
        out_specs=(split, split) + (P(),) * 14,
        check_vma=False,
    )
```

```python
import functools
import types

import jax
import jax.numpy as jnp
from jax import lax
from jax.experimental import pallas as pl
from jax.experimental.pallas import tpu as pltpu
from jax.sharding import PartitionSpec as P

HEADS = 8
HEAD = 64
SLOTS = 64
EPSILON = 1e-05
HUGE_VALUE = 1e30
MESH = pl.DeviceIdType.MESH
F32 = jnp.float32
BF16 = jnp.bfloat16
LANES = 128
HALF = 256
DP, SEQ = "dp", "seq"
CORE, LINE, NEAR, FAR = range(4)


def mm(left, right):
    return lax.dot_general(left, right, (((1,), (0,)), ((), ())), preferred_element_type=F32)


def mm_lanes(left, right):
    return lax.dot_general(left, right, (((1,), (1,)), ((), ())), preferred_element_type=F32)


def mm_rows(left, right):
    return lax.dot_general(left, right, (((0,), (0,)), ((), ())), preferred_element_type=F32)


def iota(shape, axis):
    return lax.broadcasted_iota(jnp.int32, shape, axis)


def first_head(shape):
    return iota(shape, len(shape) - 1) < HEAD


def only_head(values, head):
    keep = first_head(values.shape) if head == 0 else jnp.logical_not(first_head(values.shape))
    return jnp.where(keep, values, jnp.zeros_like(values))


def both_blocks(rows):
    doubled = jnp.concatenate([rows, rows], axis=0)
    inside = (iota(doubled.shape, 0) < HEAD) == first_head(doubled.shape)
    return jnp.where(inside, doubled, jnp.zeros_like(doubled))


def one_block(square):
    return jnp.where(first_head((HEAD, LANES)), square[:HEAD], square[HEAD:])


def stacked(values):
    return jnp.concatenate([only_head(values, 0), only_head(values, 1)], axis=0)


def masked(square, earlier):
    row = iota(square.shape, 0)
    column = jnp.bitwise_and(iota(square.shape, 1), LANES - 1)
    keep = row >= column if earlier else row <= column
    return jnp.where(keep, square, 0.0).astype(BF16)


def own_blocks(square):
    inside = (iota(square.shape, 0) < HEAD) == first_head(square.shape)
    return jnp.where(inside, square, 0.0)


def triangle(earlier):
    row, column = iota((LANES, LANES), 0), iota((LANES, LANES), 1)
    return jnp.where(row >= column if earlier else row <= column, 1.0, 0.0).astype(BF16)


def head_reduce(values, operation, empty):
    here = first_head(values.shape)
    one = operation(jnp.where(here, values, empty), axis=1, keepdims=True)
    two = operation(jnp.where(here, empty, values), axis=1, keepdims=True)
    return jnp.where(here, one, two)


def parts_of(values):
    high = values.astype(BF16)
    return jnp.concatenate([high, (values - high.astype(F32)).astype(BF16)], axis=1)


def add_parts(product):
    return product[:, :LANES] + product[:, LANES:]


def normalized(values):
    centre = values - jnp.mean(values, axis=-1, keepdims=True)
    inverse = lax.rsqrt(jnp.mean(centre * centre, axis=-1, keepdims=True) + EPSILON)
    return centre * inverse, inverse


class Exchange:
    def __init__(self, size, sent, landed, send_sem, recv_sem):
        self.size, self.sent, self.landed = size, sent, landed
        self.send_sem, self.recv_sem = send_sem, recv_sem
        self.me = lax.axis_index(SEQ)

    def copy(self, source, target, to):
        return pltpu.make_async_remote_copy(
            src_ref=source,
            dst_ref=target,
            send_sem=self.send_sem,
            recv_sem=self.recv_sem,
            device_id={SEQ: to},
            device_id_type=MESH,
        )

    def send(self, to):
        @pl.when(to != self.me)
        def _():
            self.copy(self.sent.at[to], self.landed.at[self.me], to).start()

        @pl.when(to == self.me)
        def _():
            self.landed[self.me] = self.sent[self.me]

    def send_all(self):
        self.landed[self.me] = self.sent[self.me]
        for step in range(1, self.size):
            to = lax.rem(self.me + step, self.size)
            self.copy(self.sent.at[to], self.landed.at[self.me], to).start()

    def receive(self):
        others = self.landed.at[pl.ds(0, self.size - 1)]
        self.copy(others, others, lax.rem(self.me + 1, self.size)).wait_recv()

    def finish(self):
        others = self.sent.at[pl.ds(0, self.size - 1)]
        self.copy(others, others, lax.rem(self.me + 1, self.size)).wait_send()


class Reduction:
    def __init__(self, dp, seq, held, landed, full, send_sem, recv_sem, keep_sem):
        self.held, self.landed, self.full = held, landed, full
        self.send_sem, self.recv_sem, self.keep_sem = send_sem, recv_sem, keep_sem
        dp_at, seq_at = lax.axis_index(DP), lax.axis_index(SEQ)
        slow, fast = 4, seq // 4
        core, line = lax.rem(dp_at, 2), dp_at // 2
        near, far = lax.rem(seq_at, fast), seq_at // fast
        self.groups = {
            CORE: (2, core, lambda m: {DP: line * 2 + m}),
            LINE: (dp // 2, line, lambda m: {DP: m * 2 + core}),
            NEAR: (fast, near, lambda m: {SEQ: far * fast + m}),
            FAR: (slow, far, lambda m: {SEQ: m * fast + near}),
        }
        self.ways = dp // 2 * fast * slow

    def orders(self, rows):
        half = rows // 2
        if half % (2 * self.ways * 8) == 0:
            return [(0, half // 2, (LINE, NEAR, FAR)), (half // 2, half // 2, (NEAR, LINE, FAR))]
        return [(0, half, (LINE, NEAR, FAR))]

    def steps(self, chunk, level):
        base, rows, land, _ = chunk
        core = self.groups[CORE][1]
        if level == 0:
            return [(base, rows // 2, CORE, land)], rows // 2
        orders = self.orders(rows)
        place = land + rows // 2
        sizes = [size for _, size, _ in orders]
        starts = [base + core * (rows // 2) + offset for offset, _, _ in orders]
        for depth in range(level):
            found = []
            first = place
            for at, (_, _, axes) in enumerate(orders):
                name = axes[depth]
                count, mine, _ = self.groups[name]
                sizes[at] //= count
                found.append((starts[at], sizes[at], name, place))
                starts[at] = starts[at] + mine * sizes[at]
                place = place + sizes[at] * (count - 1)
        return found, sum(size * (self.groups[name][0] - 1) for _, size, name, _ in found)

    def rows_sent(self, chunk):
        return 2 * sum(self.steps(chunk, level)[1] for level in range(4))

    def copy(self, chunk, slot, source, target, device):
        return pltpu.make_async_remote_copy(
            src_ref=source,
            dst_ref=target,
            send_sem=self.send_sem.at[chunk[3]],
            recv_sem=self.recv_sem.at[chunk[3], slot],
            device_id=device,
            device_id_type=MESH,
        )

    def start(self, chunk, level, gather):
        for start, size, name, land in self.steps(chunk, level)[0]:
            count, at, device = self.groups[name]
            for k in range(1, count):
                to = lax.rem(at + k, count)
                if gather:
                    rows = pl.ds(pl.multiple_of(start + at * size, 8), size)
                    source = (self.held if level == 3 else self.full).at[rows]
                    target = self.full.at[rows]
                else:
                    source = self.held.at[pl.ds(pl.multiple_of(start + to * size, 8), size)]
                    target = self.landed.at[pl.ds(pl.multiple_of(land + (k - 1) * size, 8), size)]
                self.copy(chunk, level + 4 * gather, source, target, device(to)).start()
            if gather and level == 3:
                rows = pl.ds(pl.multiple_of(start + at * size, 8), size)
                pltpu.make_async_copy(
                    self.held.at[rows], self.full.at[rows], self.keep_sem.at[chunk[3]]
                ).start()

    def wait(self, chunk, level, gather):
        steps, rows = self.steps(chunk, level)
        at = pl.ds(chunk[0], rows) if gather else pl.ds(steps[0][3], rows)
        ref = (self.full if gather else self.landed).at[at]
        self.copy(chunk, level + 4 * gather, ref, ref, self.groups[CORE][2](0)).wait_recv()
        if gather and level == 3:
            at = pl.ds(chunk[0], sum(size for _, size, _, _ in steps))
            pltpu.make_async_copy(
                self.held.at[at], self.full.at[at], self.keep_sem.at[chunk[3]]
            ).wait()

    def finish(self, chunk):
        ref = self.held.at[pl.ds(0, self.rows_sent(chunk))]
        self.copy(chunk, 0, ref, ref, self.groups[CORE][2](0)).wait_send()

    def add(self, chunk, level):
        for start, size, name, land in self.steps(chunk, level)[0]:
            count, at, _ = self.groups[name]
            block = min(size, 512)

            def one(step, unused, start=start, size=size, land=land, at=at, count=count, block=block):
                rows = pl.ds(pl.multiple_of(start + at * size + step * block, 8), block)
                total = self.held[rows]
                for k in range(1, count):
                    found = pl.ds(pl.multiple_of(land + (k - 1) * size + step * block, 8), block)
                    total = total + self.landed[found]
                self.held[rows] = total
                return unused

            if size == block:
                one(0, 0)
            else:
                lax.fori_loop(0, size // block, one, 0)

    def stage(self, chunk, number):
        if number:
            level, gather = (number - 1, False) if number <= 4 else (8 - number, True)
            self.wait(chunk, level, gather)
            if not gather:
                self.add(chunk, level)
        if number < 8:
            self.start(chunk, *((number, False) if number < 4 else (7 - number, True)))


def timetable(costs, begins):
    line = {0: (0, 0.9), 1: (1, 2.9), 2: (1, 1.5), 3: (2, 2.9)}
    now, free, ready, following = 0.0, [0.0] * 3, {}, {}
    table = [[] for _ in costs] + [[]]

    def take(chunk, number, place):
        nonlocal now
        now += EVENT
        place.append((chunk, number))
        following[chunk] = number + 1
        if number == 8:
            del following[chunk], ready[chunk]
            return
        link, cost = line[min(number, 7 - number)]
        free[link] = max(now, free[link]) + (cost * SCALES[chunk])
        ready[chunk] = free[link] + LATENCY

    for moment, cost in enumerate(costs):
        now += cost
        for chunk, begin in enumerate(begins):
            if begin == moment:
                take(chunk, 0, table[moment])
        while True:
            able = [chunk for chunk in following if ready[chunk] <= now]
            if not able:
                break
            take(min(able), following[min(able)], table[moment])
    while following:
        chunk = min(following, key=lambda at: (ready[at], at))
        now = max(now, ready[chunk])
        take(chunk, following[chunk], table[-1])
    order = [event for moment in table for event in moment]
    for early, late in ((0, 9), (1, 11), (2, 13), (3, 15), (4, 17)):
        assert order.index((early, 8)) < order.index((late, 0))
    return table


def block_of(combo):
    stream, pair = combo // 4, lax.rem(combo, 4)
    return (
        pl.multiple_of(stream * 512, 512),
        pl.multiple_of(pair * LANES, LANES),
    )


def gelu_parts(raised):
    root = 0.7978845608028654
    square = raised * raised
    bent = jnp.tanh(root * raised * (1.0 + 0.044715 * square))
    half = 0.5 * (1.0 + bent)
    slope = half + (0.5 * root) * raised * (1.0 - bent * bent) * (1.0 + 0.134145 * square)
    return raised * half, slope


def norm_pull(upstream, scaled, inverse, gain):
    inside = upstream * gain
    first = jnp.mean(inside, axis=-1, keepdims=True)
    second = jnp.mean(inside * scaled, axis=-1, keepdims=True)
    return inverse * (inside - first - scaled * second)


def quarters(values):
    return [values[at * LANES : (at + 1) * LANES] for at in range(4)]


def running(blocks):
    sums = [blocks[0]]
    for block in blocks[1:]:
        sums.append(sums[-1] + block)
    return sums


def column_sum(values):
    return jnp.sum(values, axis=0, keepdims=True)


LOADS = 8
ATTN_GAIN, ATTN_SHIFT, FFN_GAIN, FFN_SHIFT, DOWN_BIAS, WRITES, UP_BIAS = range(0, 28, 4)
CHUNK = 2048
EVENT = 0.35
LATENCY = 1.5
COSTS = [0.85] * 24 + [0.5] * 4 + [0.8, 1.0] + [0.9, 0.9, 1.1, 0.7, 0.3, 0.0] * 8
COSTS += [0.9, 0.8, 0.8, 0.8, 1.0, 1.8, 0.9, 0.9] + [1.0] * 4 + [0.3]
BEGINS = [4, 5, 10, 11, 16, 17, 22, 23, 28, 78, 78, 83, 83, 84, 84, 85, 85, 90]
SCALES = [1.0] * 9 + [0.5] * 8 + [0.25]
TABLE = timetable(COSTS, BEGINS)


class Sizes:
    def __init__(self, dp, seq):
        self.dp, self.seq = dp, seq
        ways = dp // 2 * seq
        self.halves = CHUNK // 4 % (ways * 8) == 0
        self.tiny = max(512, ways * 16)
        self.rows = 13 * CHUNK + self.tiny
        self.landing = 9 * CHUNK
        self.chunks = [at for at in range(18) if self.halves or at < 9 or at % 2]

    def chunk(self, index):
        if index < 9:
            return (index * CHUNK, CHUNK, index * CHUNK, index)
        if index == 17:
            return (13 * CHUNK, self.tiny, 4 * CHUNK, 17)
        first = (index - 9) * CHUNK // 2
        return (9 * CHUNK + first, CHUNK // 2 if self.halves else CHUNK, first, index)


def layer_kernel(sizes, refs):
    r = refs
    seq = sizes.seq
    dp_at, me = lax.axis_index(DP), lax.axis_index(SEQ)

    sources = (r.in_tokens, r.in_wc, r.in_wk, r.in_wv, r.in_wq, r.in_wo, r.in_down, r.in_pull)
    targets = (r.tokens, r.wc, r.wk, r.wv, r.wq, r.wo, r.down, r.pull)
    loads = [
        pltpu.make_async_copy(source, target, r.load_sem.at[at])
        for at, (source, target) in enumerate(zip(sources, targets))
    ]
    for copy in loads:
        copy.start()
    early_loads, load_wq, load_wo, load_down, load_pull = loads[:4], *loads[4:]
    up_loads = [
        pltpu.make_async_copy(
            r.in_up.at[:, pl.ds(512 * at, 512)], r.up.at[at], r.up_sem.at[at]
        )
        for at in range(4)
    ]
    for copy in up_loads:
        copy.start()

    barrier = pltpu.get_barrier_semaphore()
    count = 0
    for step in range(1, seq):
        pl.semaphore_signal(
            barrier, inc=1, device_id={SEQ: lax.rem(me + step, seq)}, device_id_type=MESH
        )
        count += 1
    core, line = lax.rem(dp_at, 2), dp_at // 2
    pl.semaphore_signal(
        barrier, inc=1, device_id={DP: line * 2 + 1 - core}, device_id_type=MESH
    )
    count += 1
    for step in range(1, sizes.dp // 2):
        other = lax.rem(line + step, sizes.dp // 2) * 2 + core
        pl.semaphore_signal(barrier, inc=1, device_id={DP: other}, device_id_type=MESH)
        count += 1

    tokens, normed, queries, keys, values = (
        r.tokens, r.normed, r.queries, r.keys, r.values
    )
    local, weights, sums, logits, chances, shares, mixed = (
        r.local, r.weights, r.sums, r.logits, r.chances, r.shares, r.mixed
    )
    notes, prior, hidden, held, small = r.notes, r.prior, r.hidden, r.held, r.small
    early = 512 // seq
    there = [
        Exchange(seq, r.box0.at[at], r.box1.at[at], r.box_sem.at[0, at], r.box_sem.at[1, at])
        for at in range(2)
    ]
    back = [
        Exchange(seq, r.box2.at[at], r.box3.at[at], r.box_sem.at[2, at], r.box_sem.at[3, at])
        for at in range(2)
    ]
    theres = [
        Exchange(seq, r.box4.at[at], r.box5.at[at], r.pair_sem.at[0, at], r.pair_sem.at[1, at])
        for at in range(4)
    ]
    backs = [
        Exchange(seq, r.box6.at[at], r.box7.at[at], r.pair_sem.at[2, at], r.pair_sem.at[3, at])
        for at in range(4)
    ]
    reduction = Reduction(
        sizes.dp, seq, held, r.landed, r.out_full, r.reduce_send, r.reduce_recv, r.keep_sem
    )

    def events(moment):
        for index, number in TABLE[moment]:
            if index in sizes.chunks:
                reduction.stage(sizes.chunk(index), number)

    def events_in(moments, *at):
        for indices, moment in moments.items():
            if TABLE[moment]:
                here = at[0] == indices[0]
                for index, value in zip(at[1:], indices[1:]):
                    here = here & (index == value)
                pl.when(here)(lambda moment=moment: events(moment))

    def put_small(at, values):
        for column in range(values.shape[1] // LANES):
            row = pl.ds(at + column, 1)
            small[row, :] = small[row, :] + values[:, column * LANES : (column + 1) * LANES]

    small[...] = jnp.zeros_like(small)
    pull, down = r.pull, r.down

    for copy in early_loads:
        copy.wait()

    def project(step, unused):
        rows = pl.ds(pl.multiple_of(step * HALF, HALF), HALF)
        scaled, _ = normalized(tokens[rows, :].astype(F32))
        low = (scaled * r.attn_gain[...] + r.attn_shift[...]).astype(BF16)
        normed[rows, :] = low
        local[rows, :] = mm(low, r.wc[...])
        keys[rows, :] = mm(low, r.wk[...]).astype(BF16)
        values[rows, :] = mm(low, r.wv[...]).astype(BF16)
        return unused

    def summarize(stream, pair, unused):
        combo = 4 * stream + pair
        row, col = block_of(combo)
        rows, cols = pl.ds(row, 512), pl.ds(col, LANES)
        control = local[rows, cols]
        block_max = jnp.floor(jnp.max(control, axis=0, keepdims=True))
        spread = jnp.exp(control - block_max)
        local[rows, cols] = spread
        pair_rows = jnp.concatenate([keys[rows, cols], values[rows, cols]], axis=1)
        memory = add_parts(mm_rows(pair_rows, parts_of(spread)))
        memory = jnp.concatenate([one_block(memory[:LANES]), one_block(memory[LANES:])], axis=0)
        total = column_sum(spread)
        flag = jnp.broadcast_to(r.starts[:, stream : stream + 1].astype(F32), (1, LANES))
        line = iota((8, LANES), 0)
        notes[combo] = jnp.where(line == 0, block_max, jnp.where(line == 1, total, flag))
        for group in range(seq // 4):
            to = pair * (seq // 4) + group
            there[stream].sent[to, :early] = memory[group * early : (group + 1) * early]
            there[stream].sent[to, early:] = notes[combo]
            there[stream].send(to)
        return unused

    for stream in range(2):
        lax.fori_loop(2 * stream, 2 * stream + 2, project, 0)
        if stream == 0:
            pl.semaphore_wait(barrier, count)
        lax.fori_loop(0, 4, functools.partial(summarize, stream), 0)

    load_wq.wait()

    def project_query(step, unused):
        rows = pl.ds(pl.multiple_of(step * HALF, HALF), HALF)
        queries[rows, :] = mm(normed[rows, :], r.wq[...]).astype(BF16)
        return unused

    lax.fori_loop(0, 4, project_query, 0)

    def accumulate(base, rows_at, values, first):
        for column in range(4):
            place = pl.ds(pl.multiple_of(base + column * 1024 + rows_at, 8), HALF)
            block = values[:, column * LANES : (column + 1) * LANES]
            held[place] = jnp.where(first, block, held[place] + block)

    def collected(base, rows_at):
        return jnp.concatenate(
            [
                held[pl.ds(pl.multiple_of(base + column * 1024 + rows_at, 8), HALF)]
                for column in range(4)
            ],
            axis=1,
        )

    def store_block(base, square, rows_at):
        for column in range(square.shape[1] // LANES):
            place = pl.ds(pl.multiple_of(base + column * 512 + rows_at, 8), square.shape[0])
            held[place] = square[:, column * LANES : (column + 1) * LANES]

    def inside(combo, unused):
        row, col = block_of(combo)
        rows, cols = pl.ds(row, 512), pl.ds(col, LANES)
        spread = local[rows, cols]
        low = quarters(spread.astype(BF16))
        query, key = quarters(queries[rows, cols]), quarters(keys[rows, cols])
        ones = triangle(True)
        totals = [add_parts(mm(ones, part)) for part in quarters(parts_of(spread))]
        scores = [mm_lanes(query[at], stacked(key[at])) for at in range(4)]
        added = [own_blocks(mm_rows(key[at], low[at])) for at in range(3)]
        scores = [masked(score, True) for score in scores]
        numbers = [mm(scores[at], stacked(low[at])) for at in range(4)]
        memories = [memory.astype(BF16) for memory in running(added)]
        for at in range(1, 4):
            numbers[at] = numbers[at] + mm(query[at], memories[at - 1])
            totals[at] = totals[at] + totals[at - 1][LANES - 1 :]
        sums[rows, cols] = jnp.concatenate(totals, axis=0)
        logits[rows, cols] = jnp.concatenate(numbers, axis=0)
        return unused

    def hand_out(stream):
        arrived, answers = there[stream], back[stream]
        arrived.receive()
        prior_max = jnp.full((1, LANES), -HUGE_VALUE, F32)
        raw_total = jnp.zeros((1, LANES), F32)
        raw_memory = jnp.zeros((early, LANES), F32)
        line = iota((8, LANES), 0)
        for source in range(seq):
            answers.sent[source, :early] = raw_memory
            answers.sent[source, early:] = jnp.where(line == 0, prior_max, raw_total)
            if source < seq - 1:
                block_max = arrived.landed[source, early : early + 1]
                total = arrived.landed[source, early + 1 : early + 2]
                flag = arrived.landed[source, early + 2 : early + 3]
                ceiling = jnp.maximum(prior_max, block_max)
                old = (1.0 - flag) * jnp.exp(prior_max - ceiling)
                new = jnp.exp(block_max - ceiling)
                raw_total = old * raw_total + new * total
                raw_memory = old * raw_memory + new * arrived.landed[source, :early]
                prior_max = ceiling
        answers.send_all()

    def pull_back(step, unused):
        rows_at = pl.multiple_of(lax.rem(step, 4) * HALF, HALF)
        along = pl.ds(pl.multiple_of(step // 4 * 512, 512), 512)
        grad = mm_lanes(pull[pl.ds(rows_at, HALF), :], down[along, :])
        accumulate(step // 4 * 2 * CHUNK, rows_at, grad, True)
        return unused

    lax.fori_loop(0, 4, inside, 0)
    hand_out(0)
    lax.fori_loop(4, 8, inside, 0)
    load_pull.wait()
    load_down.wait()
    lax.fori_loop(0, 8, pull_back, 0)
    hand_out(1)
    lax.fori_loop(8, 16, pull_back, 0)

    def attend(combo, unused):
        row, col = block_of(combo)
        cols = pl.ds(col, LANES)
        stream, first = combo // 4, lax.rem(combo, 4) * (seq // 4)
        memory = jnp.concatenate(
            [r.box3[stream, first + group, :early] for group in range(seq // 4)], axis=0
        )
        past_max = r.box3[stream, first, early : early + 1]
        past_total = r.box3[stream, first, early + 1 : early + 2]
        block_max = notes[combo, 0:1]
        flag = notes[combo, 2:3]
        ceiling = jnp.maximum(past_max, block_max)
        carried = (1.0 - flag) * jnp.exp(past_max - ceiling)
        factor = jnp.exp(block_max - ceiling)
        notes[combo, 1:2] = ceiling
        notes[combo, 3:4] = factor
        memory = (carried * memory).astype(BF16)
        prior[combo] = memory
        prior_keys = both_blocks(memory[:HEAD])
        prior_values = both_blocks(memory[HEAD:])
        rows = pl.ds(row, 512)
        weight = local[rows, cols] * factor
        low = weight.astype(BF16)
        weights[rows, cols] = low
        inverse = 1.0 / (carried * past_total + factor * sums[rows, cols])
        sums[rows, cols] = inverse
        written = column_sum(weight * inverse)
        logit = (mm(queries[rows, cols], prior_keys) + factor * logits[rows, cols]) * inverse
        logits[rows, cols] = logit
        top = head_reduce(logit, jnp.max, -HUGE_VALUE)
        raised = jnp.exp(logit - top)
        chance = raised / head_reduce(raised, jnp.sum, 0.0)
        chances[rows, cols] = chance
        share = (chance * inverse).astype(BF16)
        shares[rows, cols] = share
        attended = quarters(mm_lanes(share, prior_values))
        share, low, value = quarters(share), quarters(low), quarters(values[rows, cols])
        mixing = [mm_lanes(share[at], stacked(low[at])) for at in range(4)]
        added = [own_blocks(mm_rows(value[at], low[at])) for at in range(3)]
        mixing = [masked(square, True) for square in mixing]
        memories = [memory.astype(BF16) for memory in running(added)]
        for at in range(4):
            attended[at] = attended[at] + mm(mixing[at], stacked(value[at]))
            if at:
                attended[at] = attended[at] + mm_lanes(share[at], memories[at - 1])
        mixed[rows, cols] = jnp.concatenate(attended, axis=0).astype(BF16)
        place = pl.ds(WRITES + lax.rem(combo, 4), 1)
        small[place, :] = small[place, :] + written
        return unused

    for stream in range(2):
        back[stream].receive()
        lax.fori_loop(4 * stream, 4 * stream + 4, attend, 0)

    load_wo.wait()
    branch, turned = r.branch, r.turned

    def project_out(step, unused):
        rows = pl.ds(pl.multiple_of(step * HALF, HALF), HALF)
        wide = tokens[rows, :].astype(F32) + mm(mixed[rows, :], r.wo[...])
        hidden[rows, :] = wide
        scaled, _ = normalized(wide)
        low = (scaled * r.ffn_gain[...] + r.ffn_shift[...]).astype(BF16)
        branch[rows, :] = low
        turned[:, rows] = low.T
        put_small(DOWN_BIAS, column_sum(pull[rows, :].astype(F32)))
        return unused

    lax.fori_loop(0, 4, project_out, 0)

    for copy in up_loads:
        copy.wait()
    up, active, pushed = r.up, r.active, r.pushed
    after = 9 * CHUNK

    def feed_forward(part_at, unused):
        base = part_at * 2 * CHUNK

        def rows_of(step, unused):
            rows_at = pl.multiple_of(step * HALF, HALF)
            rows = pl.ds(rows_at, HALF)
            raised = mm(branch[rows, :], up[part_at]) + r.up_bias[:, pl.ds(pl.multiple_of(part_at * 512, 512), 512)]
            value, slope = gelu_parts(raised)
            low = value.astype(BF16)
            active[rows, :] = low
            along = pl.ds(pl.multiple_of(part_at * 512, 512), 512)
            grad = (collected(base, rows_at) * slope).astype(BF16)
            pushed[rows, :] = grad
            accumulate(after, rows_at, mm(low, down[along, :]), part_at == 0)
            accumulate(after + 4096, rows_at, mm_lanes(grad, up[part_at]), part_at == 0)
            total = column_sum(grad.astype(F32))
            for column in range(4):
                place = pl.ds(UP_BIAS + part_at * 4 + column, 1)
                small[place, :] = small[place, :] + total[:, column * LANES : (column + 1) * LANES]
            events_in(
                {(p, q): 6 * p + q for p in range(4) for q in range(4)}, part_at, step
            )
            return unused

        lax.fori_loop(0, 4, rows_of, 0)
        for block in range(2):
            wide = mm_rows(active[:, block * HALF : (block + 1) * HALF], pull[...])
            store_block(base, wide, block * HALF)
        events_in({(p,): 6 * p + 4 for p in range(4)}, part_at)
        for block in range(2):
            wide = mm(turned[block * HALF : (block + 1) * HALF, :], pushed[...])
            store_block(base + CHUNK, wide, block * HALF)
        events_in({(p,): 6 * p + 5 for p in range(4)}, part_at)
        return unused

    lax.fori_loop(0, 4, feed_forward, 0)

    def finish_rows(step, unused):
        rows_at = pl.multiple_of(step * HALF, HALF)
        rows = pl.ds(rows_at, HALF)
        wide = hidden[rows, :]
        pushed[rows, :] = (wide + collected(after, rows_at) + r.down_bias[...]).astype(BF16)
        scaled, inverse = normalized(wide)
        upstream = collected(after + 4096, rows_at)
        put_small(FFN_GAIN, column_sum(upstream * scaled))
        put_small(FFN_SHIFT, column_sum(upstream))
        grad = pull[rows, :].astype(F32) + norm_pull(upstream, scaled, inverse, r.ffn_gain[...])
        hidden[rows, :] = grad
        branch[rows, :] = grad.astype(BF16)
        events_in({(q,): 24 + q for q in range(4)}, step)
        return unused

    lax.fori_loop(0, 4, finish_rows, 0)
    result_copy = pltpu.make_async_copy(pushed, r.out_result, r.load_sem.at[LOADS])
    result_copy.start()
    for block in range(2):
        wide = mm_rows(mixed[:, block * HALF : (block + 1) * HALF], branch[...])
        store_block(8 * CHUNK, wide, block * HALF)
    events(28)

    def into_attention(step, unused):
        rows = pl.ds(pl.multiple_of(step * HALF, HALF), HALF)
        mixed[rows, :] = mm_lanes(branch[rows, :], r.wo[...]).astype(BF16)
        turned[:, rows] = normed[rows, :].T
        return unused

    lax.fori_loop(0, 4, into_attention, 0)
    events(29)

    late, outgoing = 256 // seq, r.box4
    pulled, near_grad, total_grad, query_low = mixed, r.near_grad, r.total_grad, active

    def backward(combo, step):
        row, col = block_of(combo)
        cols = pl.ds(col, LANES)
        memory = prior[combo]
        prior_keys = both_blocks(memory[:HEAD])
        prior_values = both_blocks(memory[HEAD:])
        rows = pl.ds(row, 512)
        inverse, chance = sums[rows, cols], chances[rows, cols]
        weight, share = quarters(weights[rows, cols]), quarters(shares[rows, cols])
        pulls, query = quarters(pulled[rows, cols]), quarters(queries[rows, cols])
        key, value = quarters(keys[rows, cols]), quarters(values[rows, cols])
        wide_weight = [stacked(block) for block in weight]
        squares = [mm_lanes(pulls[at], stacked(value[at])) for at in range(4)]
        added = [own_blocks(mm_rows(value[at], weight[at])) for at in range(3)]
        squares = [masked(square, True) for square in squares]
        inner = [memory.astype(BF16) for memory in running(added)]
        grads = [mm(pulls[at], prior_values) + mm(squares[at], wide_weight[at]) for at in range(4)]
        for at in range(1, 4):
            grads[at] = grads[at] + mm(pulls[at], inner[at - 1])
        events_in({(q,): 30 + 6 * q for q in range(8)}, step)
        chance_grad = jnp.concatenate(grads, axis=0) * inverse
        middle = head_reduce(chance * chance_grad, jnp.sum, 0.0)
        number_grad = chance * (chance_grad - middle) * inverse
        total_grad[...] = -(chance_grad * chance * inverse + number_grad * logits[rows, cols])
        low = number_grad.astype(BF16)
        near_grad[...] = low
        near = quarters(low)
        squares = [mm_lanes(near[at], wide_weight[at]) for at in range(4)]
        added = [own_blocks(mm_rows(key[at], weight[at])) for at in range(3)]
        squares = [masked(square, True) for square in squares]
        inner = [memory.astype(BF16) for memory in running(added)]
        grads = [mm_lanes(near[at], prior_keys) + mm(squares[at], stacked(key[at])) for at in range(4)]
        for at in range(1, 4):
            grads[at] = grads[at] + mm_lanes(near[at], inner[at - 1])
        query_low[rows, cols] = jnp.concatenate(grads, axis=0).astype(BF16)
        events_in({(q,): 31 + 6 * q for q in range(8)}, step)

        near = quarters(near_grad[...])
        wide_share, wide_near = [stacked(block) for block in share], [stacked(block) for block in near]
        wide_pulls, wide_query = [stacked(block) for block in pulls], [stacked(block) for block in query]
        added = [own_blocks(mm_rows(query[at], near[at])) for at in reversed(range(4))]
        later_keys = running(added)
        added = [own_blocks(mm_rows(pulls[at], share[at])) for at in reversed(range(4))]
        later_values = running(added)
        key_memory, value_memory = later_keys[3], later_values[3]
        later_keys = [memory.astype(BF16) for memory in reversed(later_keys[:3])]
        later_values = [memory.astype(BF16) for memory in reversed(later_values[:3])]
        ones = triangle(False)
        totals = [add_parts(mm(ones, part)) for part in quarters(parts_of(total_grad[...]))]
        for at in reversed(range(3)):
            totals[at] = totals[at] + totals[at + 1][:1]
        carry = totals[0][:1]
        one = [masked(mm_lanes(value[at], wide_pulls[at]), False) for at in range(4)]
        two = [masked(mm_lanes(key[at], wide_query[at]), False) for at in range(4)]
        for at in range(4):
            totals[at] = totals[at] + mm(one[at], wide_share[at]) + mm(two[at], wide_near[at])
            if at < 3:
                totals[at] = totals[at] + mm(value[at], later_values[at]) + mm(key[at], later_keys[at])
        sums[rows, cols] = jnp.concatenate(totals, axis=0) * (local[rows, cols] * notes[combo, 3:4])
        events_in({(q,): 32 + 6 * q for q in range(8)}, step)
        one = [masked(mm_lanes(weight[at], wide_share[at]), False) for at in range(4)]
        two = [masked(mm_lanes(weight[at], wide_near[at]), False) for at in range(4)]
        one = [mm(one[at], wide_pulls[at]) for at in range(4)]
        two = [mm(two[at], wide_query[at]) for at in range(4)]
        for at in range(3):
            one[at] = one[at] + mm_lanes(weight[at], later_values[at])
            two[at] = two[at] + mm_lanes(weight[at], later_keys[at])
        logits[rows, cols] = jnp.concatenate(two, axis=0)
        chances[rows, cols] = jnp.concatenate(one, axis=0)
        prior_total_grad = carry
        keep = 1.0 - notes[combo, 2:3]
        memory = keep * jnp.concatenate([one_block(key_memory), one_block(value_memory)], axis=0)
        line = iota((8, LANES), 0)
        extra = jnp.where(
            line == 0,
            notes[combo, 1:2],
            jnp.where(line == 1, keep * prior_total_grad, notes[combo, 2:3]),
        )
        stream = combo // 4
        for group in range(seq // 2):
            to = stream * (seq // 2) + group
            outgoing[step // 2, to, :late] = memory[group * late : (group + 1) * late]
            outgoing[step // 2, to, late:] = extra

    def handle(pair):
        arrived, answers = theres[pair], backs[pair]
        arrived.receive()
        floor = jnp.full((1, LANES), HUGE_VALUE, F32)
        total = jnp.zeros((1, LANES), F32)
        memory = jnp.zeros((late, LANES), F32)
        line = iota((8, LANES), 0)
        for source in reversed(range(seq)):
            answers.sent[source, :late] = memory
            answers.sent[source, late:] = jnp.where(line == 0, floor, total)
            if source > 0:
                ceiling = arrived.landed[source, late : late + 1]
                flag = arrived.landed[source, late + 2 : late + 3]
                lowest = jnp.minimum(floor, ceiling)
                near = jnp.exp(lowest - ceiling)
                far = (1.0 - flag) * jnp.exp(lowest - floor)
                total = near * arrived.landed[source, late + 1 : late + 2] + far * total
                memory = near * arrived.landed[source, :late] + far * memory
                floor = lowest
        answers.send_all()

    def for_pair(pair, act):
        for at in range(4):
            pl.when(pair == at)(lambda at=at: act(at))

    def finalize(pair):
        backs[pair].receive()

        def one(stream, unused):
            combo = stream * 4 + pair
            row, col = block_of(combo)
            rows, cols = pl.ds(row, 512), pl.ds(col, LANES)
            first = stream * (seq // 2)
            memory = jnp.concatenate(
                [r.box7[pair, first + group, :late] for group in range(seq // 2)], axis=0
            )
            floor = r.box7[pair, first, late : late + 1]
            total = r.box7[pair, first, late + 1 : late + 2]
            reach = jnp.exp(notes[combo, 0:1] - floor)
            total = reach * total
            memory = (reach * memory).astype(BF16)
            key_memory, value_memory = both_blocks(memory[:HEAD]), both_blocks(memory[HEAD:])
            spread = local[rows, cols]
            low = spread.astype(BF16)
            inner = mm(keys[rows, cols], key_memory) + mm(values[rows, cols], value_memory)
            weights[rows, cols] = (sums[rows, cols] + spread * (inner + total)).astype(BF16)
            key_grad = logits[rows, cols] + mm_lanes(low, key_memory)
            value_grad = chances[rows, cols] + mm_lanes(low, value_memory)
            queries[rows, cols] = key_grad.astype(BF16)
            shares[rows, cols] = value_grad.astype(BF16)
            return unused

        lax.fori_loop(0, 2, one, 0)

    def weight_grad(index, right):
        for block in range(2):
            wide = mm(turned[...], right[:, block * HALF : (block + 1) * HALF])
            store_block(index * CHUNK + block * 1024, wide, 0)

    def iteration(step, unused):
        backward((lax.rem(step, 2)) * 4 + step // 2, step)
        events_in({(q,): 33 + 6 * q for q in range(8)}, step)

        @pl.when(lax.rem(step, 2) == 1)
        def _():
            for_pair(step // 2, lambda at: theres[at].send_all())

        @pl.when((step >= 3) & (lax.rem(step, 2) == 1))
        def _():
            for_pair(step // 2 - 1, handle)

        events_in({(q,): 34 + 6 * q for q in range(8)}, step)
        events_in({(q,): 35 + 6 * q for q in range(8)}, step)
        return unused

    lax.fori_loop(0, 8, iteration, 0)
    weight_grad(9, query_low)
    events(78)
    for pair in range(3):
        finalize(pair)
        events(79 + pair)
    handle(3)
    events(82)
    finalize(3)
    key_low, value_low, control_low = queries, shares, weights
    for index, right in ((10, key_low), (11, value_low), (12, control_low)):
        weight_grad(index, right)
        events(73 + index)

    def input_rows(step, unused):
        rows = pl.ds(pl.multiple_of(step * HALF, HALF), HALF)
        upstream = mm_lanes(query_low[rows, :], r.wq[...])
        upstream = upstream + mm_lanes(key_low[rows, :], r.wk[...])
        upstream = upstream + mm_lanes(value_low[rows, :], r.wv[...])
        upstream = upstream + mm_lanes(control_low[rows, :], r.wc[...])
        scaled, inverse = normalized(tokens[rows, :].astype(F32))
        put_small(ATTN_GAIN, column_sum(upstream * scaled))
        put_small(ATTN_SHIFT, column_sum(upstream))
        hidden[rows, :] = hidden[rows, :] + norm_pull(
            upstream, scaled, inverse, r.attn_gain[...]
        )
        events_in({(q,): 86 + q for q in range(4)}, step)
        return unused

    lax.fori_loop(0, 4, input_rows, 0)
    grad_copy = pltpu.make_async_copy(
        hidden, r.out_input_grad, r.load_sem.at[LOADS + 1]
    )
    grad_copy.start()
    last = sizes.chunk(17)
    held[pl.ds(last[0], last[1])] = jnp.zeros((last[1], LANES), F32)
    held[pl.ds(last[0], small.shape[0])] = small[...]
    events(90)
    events(91)
    for copy in (result_copy, grad_copy):
        copy.wait()
    for exchange in (*there, *back, *theres, *backs):
        exchange.finish()
    for index in sizes.chunks:
        reduction.finish(sizes.chunk(index))


def deliver_kernel(full, result, input_grad, slot_means, count, *outs):
    (
        out_result, out_input_grad, attn_gain, attn_shift, wq, wk, wv, wc, wo,
        ffn_gain, ffn_shift, up, up_bias, down, down_bias, means, held, held_result, held_grad, in_sem, out_sem,
    ) = outs
    loads = [
        pltpu.make_async_copy(full.at[rows], held.at[rows], in_sem.at[at])
        for at, rows in enumerate(
            [pl.ds(13 * CHUNK, 40)] + [pl.ds(at * 1024, 1024) for at in range(26)]
        )
    ]
    loads.append(pltpu.make_async_copy(result, held_result, in_sem.at[27]))
    loads.append(pltpu.make_async_copy(input_grad, held_grad, in_sem.at[28]))
    for copy in loads:
        copy.start()
    stores = []

    def store(source, target):
        copy = pltpu.make_async_copy(source, target, out_sem.at[len(stores)])
        copy.start()
        stores.append(copy)

    for index in range(13):
        for column in range(4):
            if column % 2 == 0:
                loads[1 + 2 * index + column // 2].wait()
            lanes = pl.ds(column * LANES, LANES)
            source = held.at[pl.ds(index * CHUNK + column * 512, 512)]
            if index >= 8:
                store(source, (wo, wq, wk, wv, wc)[index - 8].at[:, lanes])
            elif index % 2:
                store(source, up.at[:, pl.ds(index // 2 * 512 + column * LANES, LANES)])
            else:
                store(source, down.at[pl.ds(index // 2 * 512, 512), lanes])
    loads[27].wait()
    store(held_result, out_result)
    loads[28].wait()
    store(held_grad, out_input_grad)
    loads[0].wait()
    small = held.at[pl.ds(13 * CHUNK, 40)]
    for at, target in (
        (ATTN_GAIN, attn_gain),
        (ATTN_SHIFT, attn_shift),
        (FFN_GAIN, ffn_gain),
        (FFN_SHIFT, ffn_shift),
        (DOWN_BIAS, down_bias),
        (UP_BIAS, up_bias),
    ):
        for column in range(target.shape[1] // LANES):
            row = pl.ds(at + column, 1)
            target[:, column * LANES : (column + 1) * LANES] = small[row, :]
    for pair in range(4):
        row = small[pl.ds(WRITES + pair, 1), :]
        for head in range(2):
            line = pl.ds(2 * pair + head, 1)
            written = row[:, head * SLOTS : (head + 1) * SLOTS]
            means[line, :] = 0.9 * slot_means[line, :] + 0.1 * written / count
    for copy in stores:
        copy.wait()


def deliver_call(count, full, result, input_grad, slot_means):
    square = jax.ShapeDtypeStruct((512, 512), F32)
    vector = jax.ShapeDtypeStruct((1, 512), F32)
    long = jax.ShapeDtypeStruct((1, 2048), F32)
    shapes = [result, input_grad, vector, vector, square, square, square, square, square]
    shapes += [vector, vector, jax.ShapeDtypeStruct((512, 2048), F32), long]
    shapes += [jax.ShapeDtypeStruct((2048, 512), F32), vector, slot_means]
    anywhere = pl.BlockSpec(memory_space=pl.ANY)
    near = pl.BlockSpec(memory_space=pltpu.VMEM)

    def kernel(full, result, input_grad, slot_means, *outs):
        deliver_kernel(full, result, input_grad, slot_means, count, *outs)

    return pl.pallas_call(
        kernel,
        out_shape=[jax.ShapeDtypeStruct(shape.shape, shape.dtype) for shape in shapes],
        in_specs=[anywhere, anywhere, anywhere, near],
        out_specs=[near if shape is vector or shape is long or shape is slot_means else anywhere for shape in shapes],
        scratch_shapes=[
            pltpu.VMEM((13 * CHUNK + 40, LANES), F32),
            pltpu.VMEM(result.shape, BF16),
            pltpu.VMEM(input_grad.shape, F32),
            pltpu.SemaphoreType.DMA((29,)),
            pltpu.SemaphoreType.DMA((54,)),
        ],
        compiler_params=pltpu.CompilerParams(vmem_limit_bytes=60 * 2**20),
        name="deliver",
    )(full, result, input_grad, slot_means)


def layer_call(sizes, **arrays):
    rows, width, hidden = 1024, 512, 2048
    outputs = dict(
        out_result=jax.ShapeDtypeStruct((rows, width), BF16),
        out_input_grad=jax.ShapeDtypeStruct((rows, width), F32),
        out_full=jax.ShapeDtypeStruct((sizes.rows, LANES), F32),
    )
    low, wide = pltpu.VMEM((rows, width), BF16), pltpu.VMEM((rows, width), F32)
    weight = pltpu.VMEM((width, width), BF16)
    box = pltpu.VMEM((2, sizes.seq, 512 // sizes.seq + 8, LANES), F32)
    pair_box = pltpu.VMEM((4, sizes.seq, 256 // sizes.seq + 8, LANES), F32)
    semaphores = pltpu.SemaphoreType.DMA
    scratch = dict(
        tokens=low, wc=weight, wk=weight, wv=weight, wq=weight, wo=weight,
        up=pltpu.VMEM((4, width, 512), BF16), down=pltpu.VMEM((hidden, width), BF16), pull=low,
        normed=low, queries=low, keys=low, values=low, local=wide, weights=low,
        sums=wide, logits=wide, chances=wide, shares=low, mixed=low, hidden=wide,
        branch=low, turned=pltpu.VMEM((width, rows), BF16), active=low, pushed=low,
        near_grad=pltpu.VMEM((512, LANES), BF16), total_grad=pltpu.VMEM((512, LANES), F32),
        prior=pltpu.VMEM((8, LANES, LANES), BF16), notes=pltpu.VMEM((8, 8, LANES), F32),
        small=pltpu.VMEM((40, LANES), F32),
        held=pltpu.VMEM((sizes.rows, LANES), F32), landed=pltpu.VMEM((sizes.landing, LANES), F32),
        box0=box, box1=box, box2=box, box3=box, box4=pair_box, box5=pair_box, box6=pair_box, box7=pair_box,
        box_sem=semaphores((4, 2)), pair_sem=semaphores((4, 4)), load_sem=semaphores((LOADS + 2,)), up_sem=semaphores((4,)),
        keep_sem=semaphores((18,)), reduce_send=semaphores((18,)),
        reduce_recv=semaphores((18, 8)),
    )
    names = list(arrays) + list(outputs) + list(scratch)

    def kernel(*refs):
        layer_kernel(sizes, types.SimpleNamespace(**dict(zip(names, refs, strict=True))))

    anywhere = pl.BlockSpec(memory_space=pl.ANY)
    near = pl.BlockSpec(memory_space=pltpu.VMEM)
    found = pl.pallas_call(
        kernel,
        out_shape=list(outputs.values()),
        in_specs=[anywhere if name.startswith("in_") else near for name in arrays],
        out_specs=[anywhere] * len(outputs),
        scratch_shapes=list(scratch.values()),
        compiler_params=pltpu.CompilerParams(
            collective_id=1, has_side_effects=True, vmem_limit_bytes=63 * 2**20
        ),
        name="layer",
    )(*arrays.values())
    return types.SimpleNamespace(**dict(zip(outputs, found, strict=True)))


def solution(mesh):
    sizes = Sizes(mesh.shape[DP], mesh.shape[SEQ])

    def shards(
        inputs, starts, attn_gain, attn_shift, query_weight, key_weight, value_weight, control_weight, output_weight,
        ffn_gain, ffn_shift, up_weight, up_bias, down_weight, down_bias, slot_means, cotangent,
    ):
        streams, length, width = inputs.shape
        rows = streams * length
        found = layer_call(
            sizes,
            in_tokens=inputs.reshape(rows, width),
            in_wc=control_weight,
            in_wk=key_weight,
            in_wv=value_weight,
            in_wq=query_weight,
            in_wo=output_weight,
            in_up=up_weight,
            in_down=down_weight,
            in_pull=cotangent.reshape(rows, width),
            starts=starts.reshape(1, streams),
            attn_gain=attn_gain[None],
            attn_shift=attn_shift[None],
            ffn_gain=ffn_gain[None],
            ffn_shift=ffn_shift[None],
            up_bias=up_bias[None],
            down_bias=down_bias[None],
        )
        outs = list(deliver_call(
            streams * sizes.dp, found.out_full, found.out_result, found.out_input_grad, slot_means)
        )
        outs[0], outs[1] = outs[0].reshape(inputs.shape), outs[1].reshape(inputs.shape)
        for at in (2, 3, 9, 10, 12, 14):
            outs[at] = outs[at].reshape(-1)
        return tuple(outs)

    split = P(DP, SEQ, None)
    return jax.shard_map(
        shards,
        mesh=mesh,
        in_specs=(split, P(DP, SEQ)) + (P(),) * 14 + (split,),
        out_specs=(split, split) + (P(),) * 14,
        check_vma=False,
    )
```
